256 devices in a mesh: gx: 32 (over z, x), gy: 8 (over y, core).
Axes of the slice: x: 4, y: 4, z: 8, core: 2. Of those that a mesh axis runs over, the one named last changes fastest.
Arguments:
- newton_residual: float32 [16, 512, 2048], P(None, 'gx', 'gy'), may hold values from -6 to 6
- pressure_head: float32 [16, 512, 2048], P(None, 'gx', 'gy'), may hold values from -6 to 1
- conductivity: float32 [16, 512, 2048], P(None, 'gx', 'gy'), may hold values from 0.1 to 10
- land_use: int32 [512, 2048], P('gx', 'gy'), may hold values from 0 to 7
- storage_table: float32 [8], replicated, may hold values from 0.002 to 0.05
- return_table: float32 [8], replicated, may hold values from 0.2 to 0.9
- well_cells: int32 [32, 8, 32], P('gx', 'gy'), may hold values from 0 to 65535
- well_rates: float32 [32, 8, 32], P('gx', 'gy'), may hold values from 0.5 to 4
- return_cells: int32 [32, 8, 32], P('gx', 'gy'), may hold values from 0 to 4095
Outputs:
- correction: float32 [16, 512, 2048], P(None, 'gx', 'gy')
The draws below stay inside these ranges and needn't reach their ends.
Inputs may be any that keep to these rules, and one draw needn't show every extreme that they name: `well_cells`: A well's cell index z * 16 * 256 + x * 256 + y addresses layer z, column x, y of its tile; wells may share a cell. `return_cells`: index x * 256 + y of a column of the well's tile.
All inputs are finite; a program needn't handle non-finite values.
Results may differ from the reference program's by a relative error of at most 0.0001.
Values sent between devices are 32-bit elements; how exact they have to be, the bound alone decides.
A program may use at most 128 MiB of HBM per device.

```python
import math
import jax
import jax.numpy as jnp
from jax import lax

CX = 16
CY = 256
NZ = 16
LEVELS = 5
COARSE_SWEEPS = 12
WELLS = 32
CLASSES = 8
NX = 512
NY = 2048
TILES_X = 32
TILES_Y = 8


def touch_ends(array, own_key, least, top_value):
    shape = array.shape
    index_at = [jax.random.randint(jax.random.fold_in(own_key, axis), (), 0, shape[axis]) for axis in range(len(shape))]
    array = array.at[tuple(index_at)].set(least)
    longest = shape.index(max(shape))
    index_at[longest] = (index_at[longest] + 1) % shape[longest]
    return array.at[tuple(index_at)].set(top_value)


def block_levels(rng, dims, split, low, high):
    loudness, own = 1.0, jax.random.fold_in(rng, 6)
    for axis_at, blocks in split:
        heights = jnp.exp(jax.random.uniform(jax.random.fold_in(own, axis_at), (blocks,), jnp.float32, low / len(split), high / len(split)))
        loudness = loudness * jnp.repeat(heights, dims[axis_at] // blocks).reshape([-1 if axis == axis_at else 1 for axis in range(len(dims))])
    return loudness


def bell_draw(own_key, extent, scale, limit, cuts=(), dtype=jnp.bfloat16):
    result = jax.random.normal(own_key, extent, jnp.float32) * scale
    if len(cuts) > 0:
        result = block_levels(own_key, extent, cuts, -0.22, 0.18) * result
    return jnp.clip(result, min=-limit, max=limit).astype(dtype)


def setup_inputs(seed: int = 0) -> dict:
    seeds = jax.random.split(jax.random.key(seed), 10)
    newton_residual = bell_draw(seeds[0], (NZ, NX, NY), 1.0, 6.0, ((1, 32), (2, 8)), jnp.float32)
    pressure_head = jnp.clip(-6.0 + 7.0 * jax.random.uniform(seeds[1], (NZ, NX, NY), jnp.float32) ** block_levels(seeds[1], (NZ, NX, NY), ((1, 32), (2, 8)), -0.2, 0.2), -6.0, 1.0)
    conductivity = jnp.clip(jnp.exp(math.log(10.0) - 4.6051702 * jax.random.uniform(seeds[2], (NZ, NX, NY), jnp.float32) ** block_levels(seeds[2], (NZ, NX, NY), ((1, 32), (2, 8)), -0.2, 0.2)), 0.1, 10.0)
    land_use = touch_ends(jax.random.randint(seeds[3], (NX, NY), 0, CLASSES), jax.random.fold_in(seeds[3], 1), 0, CLASSES - 1).astype(jnp.int32)
    storage_table = jnp.clip(jnp.exp(jax.random.uniform(seeds[4], (CLASSES,), jnp.float32, math.log(0.002), math.log(0.05))), 0.002, 0.05)
    return_table = jnp.clip(jax.random.uniform(seeds[5], (CLASSES,), jnp.float32, 0.2, 0.9), 0.2, 0.9)
    well_cells = touch_ends(jax.random.randint(seeds[6], (TILES_X, TILES_Y, WELLS), 0, NZ * CX * CY), jax.random.fold_in(seeds[6], 1), 0, (NZ * CX * CY) - 1).astype(jnp.int32)
    well_rates = jnp.clip(jnp.exp(math.log(4.0) - 2.0794415 * jax.random.uniform(seeds[7], (TILES_X, TILES_Y, WELLS), jnp.float32) ** block_levels(seeds[7], (TILES_X, TILES_Y, WELLS), ((0, 32), (1, 8)), -0.2, 0.2)), 0.5, 4.0)
    return_cells = touch_ends(jax.random.randint(seeds[8], (TILES_X, TILES_Y, WELLS), 0, CX * CY), jax.random.fold_in(seeds[8], 1), 0, (CX * CY) - 1).astype(jnp.int32)
    return dict(newton_residual=newton_residual, pressure_head=pressure_head, conductivity=conductivity, land_use=land_use, storage_table=storage_table, return_table=return_table, well_cells=well_cells, well_rates=well_rates, return_cells=return_cells)


OMEGA = 0.8
VERTICAL = 4.0
ALPHA = 0.5


def harmonic(first, second):
    return 2.0 * first * second / (first + second)


def lookup_table(land_use, table):
    summed = jnp.zeros(land_use.shape, jnp.float32)
    for category in range(CLASSES):
        summed = summed + jnp.where(land_use == category, table[category], jnp.float32(0.0))
    return summed


def fine_faces(permeable, padded, storage):
    face_west = harmonic(permeable, padded[:, :-2, 1:-1])
    face_east = harmonic(permeable, padded[:, 2:, 1:-1])
    face_south = harmonic(permeable, padded[:, 1:-1, :-2])
    face_north = harmonic(permeable, padded[:, 1:-1, 2:])
    vertical_pair = VERTICAL * harmonic(permeable[:-1], permeable[1:])
    face_down = jnp.concatenate([vertical_pair, jnp.zeros_like(permeable[:1])], axis=0)
    return (storage, face_west, face_east, face_south, face_north, face_down)


def pair_x(values):
    return values[:, 0::2] + values[:, 1::2]


def pair_y(values):
    return values[:, :, 0::2] + values[:, :, 1::2]


def aggregate(values):
    return pair_x(pair_y(values))


def prolong(values):
    return jnp.repeat(jnp.repeat(values, 2, axis=1), 2, axis=2)


def coarsen(faces):
    storage, face_west, face_east, face_south, face_north, face_down = faces
    return (aggregate(storage), pair_y(face_west[:, 0::2]), pair_y(face_east[:, 1::2]),
            pair_x(face_south[:, :, 0::2]), pair_x(face_north[:, :, 1::2]), aggregate(face_down))


def upward(face_down):
    return jnp.concatenate([jnp.zeros_like(face_down[:1]), face_down[:-1]], axis=0)


def finish(faces):
    storage, face_west, face_east, face_south, face_north, face_down = faces
    diagonal = storage + face_west + face_east + face_south + face_north + face_down + upward(face_down)
    pivots = [diagonal[0]]
    factors = [jnp.zeros_like(diagonal[0])]
    for layer in range(1, diagonal.shape[0]):
        factor = -face_down[layer - 1] / pivots[layer - 1]
        factors.append(factor)
        pivots.append(diagonal[layer] + factor * face_down[layer - 1])
    return diagonal, jnp.stack(factors), 1.0 / jnp.stack(pivots)


def line_solve(remainder, factors, inverse, face_down):
    count = remainder.shape[0]
    forward = [remainder[0]]
    for layer in range(1, count):
        forward.append(remainder[layer] - factors[layer] * forward[layer - 1])
    backward = [forward[count - 1] * inverse[count - 1]]
    for layer in range(count - 2, -1, -1):
        backward.append((forward[layer] + face_down[layer] * backward[-1]) * inverse[layer])
    return jnp.stack(backward[::-1])


def apply_padded(padded, faces, diagonal):
    storage, face_west, face_east, face_south, face_north, face_down = faces
    centre = padded[:, 1:-1, 1:-1]
    lower_cell = jnp.concatenate([centre[1:], jnp.zeros_like(centre[:1])], axis=0)
    upper_cell = jnp.concatenate([jnp.zeros_like(centre[:1]), centre[:-1]], axis=0)
    return (diagonal * centre - face_west * padded[:, :-2, 1:-1] - face_east * padded[:, 2:, 1:-1]
            - face_south * padded[:, 1:-1, :-2] - face_north * padded[:, 1:-1, 2:]
            - face_down * lower_cell - upward(face_down) * upper_cell)


def pad_plane(field):
    return jnp.pad(field, ((0, 0), (1, 1), (1, 1)))


def reference(newton_residual, pressure_head, conductivity, land_use, storage_table, return_table, well_cells, well_rates, return_cells):
    relief = jnp.exp(ALPHA * jnp.minimum(pressure_head, 0.0))
    permeable = conductivity * relief
    storage = lookup_table(land_use, storage_table)[None] * relief
    hierarchy = [fine_faces(permeable, pad_plane(permeable), storage)]
    for level_index in range(1, LEVELS):
        hierarchy.append(coarsen(hierarchy[-1]))
    factored = [finish(faces) for faces in hierarchy]

    tile_x = lax.broadcasted_iota(jnp.int32, well_cells.shape, 0)
    tile_y = lax.broadcasted_iota(jnp.int32, well_cells.shape, 1)
    layer_of = well_cells // (CX * CY)
    inside = well_cells % (CX * CY)
    row_of = tile_x * CX + inside // CY
    column_of = tile_y * CY + inside % CY
    flat_cells = (layer_of * NX + row_of) * NY + column_of
    source = newton_residual.reshape(-1).at[flat_cells.reshape(-1)].add(-well_rates.reshape(-1))
    fraction = lookup_table(land_use, return_table)
    return_row = tile_x * CX + return_cells // CY
    return_column = tile_y * CY + return_cells % CY
    recharge = fraction[return_row, return_column] * well_rates
    top_cells = return_row * NY + return_column
    source = source.at[top_cells.reshape(-1)].add(recharge.reshape(-1)).reshape(NZ, NX, NY)

    def sweep_level(level_index, iterate, rhs):
        faces = hierarchy[level_index]
        diagonal, factors, inverse = factored[level_index]
        remainder = rhs - apply_padded(pad_plane(iterate), faces, diagonal)
        return iterate + OMEGA * line_solve(remainder, factors, inverse, faces[5])

    def cycle(level_index, rhs):
        faces = hierarchy[level_index]
        diagonal, factors, inverse = factored[level_index]
        if level_index == LEVELS - 1:
            shift = jnp.sum(rhs) / jnp.sum(faces[0])
            start = jnp.full(rhs.shape, shift, jnp.float32)

            def sweep(step, current):
                return sweep_level(level_index, current, rhs)
            return lax.fori_loop(0, COARSE_SWEEPS, sweep, start)
        iterate = OMEGA * line_solve(rhs, factors, inverse, faces[5])
        iterate = sweep_level(level_index, iterate, rhs)
        remainder = rhs - apply_padded(pad_plane(iterate), faces, diagonal)
        iterate = iterate + prolong(cycle(level_index + 1, aggregate(remainder)))
        iterate = sweep_level(level_index, iterate, rhs)
        iterate = sweep_level(level_index, iterate, rhs)
        return iterate

    return cycle(0, source)
```

```python
import functools

import jax
import jax.numpy as jnp
from jax import lax
from jax.experimental import pallas as pl
from jax.experimental.pallas import tpu as pltpu
from jax.sharding import PartitionSpec as P

NZ = 16
CLASSES = 8
COARSE_SWEEPS = 12
OMEGA = 0.8
VERTICAL = 4.0
ALPHA = 0.5
F32 = jnp.float32
MESH = pl.DeviceIdType.MESH

NX = (16, 8, 4, 2)
NY = (256, 128, 64, 32)
XR = (24, 16, 8, 8)
YR = (384, 256, 128, 128)
OWN_R = (16, 8, 8, 8)
OWN_W = (256, 128, 128, 128)
EOFF = (0, 0, 4, 2)
NOFF = (0, 0, 64, 32)

THREE = ((3, 0), (2, 3), (2, 5))
FOUR = ((2, 0), (2, 2), (2, 4), (2, 6))
ONE = ((2, 0),)
EXCHANGES = {
    "e0": (0, 8, THREE),
    "c1": (1, 8, FOUR),
    "c2": (2, 8, FOUR),
    "c3": (3, 8, FOUR),
    "x1": (1, 2, ONE),
    "x2": (2, 2, ONE),
    "x3": (3, 2, ONE),
    "u3": (3, 2, ONE),
    "u2": (2, 2, ONE),
    "u1": (1, 2, ONE),
    "u0": (0, 2, ONE),
}
GY, GX = 8, 32
N_HALO = 8 * len(EXCHANGES)
N_SEM = N_HALO + 2 * (GY - 1) + 2 * (GX - 1)
LEVEL_ARRAYS = ("E", "N", "D", "diag", "g", "inv", "rhs", "u", "f")


def rot(value, shift, axis):
    shift %= value.shape[axis]
    return value if shift == 0 else pltpu.roll(value, shift, axis)


def iota(shape, axis):
    return lax.broadcasted_iota(jnp.int32, shape, axis)


def between(index, start, count):
    return (index >= start) & (index < start + count)


def exact_dot(left, right):
    return jnp.dot(left, right, precision=lax.Precision.HIGHEST, preferred_element_type=F32)


def scratch_plan():
    plan = {}
    for level in range(4):
        for name in LEVEL_ARRAYS:
            plan[f"{name}{level}"] = pltpu.VMEM((NZ, XR[level], YR[level]), F32)
    plan["P0"] = pltpu.VMEM((NZ, XR[0], YR[0]), F32)
    plan["S0"] = pltpu.VMEM((NZ, XR[0], YR[0]), F32)
    for name in ("E4", "N4", "g4", "inv4", "rhs4", "u4", "f4"):
        plan[name] = pltpu.VMEM((NZ * 16, 128), F32)
    for name in ("ta", "tb", "tc", "td"):
        plan[name] = pltpu.VMEM((NZ, 2, 16, 128), F32)
    for name, (level, group, _) in EXCHANGES.items():
        tiles = NZ * group // 8
        for kind in ("s", "r"):
            plan[f"{name}_{kind}x"] = pltpu.VMEM((2, tiles, 8, OWN_W[level]), F32)
            plan[f"{name}_{kind}y"] = pltpu.VMEM((2, OWN_R[level], 128), F32)
        plan[f"{name}_rc"] = pltpu.VMEM((4, 8, 128), F32)
    for name, count in (("gc", 4), ("gr", 1)):
        plan[f"{name}_s1"] = pltpu.VMEM((count, 8, 128), F32)
        plan[f"{name}_r1"] = pltpu.VMEM((GY, count, 8, 128), F32)
        plan[f"{name}_s2"] = pltpu.VMEM((count, 8, 128), F32)
        plan[f"{name}_r2"] = pltpu.VMEM((count, GX * 8, 128), F32)
    plan["send"] = pltpu.SemaphoreType.DMA((N_SEM,))
    plan["recv"] = pltpu.SemaphoreType.DMA((N_SEM,))
    return plan


PLAN = scratch_plan()


def kernel(
    residual, pressure, conductivity, land_use, storage_table, return_table,
    well_cells, well_rates, return_cells, out, *scratch,
):
    ref = dict(zip(PLAN, scratch))
    gx = lax.axis_index("gx")
    gy = lax.axis_index("gy")

    def device(dx, dy):
        return (lax.rem(gx + (dx + GX), GX), lax.rem(gy + (dy + GY), GY))

    peers = [(dx, dy) for dx in (-1, 1) for dy in (-1, 1)]
    peers += [(0, d) for d in range(1, GY)] + [(d, 0) for d in range(1, GX)]
    barrier = pltpu.get_barrier_semaphore()
    for dx, dy in peers:
        pl.semaphore_signal(barrier, inc=1, device_id=device(dx, dy), device_id_type=MESH)

    started = []

    def remote(src, dst, index, dx, dy):
        copy = pltpu.make_async_remote_copy(
            src_ref=src, dst_ref=dst, send_sem=ref["send"].at[index], recv_sem=ref["recv"].at[index],
            device_id=device(dx, dy), device_id_type=MESH,
        )
        copy.start()
        started.append(copy)
        return copy

    def pack(name, get):
        level, group, items = EXCHANGES[name]
        nx, ny, rows, width = NX[level], NY[level], OWN_R[level], OWN_W[level]
        row8 = iota((8, width), 0)
        lane = iota((rows, 128), 1)
        y_lo = jnp.zeros((rows, 128), F32)
        y_hi = jnp.zeros((rows, 128), F32)
        per_tile = 8 // group
        for z in range(NZ):
            if z % per_tile == 0:
                x_lo = jnp.zeros((8, width), F32)
                x_hi = jnp.zeros((8, width), F32)
            slot = z % per_tile
            for k, (w, o) in enumerate(items):
                value = get(k, z)
                lo = group * slot + o
                hi = group * (slot + 1) - o
                x_lo = jnp.where(between(row8, lo, w), rot(value[0:8], lo, 0), x_lo)
                x_hi = jnp.where(
                    between(row8, (8 - w + hi) % 8, w), rot(value[rows - 8 : rows], 8 - nx + hi, 0), x_hi
                )
                lo = group * z + o
                hi = group * (z + 1) - o
                y_lo = jnp.where(between(lane, lo, w), rot(value[:, 0:128], lo, 1), y_lo)
                y_hi = jnp.where(
                    between(lane, (128 - w + hi) % 128, w),
                    rot(value[:, width - 128 : width], 128 - ny + hi, 1),
                    y_hi,
                )
            if slot == per_tile - 1:
                ref[f"{name}_sx"][0, z // per_tile] = x_lo
                ref[f"{name}_sx"][1, z // per_tile] = x_hi
        ref[f"{name}_sy"][0] = y_lo
        ref[f"{name}_sy"][1] = y_hi

    def send(name):
        level = EXCHANGES[name][0]
        rows = OWN_R[level]
        base = 8 * list(EXCHANGES).index(name)
        sx, sy = ref[f"{name}_sx"], ref[f"{name}_sy"]
        rx, ry, rc = ref[f"{name}_rx"], ref[f"{name}_ry"], ref[f"{name}_rc"]
        first, last = pl.ds(0, 8), pl.ds(rows - 8, 8)
        moves = (
            (sx.at[0], rx.at[0], -1, 0),
            (sx.at[1], rx.at[1], 1, 0),
            (sy.at[0], ry.at[0], 0, -1),
            (sy.at[1], ry.at[1], 0, 1),
            (sy.at[0, first], rc.at[0], -1, -1),
            (sy.at[0, last], rc.at[1], 1, -1),
            (sy.at[1, first], rc.at[2], -1, 1),
            (sy.at[1, last], rc.at[3], 1, 1),
        )
        return [remote(src, dst, base + i, dx, dy) for i, (src, dst, dx, dy) in enumerate(moves)]

    def unpack(name, copies, targets, fills, masked=None):
        level, group, items = EXCHANGES[name]
        nx, ny, rows, width = NX[level], NY[level], OWN_R[level], OWN_W[level]
        eoff, noff = EOFF[level], NOFF[level]
        for copy in copies:
            copy.wait_recv()
        rx, ry, rc = ref[f"{name}_rx"], ref[f"{name}_ry"], ref[f"{name}_rc"]
        row8 = iota((8, 128), 0)
        strips = []
        for side in (0, 1):
            east, west = rc[2 * side], rc[2 * side + 1]
            if level <= 1:
                strips.append(jnp.concatenate([ry[side], jnp.where(row8 < 4, east, west)], axis=0))
            else:
                strips.append(
                    jnp.where(
                        row8 < nx, ry[side],
                        jnp.where(row8 < nx + 2, rot(east, eoff, 0), rot(west, 8 - nx, 0)),
                    )
                )
        strip_n, strip_s = strips
        rows_all = XR[level]
        lane = iota((rows_all, 128), 1)
        row = iota((8, width), 0)
        per_tile = 8 // group
        for z in range(NZ):
            tile, slot = z // per_tile, z % per_tile
            for k, (w, o) in enumerate(items):
                target, fill = targets[k], fills[k]
                from_e = rot(rx[0, tile], eoff - (group * slot + o), 0)
                from_w = rot(rx[1, tile], o - group * (slot + 1), 0)
                from_n = rot(strip_n, noff - (group * z + o), 1)
                from_s = rot(strip_s, o - group * (z + 1), 1)
                if masked is not None and k == 0:
                    from_e, from_w = from_e * masked[0], from_w * masked[1]
                    from_n, from_s = from_n * masked[2], from_s * masked[3]
                in_e, in_w = between(row, eoff, w), row >= 8 - w
                in_n, in_s = between(lane, noff, w), lane >= 128 - w
                if level <= 1:
                    target[z, rows : rows + 8, 0:width] = jnp.where(in_e, from_e, jnp.where(in_w, from_w, fill))
                    target[z, :, width : width + 128] = jnp.where(in_n, from_n, jnp.where(in_s, from_s, fill))
                else:
                    value = jnp.where(in_e, from_e, jnp.where(in_w, from_w, target[z]))
                    target[z] = jnp.where(in_n, from_n, jnp.where(in_s, from_s, value))

    def factor(level):
        diag, down, g, inv = (ref[f"{name}{level}"] for name in ("diag", "D", "g", "inv"))
        before = None
        for z in range(NZ):
            pivot = diag[z]
            if z > 0:
                pivot = pivot - before * down[z - 1]
            inverse = 1.0 / pivot
            inv[z] = inverse
            if z < NZ - 1:
                before = down[z] * inverse
                g[z] = before

    def back_substitute(level, update):
        g, inv, f = (ref[f"{name}{level}"] for name in ("g", "inv", "f"))
        value = f[NZ - 1] * inv[NZ - 1]
        update(NZ - 1, value)
        for z in range(NZ - 2, -1, -1):
            value = f[z] * inv[z] + g[z] * value
            update(z, value)

    def first_sweep(level):
        g, f, rhs, u = (ref[f"{name}{level}"] for name in ("g", "f", "rhs", "u"))
        value = rhs[0]
        f[0] = value
        for z in range(1, NZ):
            value = rhs[z] + g[z - 1] * value
            f[z] = value

        def update(z, solved):
            u[z] = OMEGA * solved

        back_substitute(level, update)

    def lateral(level, z, u):
        east, north = ref[f"E{level}"][z], ref[f"N{level}"][z]
        return (
            east * rot(u, -1, 0) + rot(east * u, 1, 0) + north * rot(u, -1, 1) + rot(north * u, 1, 1)
        )

    def sweep(level):
        g, f, rhs, u = (ref[f"{name}{level}"] for name in ("g", "f", "rhs", "u"))
        value = None
        for z in range(NZ):
            right = rhs[z] + lateral(level, z, u[z])
            value = right if z == 0 else right + g[z - 1] * value
            f[z] = value

        def update(z, solved):
            old = u[z]
            u[z] = old + OMEGA * (solved - old)

        back_substitute(level, update)

    def remainder(level, z):
        diag, down, rhs, u = (ref[f"{name}{level}"] for name in ("diag", "D", "rhs", "u"))
        here = u[z]
        value = rhs[z] + lateral(level, z, here) - diag[z] * here
        if z < NZ - 1:
            value = value + down[z] * u[z + 1]
        if z > 0:
            value = value + down[z - 1] * u[z - 1]
        return value[0 : OWN_R[level], 0 : OWN_W[level]]

    def tiles_of(level):
        return OWN_W[level] // 128

    def put_rows(buffer, level, z, value):
        for t in range(tiles_of(level)):
            buffer[z, t, 0 : OWN_R[level], :] = value[:, 128 * t : 128 * (t + 1)]

    def row_half(buffer, level, z, odd):
        return jnp.concatenate(
            [buffer[z, t, pl.ds(odd, 8, stride=2), :] for t in range(tiles_of(level))], axis=1
        )

    def lane_matrix(level, kind):
        fine = iota((OWN_W[level], 128), 0)
        coarse = iota((OWN_W[level], 128), 1)
        half = NY[level] // 2
        if kind == "sum":
            hit = between(fine - 2 * coarse, 0, 2)
        else:
            hit = fine == 2 * coarse + (1 if kind == "odd" else 0)
        return jnp.where(hit & (coarse < half), 1.0, 0.0).astype(F32)

    def keep_own(level, value, fill):
        if level == 1:
            return value
        own = (iota((8, 128), 0) < (NX[level] if level < 4 else 1)) & (
            iota((8, 128), 1) < (NY[level] if level < 4 else 16)
        )
        return jnp.where(own, value, fill)

    def clear_low_rows(buffer):
        for z in range(NZ):
            for t in range(2):
                buffer[z, t, 8:16, :] = jnp.zeros((8, 128), F32)

    def restrict(level):
        for z in range(NZ):
            put_rows(ref["ta"], level, z, remainder(level, z))
        summed = jnp.concatenate(
            [row_half(ref["ta"], level, z, 0) + row_half(ref["ta"], level, z, 1) for z in range(NZ)], axis=0
        )
        coarse = exact_dot(summed, lane_matrix(level, "sum"))
        return [keep_own(level + 1, coarse[8 * z : 8 * z + 8], 0.0) for z in range(NZ)]

    def coarsen(level):
        names = ("E", "N", "D", "diag")
        buffers = [ref[name] for name in ("ta", "tb", "tc", "td")]
        for z in range(NZ):
            for name, buffer in zip(names, buffers):
                put_rows(buffer, level, z, ref[f"{name}{level}"][z, 0 : OWN_R[level], 0 : OWN_W[level]])
        odd_e, sum_n, sum_d, sum_g = [], [], [], []
        for z in range(NZ):
            e0, e1 = (row_half(buffers[0], level, z, odd) for odd in (0, 1))
            n0, n1 = (row_half(buffers[1], level, z, odd) for odd in (0, 1))
            d0, d1 = (row_half(buffers[2], level, z, odd) for odd in (0, 1))
            g0, g1 = (row_half(buffers[3], level, z, odd) for odd in (0, 1))
            odd_e.append(e1)
            sum_n.append(n0 + n1)
            sum_d.append(d0 + d1)
            sum_g.append(g0 + g1 - 2.0 * e0)
        total = lane_matrix(level, "sum")
        count = NZ * 8
        summed = exact_dot(jnp.concatenate(odd_e + sum_d + sum_g, axis=0), total)
        north = jnp.concatenate(sum_n, axis=0)
        north_odd = exact_dot(north, lane_matrix(level, "odd"))
        north_even = exact_dot(north, lane_matrix(level, "even"))
        result = []
        for z in range(NZ):
            at = slice(8 * z, 8 * z + 8)
            result.append(
                (
                    keep_own(level + 1, summed[8 * z : 8 * z + 8], 0.0),
                    keep_own(level + 1, north_odd[at], 0.0),
                    keep_own(level + 1, summed[count + 8 * z : count + 8 * z + 8], 0.0),
                    keep_own(
                        level + 1,
                        summed[2 * count + 8 * z : 2 * count + 8 * z + 8] - 2.0 * north_even[at],
                        1.0,
                    ),
                )
            )
        return result

    def store_coarse(level, values):
        for z in range(NZ):
            for name, value in zip(("E", "N", "D", "diag"), values[z]):
                ref[f"{name}{level}"][z, 0:8, 0:128] = value

    def prolong(level):
        coarse = jnp.concatenate([ref[f"u{level + 1}"][z, 0:8, 0:128] for z in range(NZ)], axis=0)
        from_lane = iota((128, OWN_W[level]), 0)
        to_lane = iota((128, OWN_W[level]), 1)
        hit = between(to_lane - 2 * from_lane, 0, 2) & (to_lane < NY[level])
        fine = exact_dot(coarse, jnp.where(hit, 1.0, 0.0).astype(F32))
        buffer = ref["ta"]
        u = ref[f"u{level}"]
        rows, width = OWN_R[level], OWN_W[level]
        for z in range(NZ):
            for t in range(tiles_of(level)):
                piece = fine[8 * z : 8 * z + 8, 128 * t : 128 * (t + 1)]
                buffer[z, t, pl.ds(0, 8, stride=2), :] = piece
                buffer[z, t, pl.ds(1, 8, stride=2), :] = piece
        for z in range(NZ):
            add = jnp.concatenate([buffer[z, t, 0:rows, :] for t in range(tiles_of(level))], axis=1)
            u[z, 0:rows, 0:width] = u[z, 0:rows, 0:width] + add

    lane8 = iota((8, 128), 1)
    row8 = iota((8, 128), 0)
    at_sum = (lane8 == 48) & (row8 == 0)

    def pack_tile(values):
        row16 = iota((16, 128), 0)
        lane16 = iota((16, 128), 1)
        stacked = jnp.zeros((16, 128), F32)
        for z in range(NZ):
            stacked = jnp.where(row16 == z, jnp.broadcast_to(values[z][0:1], (16, 128)), stacked)
        stacked = jnp.where(lane16 < 16, stacked, 0.0)
        return rot(stacked[0:8], 16, 1) + rot(stacked[8:16], 80, 1)

    def total_of(value):
        return jnp.sum(jnp.sum(value, axis=1, keepdims=True), axis=0, keepdims=True)

    def gather_columns(name, tiles, part, base):
        for a, tile in enumerate(tiles):
            ref[f"{name}_s1"][a] = jnp.where(at_sum, part, tile) if a == 0 else tile
        return [
            remote(ref[f"{name}_s1"], ref[f"{name}_r1"].at[d], base + d - 1, 0, d) for d in range(1, GY)
        ]

    def gather_rows(name, copies, base):
        for copy in copies:
            copy.wait_recv()
        s1, r1, s2, r2 = (ref[f"{name}_{kind}"] for kind in ("s1", "r1", "s2", "r2"))
        for a in range(s1.shape[0]):
            tiles = [s1[a]] + [r1[d, a] for d in range(1, GY)]
            clean = [jnp.where(at_sum, 0.0, tiles[i]) if a == 0 else tiles[i] for i in (0, 1, GY - 1)]
            window = clean[0] + rot(clean[1], -16, 1) + rot(clean[2], 16, 1)
            if a == 0:
                parts = tiles[0]
                for tile in tiles[1:]:
                    parts = parts + tile
                window = jnp.where(at_sum, parts, window)
            s2[a] = window
            r2[a, 0:8, :] = window
        return [
            remote(s2, r2.at[:, pl.ds(8 * (GX - d), 8), :], base + d - 1, d, 0) for d in range(1, GX)
        ]

    def coarse_layer(buffer, a, z):
        sub, half = z % 8, z // 8
        pieces = [buffer[a, pl.ds(64 * i + sub, 8, stride=8), :] for i in range(4)]
        low = jnp.concatenate(pieces[0:2], axis=0)
        high = jnp.concatenate(pieces[2:4], axis=0)
        lane = iota((16, 128), 1)
        if half == 0:
            return jnp.where(lane < 64, low, rot(high, 64, 1))
        return jnp.where(lane < 64, rot(low, 64, 1), high)

    def coarse_sum(buffer):
        value = jnp.where(at_sum, buffer[0, 0:8, :], 0.0)
        for k in range(1, GX):
            value = value + jnp.where(at_sum, buffer[0, 8 * k : 8 * k + 8, :], 0.0)
        return total_of(value)

    def coarse_at(name, z):
        return ref[name][16 * z : 16 * z + 16, :]

    clear_low_rows(ref["ta"])
    clear_low_rows(ref["tb"])
    clear_low_rows(ref["tc"])
    clear_low_rows(ref["td"])
    use = land_use[...]
    table = jnp.zeros(use.shape, F32)
    fraction = jnp.zeros(use.shape, F32)
    for category in range(CLASSES):
        table = table + jnp.where(use == category, storage_table[category], 0.0)
        fraction = fraction + jnp.where(use == category, return_table[category], 0.0)
    cells, rates, returns = well_cells[...], well_rates[...], return_cells[...]
    wells = rates.shape[1]

    def hits(count, index):
        return iota((count, wells), 0) == index

    def outer(count, index_row, index_column):
        left = jnp.where(hits(count, index_row), rates, 0.0)
        right = jnp.where(hits(256, index_column), 1.0, 0.0).astype(F32)
        return lax.dot_general(
            left, right, (((1,), (1,)), ((), ())),
            precision=lax.Precision.HIGHEST, preferred_element_type=F32,
        )

    pumped = outer(256, cells >> 8, cells & 255)
    recharge = fraction * outer(16, returns >> 8, returns & 255)
    storage_sum = jnp.zeros((16, 256), F32)
    for z in range(NZ):
        relief = jnp.exp(ALPHA * jnp.minimum(pressure[z], 0.0))
        ref["P0"][z, 0:16, 0:256] = conductivity[z] * relief
        storage = table * relief
        ref["S0"][z, 0:16, 0:256] = storage
        storage_sum = storage_sum + storage
        source = residual[z] - pumped[16 * z : 16 * z + 16]
        if z == 0:
            source = source + recharge
        ref["rhs0"][z, 0:16, 0:256] = source
    first = [ref["P0"], ref["S0"], ref["rhs0"]]
    pack("e0", lambda k, z: first[k][z, 0:16, 0:256])
    pl.semaphore_wait(barrier, len(peers))
    copies = send("e0")

    flags = [
        jnp.where(inside, 1.0, 0.0).astype(F32)
        for inside in (gx < GX - 1, gx > 0, gy < GY - 1, gy > 0)
    ]
    row24 = iota((24, 128), 0)
    by_row = jnp.where(row24 < 16, 1.0, jnp.where(row24 < 20, flags[0], flags[1]))
    unpack("e0", copies, first, (0.0, 1.0, 0.0), (flags[0], flags[1], by_row * flags[2], by_row * flags[3]))

    def harmonic(first_value, second_value):
        return 2.0 * first_value * second_value / (first_value + second_value + 1e-30)

    above = None
    for z in range(NZ):
        here = ref["P0"][z]
        east = harmonic(here, rot(here, -1, 0))
        north = harmonic(here, rot(here, -1, 1))
        diagonal = ref["S0"][z] + east + rot(east, 1, 0) + north + rot(north, 1, 1)
        if z > 0:
            diagonal = diagonal + above
        if z < NZ - 1:
            above = VERTICAL * harmonic(here, ref["P0"][z + 1])
            diagonal = diagonal + above
        else:
            above = jnp.zeros_like(here)
        ref["D0"][z] = above
        ref["E0"][z] = east
        ref["N0"][z] = north
        ref["diag0"][z] = diagonal
    factor(0)

    arrays = {level: [ref[f"{name}{level}"] for name in ("E", "N", "D", "diag")] for level in (1, 2, 3)}
    fills = (0.0, 0.0, 0.0, 1.0)
    sent = {}

    def own_coefficients(level):
        store_coarse(level, coarsen(level - 1))
        pack(f"c{level}", lambda k, z: arrays[level][k][z, 0:8, 0:128])
        sent[level] = send(f"c{level}")

    own_coefficients(1)

    def down(level):
        first_sweep(level)
        sweep(level)
        values = restrict(level)
        if level < 3:
            for z in range(NZ):
                ref[f"rhs{level + 1}"][z, 0:8, 0:128] = values[z]
            pack(f"x{level + 1}", lambda k, z: values[z])
            return send(f"x{level + 1}")
        return values

    def enter(level, copies):
        unpack(f"c{level}", sent[level], arrays[level], fills)
        factor(level)
        unpack(f"x{level}", copies, [ref[f"rhs{level}"]], (0.0,))

    copies = down(0)
    own_coefficients(2)
    own_coefficients(3)
    bottom = coarsen(3)
    tiles = [pack_tile([bottom[z][k] for z in range(NZ)]) for k in range(4)]
    tiles = [tiles[3], tiles[0], tiles[1], tiles[2]]
    stage = gather_columns("gc", tiles, total_of(storage_sum), N_HALO)
    enter(1, copies)
    copies = down(1)
    stage_c = gather_rows("gc", stage, N_HALO + GY - 1)
    enter(2, copies)
    copies = down(2)
    enter(3, copies)
    values = down(3)
    tile = pack_tile(values)
    stage = gather_columns("gr", [tile], total_of(tile), N_HALO + GY - 1 + GX - 1)
    stage_r = gather_rows("gr", stage, N_HALO + 2 * (GY - 1) + GX - 1)

    for copy in stage_c:
        copy.wait_recv()
    lane = iota((16, 128), 1)
    row = iota((16, 128), 0)
    gap = (lane & 63) >= 48
    before = None
    for z in range(NZ):
        pivot = jnp.where(gap, 1.0, coarse_layer(ref["gc_r2"], 0, z))
        if z > 0:
            pivot = pivot - before * below
        inverse = 1.0 / pivot
        below = coarse_layer(ref["gc_r2"], 3, z)
        before = below * inverse
        at = slice(16 * z, 16 * z + 16)
        ref["inv4"][at, :] = inverse
        ref["g4"][at, :] = before
        ref["E4"][at, :] = coarse_layer(ref["gc_r2"], 1, z)
        ref["N4"][at, :] = coarse_layer(ref["gc_r2"], 2, z)
    storage_total = coarse_sum(ref["gc_r2"])
    for copy in stage_r:
        copy.wait_recv()
    shift = coarse_sum(ref["gr_r2"]) / storage_total
    for z in range(NZ):
        at = slice(16 * z, 16 * z + 16)
        ref["rhs4"][at, :] = coarse_layer(ref["gr_r2"], 0, z)
        ref["u4"][at, :] = jnp.broadcast_to(shift, (16, 128))

    def coarse_sweep(step, carry):
        value = None
        for z in range(NZ):
            u, east, north = coarse_at("u4", z), coarse_at("E4", z), coarse_at("N4", z)
            from_e = rot(u, -1, 0)
            from_e = jnp.where(row == 15, rot(from_e, 64, 1), from_e)
            from_w = rot(east * u, 1, 0)
            from_w = jnp.where(row == 0, rot(from_w, 64, 1), from_w)
            right = coarse_at("rhs4", z) + east * from_e + from_w + north * rot(u, -1, 1) + rot(north * u, 1, 1)
            value = right if z == 0 else right + coarse_at("g4", z - 1) * value
            ref["f4"][16 * z : 16 * z + 16, :] = value
        for z in range(NZ - 1, -1, -1):
            solved = coarse_at("f4", z) * coarse_at("inv4", z)
            value = solved if z == NZ - 1 else solved + coarse_at("g4", z) * value
            old = coarse_at("u4", z)
            ref["u4"][16 * z : 16 * z + 16, :] = old + OMEGA * (value - old)
        return carry

    lax.fori_loop(0, COARSE_SWEEPS, coarse_sweep, 0)

    columns = jnp.concatenate(
        [ref["u4"][pl.ds(0, 8, stride=16), :], ref["u4"][pl.ds(128, 8, stride=16), :]], axis=0
    )
    hit = between(iota((128, 128), 1) - 2 * (iota((128, 128), 0) - 16), 0, 2) & (iota((128, 128), 1) < 32)
    fine = exact_dot(columns, jnp.where(hit, 1.0, 0.0).astype(F32))
    for z in range(NZ):
        ref["u3"][z] = ref["u3"][z] + jnp.broadcast_to(fine[z : z + 1], (8, 128))
    for level in (3, 2, 1, 0):
        if level < 3:
            prolong(level)
        u = ref[f"u{level}"]
        pack(f"u{level}", lambda k, z: u[z, 0 : OWN_R[level], 0 : OWN_W[level]])
        unpack(f"u{level}", send(f"u{level}"), [u], (0.0,))
        sweep(level)
        sweep(level)
    for z in range(NZ):
        out[z] = ref["u0"][z, 0:16, 0:256]
    for copy in started:
        copy.wait_send()


def shards(
    newton_residual, pressure_head, conductivity, land_use, storage_table, return_table,
    well_cells, well_rates, return_cells,
):
    vmem = pl.BlockSpec(memory_space=pltpu.VMEM)
    smem = pl.BlockSpec(memory_space=pltpu.SMEM)
    wells = well_cells.shape[-1]
    return pl.pallas_call(
        kernel,
        out_shape=jax.ShapeDtypeStruct(newton_residual.shape, F32),
        in_specs=[vmem] * 4 + [smem] * 2 + [vmem] * 3,
        out_specs=vmem,
        scratch_shapes=list(PLAN.values()),
        compiler_params=pltpu.CompilerParams(
            collective_id=0, has_side_effects=True, vmem_limit_bytes=48 * 1024 * 1024
        ),
    )(
        newton_residual, pressure_head, conductivity, land_use, storage_table, return_table,
        well_cells.reshape(1, wells), well_rates.reshape(1, wells), return_cells.reshape(1, wells),
    )


def solution(mesh):
    return jax.shard_map(
        shards,
        mesh=mesh,
        in_specs=(
            P(None, "gx", "gy"),
            P(None, "gx", "gy"),
            P(None, "gx", "gy"),
            P("gx", "gy"),
            P(),
            P(),
            P("gx", "gy", None),
            P("gx", "gy", None),
            P("gx", "gy", None),
        ),
        out_specs=P(None, "gx", "gy"),
        check_vma=False,
    )
```

```python
import functools

import jax
import jax.numpy as jnp
from jax import lax
from jax.experimental import pallas as pl
from jax.experimental.pallas import tpu as pltpu
from jax.sharding import PartitionSpec as P

NZ = 16
CLASSES = 8
COARSE_SWEEPS = 12
OMEGA = 0.8
VERTICAL = 4.0
ALPHA = 0.5
F32 = jnp.float32
MESH = pl.DeviceIdType.MESH

NX = (16, 8, 4, 2)
NY = (256, 128, 64, 32)
XR = (32, 16, 32, 16)
YR = (384, 256, 128, 128)
REACH = 3
SIDES = [d for d in range(-REACH, REACH + 1) if d != 0]
GY, GX = 8, 32
N_E0 = 12
N_WIDE = 6 * REACH + 2
N_V1 = 8
B_E0 = 0
B_C2 = B_E0 + N_E0
B_X2 = B_C2 + N_WIDE
B_V1 = B_X2 + N_WIDE
N_HALO = B_V1 + N_V1
N_SEM = N_HALO + 2 * (GY - 1) + 2 * (GX - 1)
LEVEL_ARRAYS = ("E", "N", "D", "diag", "g", "inv", "rhs", "u", "f")


def rot(value, shift, axis):
    shift %= value.shape[axis]
    return value if shift == 0 else pltpu.roll(value, shift, axis)


def iota(shape, axis):
    return lax.broadcasted_iota(jnp.int32, shape, axis)


def between(index, start, count):
    return (index >= start) & (index < start + count)


def exact_dot(left, right):
    return jnp.dot(left, right, precision=lax.Precision.HIGHEST, preferred_element_type=F32)


def scratch_plan():
    plan = {}
    for level in range(4):
        for name in LEVEL_ARRAYS:
            plan[f"{name}{level}"] = pltpu.VMEM((NZ, XR[level], YR[level]), F32)
    plan["P0"] = pltpu.VMEM((NZ, XR[0], YR[0]), F32)
    plan["S0"] = pltpu.VMEM((NZ, XR[0], YR[0]), F32)
    for name in ("E4", "N4", "g4", "inv4", "rhs4", "u4", "f4"):
        plan[name] = pltpu.VMEM((NZ * 16, 128), F32)
    for name in ("ta", "tb", "tc", "td"):
        plan[name] = pltpu.VMEM((NZ, 3, 32, 128), F32)
    plan["e0_sy"] = pltpu.VMEM((2, 3, 16, 128), F32)
    plan["e0_ry"] = pltpu.VMEM((2, 3, 16, 128), F32)
    plan["e0_rc"] = pltpu.VMEM((4, 3, 8, 128), F32)
    for name, count in (("c2", 4), ("x2", 1)):
        plan[f"{name}_sx"] = pltpu.VMEM((count, 4, 8, 128), F32)
        plan[f"{name}_rx"] = pltpu.VMEM((2 * REACH + 1, count, 4, 8, 128), F32)
        plan[f"{name}_sy"] = pltpu.VMEM((2, count, 8, 128), F32)
        plan[f"{name}_ry"] = pltpu.VMEM((2, 2 * REACH + 1, count, 8, 128), F32)
    for kind in ("s", "r"):
        plan[f"v1_{kind}x"] = pltpu.VMEM((2, 8, 8, 128), F32)
        plan[f"v1_{kind}y"] = pltpu.VMEM((2, 8, 128), F32)
    plan["v1_rc"] = pltpu.VMEM((4, 8, 128), F32)
    for name in ("residual", "pressure", "conductivity"):
        plan[name] = pltpu.VMEM((NZ, NX[0], NY[0]), F32)
    plan["land_use"] = pltpu.VMEM((NX[0], NY[0]), jnp.int32)
    plan["load"] = pltpu.SemaphoreType.DMA((4,))
    for name, count in (("gc", 4), ("gr", 1)):
        plan[f"{name}_s1"] = pltpu.VMEM((count, 8, 128), F32)
        plan[f"{name}_r1"] = pltpu.VMEM((GY, count, 8, 128), F32)
        plan[f"{name}_s2"] = pltpu.VMEM((count, 8, 128), F32)
        plan[f"{name}_r2"] = pltpu.VMEM((count, GX * 8, 128), F32)
    plan["send"] = pltpu.SemaphoreType.DMA((N_SEM,))
    plan["recv"] = pltpu.SemaphoreType.DMA((N_SEM,))
    return plan


PLAN = scratch_plan()


def kernel(
    residual_in, pressure_in, conductivity_in, land_use_in, storage_table, return_table,
    well_cells, well_rates, return_cells, out, *scratch,
):
    ref = dict(zip(PLAN, scratch))
    gx = lax.axis_index("gx")
    gy = lax.axis_index("gy")

    def device(dx, dy):
        return (lax.rem(gx + (dx + GX), GX), lax.rem(gy + (dy + GY), GY))

    peers = [(dx, dy) for dx in SIDES for dy in (-1, 1)]
    peers += [(0, d) for d in range(1, GY)] + [(d, 0) for d in range(1, GX)]
    barrier = pltpu.get_barrier_semaphore()
    for dx, dy in peers:
        pl.semaphore_signal(barrier, inc=1, device_id=device(dx, dy), device_id_type=MESH)

    loads = []
    for i, (name, source) in enumerate(
        (("land_use", land_use_in), ("pressure", pressure_in), ("conductivity", conductivity_in), ("residual", residual_in))
    ):
        loads.append(pltpu.make_async_copy(source, ref[name], ref["load"].at[i]))
        loads[-1].start()
    residual, pressure, conductivity, land_use = (
        ref[name] for name in ("residual", "pressure", "conductivity", "land_use")
    )
    started = []

    def remote(src, dst, index, dx, dy):
        copy = pltpu.make_async_remote_copy(
            src_ref=src, dst_ref=dst, send_sem=ref["send"].at[index], recv_sem=ref["recv"].at[index],
            device_id=device(dx, dy), device_id_type=MESH,
        )
        copy.start()
        started.append(copy)
        return copy

    row8 = iota((8, 128), 0)
    lane8 = iota((8, 128), 1)

    def send_fine(arrays):
        sy, ry, rc = ref["e0_sy"], ref["e0_ry"], ref["e0_rc"]
        copies = []
        for k, array in enumerate(arrays):
            for side, (own, there, dx) in enumerate(((0, 16, -1), (8, 24, 1))):
                copies.append(
                    remote(
                        array.at[:, pl.ds(own, 8), pl.ds(0, 256)],
                        array.at[:, pl.ds(there, 8), pl.ds(0, 256)],
                        B_E0 + 2 * k + side, dx, 0,
                    )
                )
        lane = iota((16, 128), 1)
        for k, array in enumerate(arrays):
            low = jnp.zeros((16, 128), F32)
            high = jnp.zeros((16, 128), F32)
            for z in range(NZ):
                here = between(lane, 8 * z, 8)
                low = jnp.where(here, rot(array[z, 0:16, 0:128], 8 * z, 1), low)
                high = jnp.where(here, rot(array[z, 0:16, 128:256], 8 * z + 8, 1), high)
            sy[0, k] = low
            sy[1, k] = high
        first, last = pl.ds(0, 8), pl.ds(8, 8)
        moves = (
            (sy.at[0], ry.at[0], 0, -1),
            (sy.at[1], ry.at[1], 0, 1),
            (sy.at[0, :, first], rc.at[0], -1, -1),
            (sy.at[0, :, last], rc.at[1], 1, -1),
            (sy.at[1, :, first], rc.at[2], -1, 1),
            (sy.at[1, :, last], rc.at[3], 1, 1),
        )
        for i, (src, dst, dx, dy) in enumerate(moves):
            copies.append(remote(src, dst, B_E0 + 6 + i, dx, dy))
        return copies

    def receive_fine(copies, arrays, fills):
        for copy in copies:
            copy.wait_recv()
        ry, rc = ref["e0_ry"], ref["e0_rc"]
        lane = iota((32, 128), 1)
        for k, (array, fill) in enumerate(zip(arrays, fills)):
            north = jnp.concatenate([ry[0, k], rc[0, k], rc[1, k]], axis=0)
            south = jnp.concatenate([ry[1, k], rc[2, k], rc[3, k]], axis=0)
            for z in range(NZ):
                value = jnp.where(lane >= 120, rot(south, -8 * (z + 1), 1), fill)
                array[z, :, 256:384] = jnp.where(lane < 8, rot(north, -8 * z, 1), value)

    def send_wide(name, base, get):
        sx, sy, rx, ry = (ref[f"{name}_{kind}"] for kind in ("sx", "sy", "rx", "ry"))
        for a in range(sx.shape[0]):
            values = [get(a, z) for z in range(NZ)]
            for t in range(4):
                left = jnp.where(row8 < 4, values[t], rot(values[t + 4], 4, 0))
                right = jnp.where(row8 < 4, values[t + 8], rot(values[t + 12], 4, 0))
                tile = jnp.where(lane8 < 64, left, rot(right, 64, 1))
                sx[a, t] = tile
                rx[REACH, a, t] = tile
            low = jnp.zeros((8, 128), F32)
            high = jnp.zeros((8, 128), F32)
            for q in range(8):
                both = jnp.where(row8 < 4, values[q], rot(values[q + 8], 4, 0))
                here = between(lane8, 16 * q, 16)
                low = jnp.where(here, rot(both, 16 * q, 1), low)
                high = jnp.where(here, rot(both, 16 * q - 48, 1), high)
            sy[0, a] = low
            sy[1, a] = high
        copies = []
        for d in SIDES:
            copies.append(remote(sx, rx.at[REACH - d], base + len(copies), d, 0))
        for side, dy in ((0, -1), (1, 1)):
            for d in range(-REACH, REACH + 1):
                copies.append(remote(sy.at[side], ry.at[side, REACH - d], base + len(copies), d, dy))
        return copies

    def receive_wide(name, copies, targets, fills):
        for copy in copies:
            copy.wait_recv()
        rx, ry = ref[f"{name}_rx"], ref[f"{name}_ry"]
        empty = jnp.zeros((8, 128), F32)

        def join(first, second):
            return (
                jnp.where(row8 < 4, first, rot(second, 4, 0)),
                jnp.where(row8 < 4, rot(first, 4, 0), second),
            )

        for a, (target, fill) in enumerate(zip(targets, fills)):
            for p, (k0, k1) in enumerate(((0, 1), (2, 3), (None, -3), (-2, -1))):
                layers = [None] * NZ
                for t in range(4):
                    first = empty if k0 is None else rx[REACH + k0, a, t]
                    for i, both in enumerate(join(first, rx[REACH + k1, a, t])):
                        layers[t + 4 * i] = both
                        layers[t + 4 * i + 8] = rot(both, 64, 1)
                sides = []
                for side in (0, 1):
                    first = empty if k0 is None else ry[side, REACH + k0, a]
                    sides.append(join(first, ry[side, REACH + k1, a]))
                for z in range(NZ):
                    q = z % 8
                    north = rot(sides[0][z // 8], 64 - 16 * q, 1)
                    south = rot(sides[1][z // 8], 112 - 16 * q, 1)
                    value = jnp.where(lane8 < 80, north, jnp.where(lane8 >= 112, south, fill))
                    value = jnp.where(lane8 < 64, layers[z], value)
                    if k0 is None:
                        value = jnp.where(row8 < 4, fill, value)
                    target[z, 8 * p : 8 * p + 8, :] = value

    def send_u1():
        sx, sy, rx, ry, rc = (ref[f"v1_{kind}"] for kind in ("sx", "sy", "rx", "ry", "rc"))
        low = jnp.zeros((8, 128), F32)
        high = jnp.zeros((8, 128), F32)
        for z in range(NZ):
            u = ref["u1"][z, 0:8, 0:128]
            if z % 2 == 0:
                before = u
            else:
                sx[0, z // 2] = jnp.where(row8 < 4, before, rot(u, 4, 0))
                sx[1, z // 2] = jnp.where(row8 < 4, rot(before, 4, 0), u)
            here = between(lane8, 4 * z, 4)
            low = jnp.where(here, rot(u, 4 * z, 1), low)
            high = jnp.where(here, rot(u, 4 * z + 4, 1), high)
        sy[0] = low
        sy[1] = high
        moves = (
            (sx.at[0], rx.at[0], -1, 0),
            (sx.at[1], rx.at[1], 1, 0),
            (sy.at[0], ry.at[0], 0, -1),
            (sy.at[1], ry.at[1], 0, 1),
            (sy.at[0], rc.at[0], -1, -1),
            (sy.at[0], rc.at[1], 1, -1),
            (sy.at[1], rc.at[2], -1, 1),
            (sy.at[1], rc.at[3], 1, 1),
        )
        return [remote(src, dst, B_V1 + i, dx, dy) for i, (src, dst, dx, dy) in enumerate(moves)]

    def receive_u1(copies):
        for copy in copies:
            copy.wait_recv()
        rx, ry, rc = (ref[f"v1_{kind}"] for kind in ("rx", "ry", "rc"))
        lane = iota((16, 128), 1)
        north = jnp.concatenate([ry[0], jnp.where(row8 < 4, rc[0], rc[1])], axis=0)
        south = jnp.concatenate([ry[1], jnp.where(row8 < 4, rc[2], rc[3])], axis=0)
        u = ref["u1"]
        for z in range(NZ):
            east, west = rx[0, z // 2], rx[1, z // 2]
            if z % 2 == 0:
                value = jnp.where(row8 < 4, east, rot(west, 4, 0))
            else:
                value = jnp.where(row8 < 4, rot(east, 4, 0), west)
            u[z, 8:16, 0:128] = value
            value = jnp.where(lane >= 124, rot(south, -4 * (z + 1), 1), 0.0)
            u[z, :, 128:256] = jnp.where(lane < 4, rot(north, -4 * z, 1), value)

    def factor(level):
        diag, down, g, inv = (ref[f"{name}{level}"] for name in ("diag", "D", "g", "inv"))
        before = None
        for z in range(NZ):
            pivot = diag[z]
            if z > 0:
                pivot = pivot - before * down[z - 1]
            inverse = 1.0 / pivot
            inv[z] = inverse
            if z < NZ - 1:
                before = down[z] * inverse
                g[z] = before

    def back_substitute(level, update):
        g, inv, f = (ref[f"{name}{level}"] for name in ("g", "inv", "f"))
        value = f[NZ - 1] * inv[NZ - 1]
        update(NZ - 1, value)
        for z in range(NZ - 2, -1, -1):
            value = f[z] * inv[z] + g[z] * value
            update(z, value)

    def first_sweep(level):
        g, f, rhs, u = (ref[f"{name}{level}"] for name in ("g", "f", "rhs", "u"))
        value = rhs[0]
        f[0] = value
        for z in range(1, NZ):
            value = rhs[z] + g[z - 1] * value
            f[z] = value

        def update(z, solved):
            u[z] = OMEGA * solved

        back_substitute(level, update)

    def lateral(level, z, u):
        east, north = ref[f"E{level}"][z], ref[f"N{level}"][z]
        return (
            east * rot(u, -1, 0) + rot(east * u, 1, 0) + north * rot(u, -1, 1) + rot(north * u, 1, 1)
        )

    def sweep(level):
        g, f, rhs, u = (ref[f"{name}{level}"] for name in ("g", "f", "rhs", "u"))
        value = None
        for z in range(NZ):
            right = rhs[z] + lateral(level, z, u[z])
            value = right if z == 0 else right + g[z - 1] * value
            f[z] = value

        def update(z, solved):
            old = u[z]
            u[z] = old + OMEGA * (solved - old)

        back_substitute(level, update)

    def remainder(level, z):
        diag, down, rhs, u = (ref[f"{name}{level}"] for name in ("diag", "D", "rhs", "u"))
        here = u[z]
        value = rhs[z] + lateral(level, z, here) - diag[z] * here
        if z < NZ - 1:
            value = value + down[z] * u[z + 1]
        if z > 0:
            value = value + down[z - 1] * u[z - 1]
        return value

    PIECES = (
        ((0, 256, 256, 256), (256, 128, 64, 128)),
        ((0, 128, 128, 128),),
        ((0, 128, 96, 128),),
        ((0, 128, 128, 32),),
    )
    ROWS = (32, 8, 32, 8)

    def lane_matrix(piece, kind, transpose=False):
        _, count, turn, limit = piece
        shape = (128, count) if transpose else (count, 128)
        fine = iota(shape, 1 if transpose else 0)
        coarse = iota(shape, 0 if transpose else 1)
        hit = (((fine >> 1) + jnp.where(fine >= turn, 64, 0)) == coarse) & (fine < limit)
        if kind != "sum":
            hit = hit & ((fine & 1) == (1 if kind == "odd" else 0))
        return jnp.where(hit, 1.0, 0.0).astype(F32)

    def put_rows(buffer, level, z, value):
        for t in range(YR[level] // 128 if len(PIECES[level]) > 1 else 1):
            buffer[z, t, 0 : ROWS[level], :] = value[0 : ROWS[level], 128 * t : 128 * (t + 1)]

    def row_half(buffer, level, piece, z, odd):
        start, count = piece[0], piece[1]
        parts = []
        for t in range(start // 128, (start + count) // 128):
            rows = [buffer[z, t, pl.ds(i + odd, 8, stride=2), :] for i in range(0, ROWS[level], 16)]
            parts.append(rows[0] if len(rows) == 1 else jnp.concatenate(rows, axis=0))
        return parts[0] if len(parts) == 1 else jnp.concatenate(parts, axis=1)

    def coarse_rows(level):
        return max(8, ROWS[level] // 2)

    def layers_of(value, rows):
        return [value[rows * z : rows * (z + 1)] for z in range(NZ)]

    def keep_own(level, value, fill):
        rows, lanes = (4, 64) if level == 2 else (1, 16)
        return jnp.where((row8 < rows) & (lane8 < lanes), value, fill)

    def restrict(level):
        for z in range(NZ):
            put_rows(ref["ta"], level, z, remainder(level, z))
        pieces = []
        for piece in PIECES[level]:
            summed = jnp.concatenate(
                [
                    row_half(ref["ta"], level, piece, z, 0) + row_half(ref["ta"], level, piece, z, 1)
                    for z in range(NZ)
                ],
                axis=0,
            )
            pieces.append(layers_of(exact_dot(summed, lane_matrix(piece, "sum")), coarse_rows(level)))
        return pieces

    def coarsen(level):
        names = ("E", "N", "D", "diag")
        buffers = [ref[name] for name in ("ta", "tb", "tc", "td")]
        for z in range(NZ):
            for name, buffer in zip(names, buffers):
                put_rows(buffer, level, z, ref[f"{name}{level}"][z])
        pieces = []
        for piece in PIECES[level]:
            odd_e, sum_n, sum_d, sum_g = [], [], [], []
            for z in range(NZ):
                (e0, e1), (n0, n1), (d0, d1), (g0, g1) = (
                    [row_half(buffer, level, piece, z, odd) for odd in (0, 1)] for buffer in buffers
                )
                odd_e.append(e1)
                sum_n.append(n0 + n1)
                sum_d.append(d0 + d1)
                sum_g.append(g0 + g1 - 2.0 * e0)
            total = lane_matrix(piece, "sum")
            rows = coarse_rows(level)
            east = exact_dot(jnp.concatenate(odd_e, axis=0), total)
            down = exact_dot(jnp.concatenate(sum_d, axis=0), total)
            north = jnp.concatenate(sum_n, axis=0)
            diagonal = exact_dot(jnp.concatenate(sum_g, axis=0), total) - 2.0 * exact_dot(
                north, lane_matrix(piece, "even")
            )
            north = exact_dot(north, lane_matrix(piece, "odd"))
            pieces.append([layers_of(value, rows) for value in (east, north, down, diagonal)])
        return pieces

    def prolong(level, coarse):
        buffer = ref["ta"]
        u = ref[f"u{level}"]
        pieces = {
            0: ((0, 256, 256, 256), (256, 128, 64, 128)),
            1: ((0, 128, 128, 128), (128, 128, 128, 128)),
            2: ((0, 128, 96, 128),),
            3: ((0, 128, 96, 128),),
        }[level]
        for i, piece in enumerate(pieces):
            value = jnp.concatenate([coarse(i, z) for z in range(NZ)], axis=0)
            rows = value.shape[0] // NZ
            fine = exact_dot(value, lane_matrix(piece, "sum", transpose=True))
            start, count = piece[0], piece[1]
            for z in range(NZ):
                for t in range(count // 128):
                    for r in range(0, rows, 8):
                        part = fine[rows * z + r : rows * z + r + 8, 128 * t : 128 * (t + 1)]
                        for odd in (0, 1):
                            buffer[z, start // 128 + t, pl.ds(2 * r + odd, 8, stride=2), :] = part
        for z in range(NZ):
            add = [buffer[z, t, 0 : XR[level], :] for t in range(YR[level] // 128)]
            u[z] = u[z] + (add[0] if len(add) == 1 else jnp.concatenate(add, axis=1))

    at_sum = (lane8 == 48) & (row8 == 0)

    def pack_tile(values):
        row16 = iota((16, 128), 0)
        lane16 = iota((16, 128), 1)
        stacked = jnp.zeros((16, 128), F32)
        for z in range(NZ):
            stacked = jnp.where(row16 == z, jnp.broadcast_to(values[z][0:1], (16, 128)), stacked)
        stacked = jnp.where(lane16 < 16, stacked, 0.0)
        return rot(stacked[0:8], 16, 1) + rot(stacked[8:16], 80, 1)

    def total_of(value):
        return jnp.sum(jnp.sum(value, axis=1, keepdims=True), axis=0, keepdims=True)

    def gather_columns(name, tiles, part, base):
        for a, tile in enumerate(tiles):
            ref[f"{name}_s1"][a] = jnp.where(at_sum, part, tile) if a == 0 else tile
        return [
            remote(ref[f"{name}_s1"], ref[f"{name}_r1"].at[d], base + d - 1, 0, d) for d in range(1, GY)
        ]

    def gather_rows(name, copies, base):
        for copy in copies:
            copy.wait_recv()
        s1, r1, s2, r2 = (ref[f"{name}_{kind}"] for kind in ("s1", "r1", "s2", "r2"))
        for a in range(s1.shape[0]):
            tiles = [s1[a]] + [r1[d, a] for d in range(1, GY)]
            clean = [jnp.where(at_sum, 0.0, tiles[i]) if a == 0 else tiles[i] for i in (0, 1, GY - 1)]
            window = clean[0] + rot(clean[1], -16, 1) + rot(clean[2], 16, 1)
            if a == 0:
                parts = tiles[0]
                for tile in tiles[1:]:
                    parts = parts + tile
                window = jnp.where(at_sum, parts, window)
            s2[a] = window
            r2[a, 0:8, :] = window
        return [
            remote(s2, r2.at[:, pl.ds(8 * (GX - d), 8), :], base + d - 1, d, 0) for d in range(1, GX)
        ]

    def coarse_layer(buffer, a, z):
        sub, half = z % 8, z // 8
        pieces = [buffer[a, pl.ds(64 * i + sub, 8, stride=8), :] for i in range(4)]
        low = jnp.concatenate(pieces[0:2], axis=0)
        high = jnp.concatenate(pieces[2:4], axis=0)
        lane = iota((16, 128), 1)
        if half == 0:
            return jnp.where(lane < 64, low, rot(high, 64, 1))
        return jnp.where(lane < 64, rot(low, 64, 1), high)

    def coarse_sum(buffer):
        value = jnp.where(at_sum, buffer[0, 0:8, :], 0.0)
        for k in range(1, GX):
            value = value + jnp.where(at_sum, buffer[0, 8 * k : 8 * k + 8, :], 0.0)
        return total_of(value)

    def coarse_at(name, z):
        return ref[name][16 * z : 16 * z + 16, :]

    for copy in loads:
        copy.wait()
    use = land_use[...]
    table = jnp.zeros(use.shape, F32)
    fraction = jnp.zeros(use.shape, F32)
    for category in range(CLASSES):
        table = table + jnp.where(use == category, storage_table[category], 0.0)
        fraction = fraction + jnp.where(use == category, return_table[category], 0.0)
    cells, rates, returns = well_cells[...], well_rates[...], return_cells[...]
    wells = rates.shape[1]

    def hits(count, index):
        return iota((count, wells), 0) == index

    def outer(count, index_row, index_column):
        left = jnp.where(hits(count, index_row), rates, 0.0)
        right = jnp.where(hits(256, index_column), 1.0, 0.0).astype(F32)
        return lax.dot_general(
            left, right, (((1,), (1,)), ((), ())),
            precision=lax.Precision.HIGHEST, preferred_element_type=F32,
        )

    pumped = outer(256, cells >> 8, cells & 255)
    recharge = fraction * outer(16, returns >> 8, returns & 255)
    storage_sum = jnp.zeros((16, 256), F32)
    for z in range(NZ):
        relief = jnp.exp(ALPHA * jnp.minimum(pressure[z], 0.0))
        ref["P0"][z, 0:16, 0:256] = conductivity[z] * relief
        storage = table * relief
        ref["S0"][z, 0:16, 0:256] = storage
        storage_sum = storage_sum + storage
        source = residual[z] - pumped[16 * z : 16 * z + 16]
        if z == 0:
            source = source + recharge
        ref["rhs0"][z, 0:16, 0:256] = source
    first = [ref["P0"], ref["S0"], ref["rhs0"]]
    pl.semaphore_wait(barrier, len(peers))
    copies = send_fine(first)
    receive_fine(copies, first, (0.0, 1.0, 0.0))

    flags = [
        jnp.where(inside, 1.0, 0.0).astype(F32)
        for inside in (gx < GX - 1, gx > 0, gy < GY - 1, gy > 0)
    ]
    row = iota((32, 384), 0)
    lane = iota((32, 384), 1)
    inside = jnp.where(row < 16, 1.0, jnp.where(row < 24, flags[0], flags[1]))
    inside = inside * jnp.where(lane < 256, 1.0, jnp.where(lane < 320, flags[2], flags[3]))

    def harmonic(first_value, second_value):
        return 2.0 * first_value * second_value / (first_value + second_value + 1e-30)

    above = None
    for z in range(NZ):
        here = ref["P0"][0] * inside if z == 0 else beneath
        east = harmonic(here, rot(here, -1, 0))
        north = harmonic(here, rot(here, -1, 1))
        diagonal = ref["S0"][z] + east + rot(east, 1, 0) + north + rot(north, 1, 1)
        if z > 0:
            diagonal = diagonal + above
        if z < NZ - 1:
            beneath = ref["P0"][z + 1] * inside
            above = VERTICAL * harmonic(here, beneath)
            diagonal = diagonal + above
        else:
            above = jnp.zeros_like(here)
        ref["D0"][z] = above
        ref["E0"][z] = east
        ref["N0"][z] = north
        ref["diag0"][z] = diagonal
    factor(0)

    def place(level, names, pieces):
        for z in range(NZ):
            for k, name in enumerate(names):
                fill = 1.0 if name == "diag" else 0.0
                target = ref[f"{name}{level}"]
                if level == 1:
                    target[z, :, 0:128] = pieces[0][k][z]
                    lane = iota((16, 128), 1)
                    target[z, :, 128:256] = jnp.where((lane < 32) | (lane >= 96), pieces[1][k][z], fill)
                else:
                    lane = iota((16, 128), 1)
                    target[z] = jnp.where((lane < 48) | (lane >= 112), pieces[0][k][z], fill)

    names = ("E", "N", "D", "diag")
    fills = (0.0, 0.0, 0.0, 1.0)
    place(1, names, coarsen(0))
    (coarse2,) = coarsen(1)
    own2 = [[keep_own(2, coarse2[k][z], fills[k]) for z in range(NZ)] for k in range(4)]
    copies_c2 = send_wide("c2", B_C2, lambda k, z: own2[k][z])

    first_sweep(0)
    sweep(0)
    place(1, ("rhs",), [[piece] for piece in restrict(0)])
    factor(1)
    first_sweep(1)
    sweep(1)
    (values,) = restrict(1)
    copies_x2 = send_wide("x2", B_X2, lambda k, z: values[z])
    copies_v1 = send_u1()

    receive_wide("c2", copies_c2, [ref[f"{name}2"] for name in names], fills)
    place(3, names, coarsen(2))
    (bottom,) = coarsen(3)
    tiles = [pack_tile(bottom[k]) for k in (3, 0, 1, 2)]
    stage = gather_columns("gc", tiles, total_of(storage_sum), N_HALO)
    factor(2)
    factor(3)
    stage_c = gather_rows("gc", stage, N_HALO + GY - 1)
    receive_wide("x2", copies_x2, [ref["rhs2"]], (0.0,))
    first_sweep(2)
    sweep(2)
    place(3, ("rhs",), [[piece] for piece in restrict(2)])
    first_sweep(3)
    sweep(3)
    (values,) = restrict(3)
    tile = pack_tile(values)
    stage = gather_columns("gr", [tile], total_of(tile), N_HALO + GY - 1 + GX - 1)
    receive_u1(copies_v1)
    stage_r = gather_rows("gr", stage, N_HALO + 2 * (GY - 1) + GX - 1)

    for copy in stage_c:
        copy.wait_recv()
    lane = iota((16, 128), 1)
    row = iota((16, 128), 0)
    gap = (lane & 63) >= 48
    before = None
    for z in range(NZ):
        pivot = jnp.where(gap, 1.0, coarse_layer(ref["gc_r2"], 0, z))
        if z > 0:
            pivot = pivot - before * below
        inverse = 1.0 / pivot
        below = coarse_layer(ref["gc_r2"], 3, z)
        before = below * inverse
        at = slice(16 * z, 16 * z + 16)
        ref["inv4"][at, :] = inverse
        ref["g4"][at, :] = before
        ref["E4"][at, :] = coarse_layer(ref["gc_r2"], 1, z)
        ref["N4"][at, :] = coarse_layer(ref["gc_r2"], 2, z)
    storage_total = coarse_sum(ref["gc_r2"])
    for copy in stage_r:
        copy.wait_recv()
    shift = coarse_sum(ref["gr_r2"]) / storage_total
    for z in range(NZ):
        at = slice(16 * z, 16 * z + 16)
        ref["rhs4"][at, :] = coarse_layer(ref["gr_r2"], 0, z)
        ref["u4"][at, :] = jnp.broadcast_to(shift, (16, 128))

    def coarse_sweep(step, carry):
        value = None
        for z in range(NZ):
            u, east, north = coarse_at("u4", z), coarse_at("E4", z), coarse_at("N4", z)
            from_e = rot(u, -1, 0)
            from_e = jnp.where(row == 15, rot(from_e, 64, 1), from_e)
            from_w = rot(east * u, 1, 0)
            from_w = jnp.where(row == 0, rot(from_w, 64, 1), from_w)
            right = coarse_at("rhs4", z) + east * from_e + from_w + north * rot(u, -1, 1) + rot(north * u, 1, 1)
            value = right if z == 0 else right + coarse_at("g4", z - 1) * value
            ref["f4"][16 * z : 16 * z + 16, :] = value
        for z in range(NZ - 1, -1, -1):
            solved = coarse_at("f4", z) * coarse_at("inv4", z)
            value = solved if z == NZ - 1 else solved + coarse_at("g4", z) * value
            old = coarse_at("u4", z)
            ref["u4"][16 * z : 16 * z + 16, :] = old + OMEGA * (value - old)
        return carry

    lax.fori_loop(0, COARSE_SWEEPS, coarse_sweep, 0)

    def coarsest(_, z):
        value = coarse_at("u4", z)
        both = jnp.where(row8 < 4, value[0:8], rot(value[8:16], 64, 1))
        both = rot(both, -16, 1)
        return jnp.where((lane8 < 24) | (lane8 >= 112), both, 0.0)

    def from2(i, z):
        value = jnp.where(row8 < 6, ref["u2"][z, 0:8, :], ref["u2"][z, 24:32, :])
        return value if i == 0 else rot(value, 64, 1)

    prolong(3, coarsest)
    sweep(3)
    sweep(3)
    prolong(2, lambda i, z: ref["u3"][z])
    sweep(2)
    sweep(2)
    prolong(1, from2)
    sweep(1)
    sweep(1)
    prolong(0, lambda i, z: ref["u1"][z, :, 128 * i : 128 * (i + 1)])
    sweep(0)
    sweep(0)
    for z in range(NZ):
        out[z] = ref["u0"][z, 0:16, 0:256]
    for copy in started:
        copy.wait_send()


def shards(
    newton_residual, pressure_head, conductivity, land_use, storage_table, return_table,
    well_cells, well_rates, return_cells,
):
    vmem = pl.BlockSpec(memory_space=pltpu.VMEM)
    hbm = pl.BlockSpec(memory_space=pl.ANY)
    smem = pl.BlockSpec(memory_space=pltpu.SMEM)
    wells = well_cells.shape[-1]
    return pl.pallas_call(
        kernel,
        out_shape=jax.ShapeDtypeStruct(newton_residual.shape, F32),
        in_specs=[hbm] * 4 + [smem] * 2 + [vmem] * 3,
        out_specs=vmem,
        scratch_shapes=list(PLAN.values()),
        compiler_params=pltpu.CompilerParams(
            collective_id=0, has_side_effects=True, vmem_limit_bytes=60 * 1024 * 1024
        ),
    )(
        newton_residual, pressure_head, conductivity, land_use, storage_table, return_table,
        well_cells.reshape(1, wells), well_rates.reshape(1, wells), return_cells.reshape(1, wells),
    )


def solution(mesh):
    return jax.shard_map(
        shards,
        mesh=mesh,
        in_specs=(
            P(None, "gx", "gy"),
            P(None, "gx", "gy"),
            P(None, "gx", "gy"),
            P("gx", "gy"),
            P(),
            P(),
            P("gx", "gy", None),
            P("gx", "gy", None),
            P("gx", "gy", None),
        ),
        out_specs=P(None, "gx", "gy"),
        check_vma=False,
    )
```

```python
import functools

import jax
import jax.numpy as jnp
from jax import lax
from jax.experimental import pallas as pl
from jax.experimental.pallas import tpu as pltpu
from jax.sharding import PartitionSpec as P

NZ = 16
CLASSES = 8
COARSE_SWEEPS = 12
OMEGA = 0.8
VERTICAL = 4.0
ALPHA = 0.5
F32 = jnp.float32
MESH = pl.DeviceIdType.MESH

NX = (16, 8, 4, 2)
NY = (256, 128, 64, 32)
XR = (32, 16, 32, 16)
YR = (384, 256, 128, 128)
REACH = 3
SIDES = [d for d in range(-REACH, REACH + 1) if d != 0]
GY, GX = 8, 32
N_E0 = 24
N_WIDE = 6 * REACH + 2
N_V1 = 8
B_E0 = 0
B_C2 = B_E0 + N_E0
B_X2 = B_C2 + N_WIDE
B_V1 = B_X2 + N_WIDE
N_HALO = B_V1 + N_V1
GZ, GXX = 8, 4
B_GC1 = N_HALO
B_GCZ = B_GC1 + GY - 1
B_GCX = B_GCZ + GZ - 1
B_GR1 = B_GCX + GZ * (GXX - 1)
B_GR2 = B_GR1 + GY - 1
N_SEM = B_GR2 + GX - 1
LEVEL_ARRAYS = ("E", "N", "D", "diag", "g", "inv", "rhs", "u", "f")


def rot(value, shift, axis):
    shift %= value.shape[axis]
    return value if shift == 0 else pltpu.roll(value, shift, axis)


def iota(shape, axis):
    return lax.broadcasted_iota(jnp.int32, shape, axis)


def between(index, start, count):
    return (index >= start) & (index < start + count)


def exact_dot(left, right):
    return jnp.dot(left, right, precision=lax.Precision.HIGHEST, preferred_element_type=F32)


def scratch_plan():
    plan = {}
    for level in range(4):
        for name in LEVEL_ARRAYS:
            plan[f"{name}{level}"] = pltpu.VMEM((NZ, XR[level], YR[level]), F32)
    for name in ("E", "N", "g", "inv", "rhs", "u", "f"):
        plan[f"{name}2c"] = pltpu.VMEM((NZ, 16, 128), F32)
    plan["P0"] = pltpu.VMEM((NZ, XR[0], YR[0]), F32)
    plan["S0"] = pltpu.VMEM((NZ, XR[0], YR[0]), F32)
    for name in ("E4", "N4", "g4", "inv4", "rhs4", "u4", "f4"):
        plan[name] = pltpu.VMEM((NZ * 16, 128), F32)
    for name in ("ta", "tb", "tc", "td"):
        plan[name] = pltpu.VMEM((NZ, 3, 32, 128), F32)
    plan["e0_sy"] = pltpu.VMEM((2, 3, 16, 128), F32)
    plan["e0_ry"] = pltpu.VMEM((2, 3, 16, 128), F32)
    plan["e0_rc"] = pltpu.VMEM((4, 3, 8, 128), F32)
    for name, count in (("c2", 4), ("x2", 1)):
        plan[f"{name}_sx"] = pltpu.VMEM((count, 4, 8, 128), F32)
        plan[f"{name}_rx"] = pltpu.VMEM((2 * REACH + 1, count, 4, 8, 128), F32)
        plan[f"{name}_sy"] = pltpu.VMEM((2, count, 8, 128), F32)
        plan[f"{name}_ry"] = pltpu.VMEM((2, 2 * REACH + 1, count, 8, 128), F32)
    for kind in ("s", "r"):
        plan[f"v1_{kind}x"] = pltpu.VMEM((2, 8, 8, 128), F32)
        plan[f"v1_{kind}y"] = pltpu.VMEM((2, 8, 128), F32)
    plan["v1_rc"] = pltpu.VMEM((4, 8, 128), F32)
    for name in ("residual", "pressure", "conductivity"):
        plan[name] = pltpu.VMEM((NZ, NX[0], NY[0]), F32)
    plan["land_use"] = pltpu.VMEM((NX[0], NY[0]), jnp.int32)
    plan["load"] = pltpu.SemaphoreType.DMA((4,))
    for name, count in (("gc", 4), ("gr", 1)):
        plan[f"{name}_s1"] = pltpu.VMEM((count, 8, 128), F32)
        plan[f"{name}_r1"] = pltpu.VMEM((GY, count, 8, 128), F32)
        plan[f"{name}_s2"] = pltpu.VMEM((count, 8, 128), F32)
        plan[f"{name}_r2"] = pltpu.VMEM((count, GX * 8, 128), F32)
    plan["send"] = pltpu.SemaphoreType.DMA((N_SEM,))
    plan["recv"] = pltpu.SemaphoreType.DMA((N_SEM,))
    return plan


PLAN = scratch_plan()


def kernel(
    residual_in, pressure_in, conductivity_in, land_use_in, storage_table, return_table,
    well_cells, well_rates, return_cells, out, *scratch,
):
    ref = dict(zip(PLAN, scratch))
    gx = lax.axis_index("gx")
    gy = lax.axis_index("gy")

    def device(dx, dy):
        return (lax.rem(gx + (dx + GX), GX), lax.rem(gy + (dy + GY), GY))

    peers = [(dx, dy) for dx in SIDES for dy in (-1, 1)]
    peers += [(0, d) for d in range(1, GY)] + [(d, 0) for d in range(1, GX)]
    barrier = pltpu.get_barrier_semaphore()
    for dx, dy in peers:
        pl.semaphore_signal(barrier, inc=1, device_id=device(dx, dy), device_id_type=MESH)

    loads = []
    for i, (name, source) in enumerate(
        (("land_use", land_use_in), ("pressure", pressure_in), ("conductivity", conductivity_in), ("residual", residual_in))
    ):
        loads.append(pltpu.make_async_copy(source, ref[name], ref["load"].at[i]))
        loads[-1].start()
    residual, pressure, conductivity, land_use = (
        ref[name] for name in ("residual", "pressure", "conductivity", "land_use")
    )
    started = []

    def remote(src, dst, index, dx, dy):
        copy = pltpu.make_async_remote_copy(
            src_ref=src, dst_ref=dst, send_sem=ref["send"].at[index], recv_sem=ref["recv"].at[index],
            device_id=device(dx, dy), device_id_type=MESH,
        )
        copy.start()
        started.append(copy)
        return copy

    row8 = iota((8, 128), 0)
    lane8 = iota((8, 128), 1)

    def send_fine(array, k):
        sy, ry, rc = ref["e0_sy"], ref["e0_ry"], ref["e0_rc"]
        base = B_E0 + 8 * k
        copies = []
        for side, (own, there, dx) in enumerate(((0, 16, -1), (8, 24, 1))):
            copies.append(
                remote(
                    array.at[:, pl.ds(own, 8), pl.ds(0, 256)],
                    array.at[:, pl.ds(there, 8), pl.ds(0, 256)],
                    base + side, dx, 0,
                )
            )
        lane = iota((16, 128), 1)
        low = jnp.zeros((16, 128), F32)
        high = jnp.zeros((16, 128), F32)
        for z in range(NZ):
            here = between(lane, 8 * z, 8)
            low = jnp.where(here, rot(array[z, 0:16, 0:128], 8 * z, 1), low)
            high = jnp.where(here, rot(array[z, 0:16, 128:256], 8 * z + 8, 1), high)
        sy[0, k] = low
        sy[1, k] = high
        first, last = pl.ds(0, 8), pl.ds(8, 8)
        moves = (
            (sy.at[0, k], ry.at[0, k], 0, -1),
            (sy.at[1, k], ry.at[1, k], 0, 1),
            (sy.at[0, k, first], rc.at[0, k], -1, -1),
            (sy.at[0, k, last], rc.at[1, k], 1, -1),
            (sy.at[1, k, first], rc.at[2, k], -1, 1),
            (sy.at[1, k, last], rc.at[3, k], 1, 1),
        )
        for i, (src, dst, dx, dy) in enumerate(moves):
            copies.append(remote(src, dst, base + 2 + i, dx, dy))
        return copies

    def receive_fine(copies, array, k, fill):
        for copy in copies:
            copy.wait_recv()
        ry, rc = ref["e0_ry"], ref["e0_rc"]
        lane = iota((32, 128), 1)
        north = jnp.concatenate([ry[0, k], rc[0, k], rc[1, k]], axis=0)
        south = jnp.concatenate([ry[1, k], rc[2, k], rc[3, k]], axis=0)
        for z in range(NZ):
            value = jnp.where(lane >= 120, rot(south, -8 * (z + 1), 1), fill)
            array[z, :, 256:384] = jnp.where(lane < 8, rot(north, -8 * z, 1), value)

    def send_wide(name, base, get):
        sx, sy, rx, ry = (ref[f"{name}_{kind}"] for kind in ("sx", "sy", "rx", "ry"))
        for a in range(sx.shape[0]):
            values = [get(a, z) for z in range(NZ)]
            for t in range(4):
                left = jnp.where(row8 < 4, values[t], rot(values[t + 4], 4, 0))
                right = jnp.where(row8 < 4, values[t + 8], rot(values[t + 12], 4, 0))
                tile = jnp.where(lane8 < 64, left, rot(right, 64, 1))
                sx[a, t] = tile
                rx[REACH, a, t] = tile
            low = jnp.zeros((8, 128), F32)
            high = jnp.zeros((8, 128), F32)
            for q in range(8):
                both = jnp.where(row8 < 4, values[q], rot(values[q + 8], 4, 0))
                here = between(lane8, 16 * q, 16)
                low = jnp.where(here, rot(both, 16 * q, 1), low)
                high = jnp.where(here, rot(both, 16 * q - 48, 1), high)
            sy[0, a] = low
            sy[1, a] = high
        copies = []
        for d in SIDES:
            copies.append(remote(sx, rx.at[REACH - d], base + len(copies), d, 0))
        for side, dy in ((0, -1), (1, 1)):
            for d in range(-REACH, REACH + 1):
                copies.append(remote(sy.at[side], ry.at[side, REACH - d], base + len(copies), d, dy))
        return copies

    def receive_wide(name, copies, targets, fills):
        for copy in copies:
            copy.wait_recv()
        rx, ry = ref[f"{name}_rx"], ref[f"{name}_ry"]
        empty = jnp.zeros((8, 128), F32)

        def join(first, second):
            return (
                jnp.where(row8 < 4, first, rot(second, 4, 0)),
                jnp.where(row8 < 4, rot(first, 4, 0), second),
            )

        for a, (target, fill) in enumerate(zip(targets, fills)):
            for p, (k0, k1) in enumerate(((0, 1), (2, 3), (None, -3), (-2, -1))):
                layers = [None] * NZ
                for t in range(4):
                    first = empty if k0 is None else rx[REACH + k0, a, t]
                    for i, both in enumerate(join(first, rx[REACH + k1, a, t])):
                        layers[t + 4 * i] = both
                        layers[t + 4 * i + 8] = rot(both, 64, 1)
                sides = []
                for side in (0, 1):
                    first = empty if k0 is None else ry[side, REACH + k0, a]
                    sides.append(join(first, ry[side, REACH + k1, a]))
                for z in range(NZ):
                    q = z % 8
                    north = rot(sides[0][z // 8], 64 - 16 * q, 1)
                    south = rot(sides[1][z // 8], 112 - 16 * q, 1)
                    value = jnp.where(lane8 < 80, north, jnp.where(lane8 >= 112, south, fill))
                    value = jnp.where(lane8 < 64, layers[z], value)
                    if k0 is None:
                        value = jnp.where(row8 < 4, fill, value)
                    target[z, 8 * p : 8 * p + 8, :] = value

    def send_u1():
        sx, sy, rx, ry, rc = (ref[f"v1_{kind}"] for kind in ("sx", "sy", "rx", "ry", "rc"))
        low = jnp.zeros((8, 128), F32)
        high = jnp.zeros((8, 128), F32)
        for z in range(NZ):
            u = ref["u1"][z, 0:8, 0:128]
            if z % 2 == 0:
                before = u
            else:
                sx[0, z // 2] = jnp.where(row8 < 4, before, rot(u, 4, 0))
                sx[1, z // 2] = jnp.where(row8 < 4, rot(before, 4, 0), u)
            here = between(lane8, 4 * z, 4)
            low = jnp.where(here, rot(u, 4 * z, 1), low)
            high = jnp.where(here, rot(u, 4 * z + 4, 1), high)
        sy[0] = low
        sy[1] = high
        moves = (
            (sx.at[0], rx.at[0], -1, 0),
            (sx.at[1], rx.at[1], 1, 0),
            (sy.at[0], ry.at[0], 0, -1),
            (sy.at[1], ry.at[1], 0, 1),
            (sy.at[0], rc.at[0], -1, -1),
            (sy.at[0], rc.at[1], 1, -1),
            (sy.at[1], rc.at[2], -1, 1),
            (sy.at[1], rc.at[3], 1, 1),
        )
        return [remote(src, dst, B_V1 + i, dx, dy) for i, (src, dst, dx, dy) in enumerate(moves)]

    def receive_u1(copies):
        for copy in copies:
            copy.wait_recv()
        rx, ry, rc = (ref[f"v1_{kind}"] for kind in ("rx", "ry", "rc"))
        lane = iota((16, 128), 1)
        north = jnp.concatenate([ry[0], jnp.where(row8 < 4, rc[0], rc[1])], axis=0)
        south = jnp.concatenate([ry[1], jnp.where(row8 < 4, rc[2], rc[3])], axis=0)
        u = ref["u1"]
        for z in range(NZ):
            east, west = rx[0, z // 2], rx[1, z // 2]
            if z % 2 == 0:
                value = jnp.where(row8 < 4, east, rot(west, 4, 0))
            else:
                value = jnp.where(row8 < 4, rot(east, 4, 0), west)
            u[z, 8:16, 0:128] = value
            value = jnp.where(lane >= 124, rot(south, -4 * (z + 1), 1), 0.0)
            u[z, :, 128:256] = jnp.where(lane < 4, rot(north, -4 * z, 1), value)

    def factor(level):
        diag, down, g, inv = (ref[f"{name}{level}"] for name in ("diag", "D", "g", "inv"))
        before = None
        for z in range(NZ):
            pivot = diag[z]
            if z > 0:
                pivot = pivot - before * down[z - 1]
            inverse = 1.0 / pivot
            inv[z] = inverse
            if z < NZ - 1:
                before = down[z] * inverse
                g[z] = before

    def back_substitute(level, update):
        g, inv, f = (ref[f"{name}{level}"] for name in ("g", "inv", "f"))
        value = f[NZ - 1] * inv[NZ - 1]
        update(NZ - 1, value)
        for z in range(NZ - 2, -1, -1):
            value = f[z] * inv[z] + g[z] * value
            update(z, value)

    def first_sweep(level):
        g, f, rhs, u = (ref[f"{name}{level}"] for name in ("g", "f", "rhs", "u"))
        value = rhs[0]
        f[0] = value
        for z in range(1, NZ):
            value = rhs[z] + g[z - 1] * value
            f[z] = value

        def update(z, solved):
            u[z] = OMEGA * solved

        back_substitute(level, update)

    def lateral(level, z, u):
        east, north = ref[f"E{level}"][z], ref[f"N{level}"][z]
        return (
            east * rot(u, -1, 0) + rot(east * u, 1, 0) + north * rot(u, -1, 1) + rot(north * u, 1, 1)
        )

    def sweep(level, last=None):
        g, f, rhs, u = (ref[f"{name}{level}"] for name in ("g", "f", "rhs", "u"))
        inv = ref[f"inv{level}"]
        rows, lanes = u.shape[1:] if last is None else last.shape[1:]
        at = (slice(0, rows), slice(0, lanes))
        value = None
        for z in range(NZ):
            right = rhs[(z, *at)] + lateral(level, z, u[z])[at]
            value = right if z == 0 else right + g[(z - 1, *at)] * value
            f[(z, *at)] = value
        for z in range(NZ - 1, -1, -1):
            solved = f[(z, *at)] * inv[(z, *at)]
            value = solved if z == NZ - 1 else solved + g[(z, *at)] * value
            old = u[(z, *at)]
            value_new = old + OMEGA * (value - old)
            if last is None:
                u[z] = value_new
            else:
                last[z] = value_new

    def remainder(level, z):
        diag, down, rhs, u = (ref[f"{name}{level}"] for name in ("diag", "D", "rhs", "u"))
        here = u[z]
        value = rhs[z] + lateral(level, z, here) - diag[z] * here
        if z < NZ - 1:
            value = value + down[z] * u[z + 1]
        if z > 0:
            value = value + down[z - 1] * u[z - 1]
        return value

    PIECES = (
        ((0, 256, 256, 256), (256, 128, 64, 128)),
        ((0, 128, 128, 128),),
        ((0, 128, 96, 128),),
        ((0, 128, 128, 32),),
    )
    ROWS = (32, 8, 32, 8)

    def lane_matrix(piece, kind, transpose=False):
        _, count, turn, limit = piece
        shape = (128, count) if transpose else (count, 128)
        fine = iota(shape, 1 if transpose else 0)
        coarse = iota(shape, 0 if transpose else 1)
        hit = (((fine >> 1) + jnp.where(fine >= turn, 64, 0)) == coarse) & (fine < limit)
        if kind != "sum":
            hit = hit & ((fine & 1) == (1 if kind == "odd" else 0))
        return jnp.where(hit, 1.0, 0.0).astype(F32)

    def put_rows(buffer, level, z, value):
        for t in range(YR[level] // 128 if len(PIECES[level]) > 1 else 1):
            buffer[z, t, 0 : ROWS[level], :] = value[0 : ROWS[level], 128 * t : 128 * (t + 1)]

    def row_half(buffer, level, piece, z, odd):
        start, count = piece[0], piece[1]
        parts = []
        for t in range(start // 128, (start + count) // 128):
            rows = [buffer[z, t, pl.ds(i + odd, 8, stride=2), :] for i in range(0, ROWS[level], 16)]
            parts.append(rows[0] if len(rows) == 1 else jnp.concatenate(rows, axis=0))
        return parts[0] if len(parts) == 1 else jnp.concatenate(parts, axis=1)

    def coarse_rows(level):
        return max(8, ROWS[level] // 2)

    def layers_of(value, rows):
        return [value[rows * z : rows * (z + 1)] for z in range(NZ)]

    def keep_own(value, fill):
        return jnp.where((row8 < 4) & (lane8 < 64), value, fill)

    def restrict(level):
        for z in range(NZ):
            put_rows(ref["ta"], level, z, remainder(level, z))
        pieces = []
        for piece in PIECES[level]:
            summed = jnp.concatenate(
                [
                    row_half(ref["ta"], level, piece, z, 0) + row_half(ref["ta"], level, piece, z, 1)
                    for z in range(NZ)
                ],
                axis=0,
            )
            pieces.append(layers_of(exact_dot(summed, lane_matrix(piece, "sum")), coarse_rows(level)))
        return pieces

    def coarsen(level):
        names = ("E", "N", "D", "diag")
        buffers = [ref[name] for name in ("ta", "tb", "tc", "td")]
        for z in range(NZ):
            for name, buffer in zip(names, buffers):
                put_rows(buffer, level, z, ref[f"{name}{level}"][z])
        pieces = []
        for piece in PIECES[level]:
            odd_e, sum_n, sum_d, sum_g = [], [], [], []
            for z in range(NZ):
                (e0, e1), (n0, n1), (d0, d1), (g0, g1) = (
                    [row_half(buffer, level, piece, z, odd) for odd in (0, 1)] for buffer in buffers
                )
                odd_e.append(e1)
                sum_n.append(n0 + n1)
                sum_d.append(d0 + d1)
                sum_g.append(g0 + g1 - 2.0 * e0)
            total = lane_matrix(piece, "sum")
            rows = coarse_rows(level)
            east = exact_dot(jnp.concatenate(odd_e, axis=0), total)
            down = exact_dot(jnp.concatenate(sum_d, axis=0), total)
            north = jnp.concatenate(sum_n, axis=0)
            diagonal = exact_dot(jnp.concatenate(sum_g, axis=0), total) - 2.0 * exact_dot(
                north, lane_matrix(piece, "even")
            )
            north = exact_dot(north, lane_matrix(piece, "odd"))
            pieces.append([layers_of(value, rows) for value in (east, north, down, diagonal)])
        return pieces

    def prolong(level, coarse):
        buffer = ref["ta"]
        u = ref[f"u{level}"]
        pieces = {
            0: ((0, 256, 256, 256), (256, 128, 64, 128)),
            1: ((0, 128, 128, 128), (128, 128, 128, 128)),
            "2c": ((0, 128, 96, 128),),
            3: ((0, 128, 96, 128),),
        }[level]
        for i, piece in enumerate(pieces):
            value = jnp.concatenate([coarse(i, z) for z in range(NZ)], axis=0)
            rows = value.shape[0] // NZ
            fine = exact_dot(value, lane_matrix(piece, "sum", transpose=True))
            start, count = piece[0], piece[1]
            for z in range(NZ):
                for t in range(count // 128):
                    for r in range(0, rows, 8):
                        part = fine[rows * z + r : rows * z + r + 8, 128 * t : 128 * (t + 1)]
                        for odd in (0, 1):
                            buffer[z, start // 128 + t, pl.ds(2 * r + odd, 8, stride=2), :] = part
        for z in range(NZ):
            add = [buffer[z, t, 0 : u.shape[1], :] for t in range(u.shape[2] // 128)]
            u[z] = u[z] + (add[0] if len(add) == 1 else jnp.concatenate(add, axis=1))

    at_sum = (lane8 == 48) & (row8 == 0)

    def pack_tile(stacked):
        stacked = jnp.where(iota((16, 128), 1) < 16, stacked, 0.0)
        return rot(stacked[0:8], 16, 1) + rot(stacked[8:16], 80, 1)

    def stack_layers(values):
        row16 = iota((16, 128), 0)
        stacked = jnp.zeros((16, 128), F32)
        for z in range(NZ):
            stacked = jnp.where(row16 == z, jnp.broadcast_to(values[z][0:1], (16, 128)), stacked)
        return stacked

    def coarsest_coefficients(coarse2):
        east, north, down, diagonal = (
            jnp.concatenate([keep_own(value, 0.0) for value in values], axis=0) for values in coarse2
        )
        layer, row_of = iota((16, 128), 0), iota((16, 128), 1)
        rows = jnp.where((row_of >> 3) == layer, 1.0, 0.0).astype(F32)
        last_row = jnp.where(row_of == 8 * layer + 3, 1.0, 0.0).astype(F32)
        inner = jnp.where((iota((128, 128), 0) & 7) < 3, 2.0, 0.0) * east
        fine, coarse = iota((128, 128), 0), iota((128, 128), 1)
        hit = ((fine >> 2) == coarse) & (fine < 64)
        lanes = jnp.where(hit, 1.0, 0.0).astype(F32)
        last_lane = jnp.where(hit & ((fine & 3) == 3), 1.0, 0.0).astype(F32)
        summed = exact_dot(
            jnp.concatenate(
                [exact_dot(last_row, east), exact_dot(rows, down), exact_dot(rows, diagonal - inner)], axis=0
            ),
            lanes,
        )
        north = exact_dot(rows, north)
        north4 = exact_dot(north, last_lane)
        diagonal4 = summed[32:48] - 2.0 * exact_dot(north, lanes - last_lane)
        return diagonal4, summed[0:16], north4, summed[16:32]

    def total_of(value):
        return jnp.sum(jnp.sum(value, axis=1, keepdims=True), axis=0, keepdims=True)

    def gather_columns(name, tiles, part, base):
        s1, r1 = ref[f"{name}_s1"], ref[f"{name}_r1"]
        for a, tile in enumerate(tiles):
            s1[a] = jnp.where(at_sum, part, tile) if a == 0 else tile
        copies = []
        for d in range(1, GY):
            near = d in (1, GY - 1)
            copies.append(
                remote(s1 if near else s1.at[0], r1.at[d] if near else r1.at[d, 0], base + d - 1, 0, d)
            )
        return copies

    def at_row(gx_of):
        return pl.ds(pl.multiple_of(8 * gx_of, 8), 8)

    def window_of(name, copies):
        for copy in copies:
            copy.wait_recv()
        s1, r1, s2, r2 = (ref[f"{name}_{kind}"] for kind in ("s1", "r1", "s2", "r2"))
        for a in range(s1.shape[0]):
            clean = [s1[a], r1[1, a], r1[GY - 1, a]]
            if a == 0:
                clean = [jnp.where(at_sum, 0.0, tile) for tile in clean]
            window = clean[0] + rot(clean[1], -16, 1) + rot(clean[2], 16, 1)
            if a == 0:
                parts = s1[0]
                for d in range(1, GY):
                    parts = parts + r1[d, 0]
                window = jnp.where(at_sum, parts, window)
            s2[a] = window
            r2[a, at_row(gx), :] = window
        return s2, r2

    def gather_rows(name, copies, base):
        s2, r2 = window_of(name, copies)
        return [remote(s2, r2.at[:, at_row(gx), :], base + d - 1, d, 0) for d in range(1, GX)]

    def gather_along_z(name, copies, base):
        s2, r2 = window_of(name, copies)
        return [remote(s2, r2.at[:, at_row(gx), :], base + d - 1, GXX * d, 0) for d in range(1, GZ)]

    def gather_along_x(name, copies, base):
        for copy in copies:
            copy.wait_recv()
        r2 = ref[f"{name}_r2"]
        x = lax.rem(gx, GXX)
        result = []
        for d in range(1, GXX):
            there = lax.rem(x + d, GXX) - x
            for z in range(GZ):
                rows = r2.at[:, at_row(GXX * z + x), :]
                copy = pltpu.make_async_remote_copy(
                    src_ref=rows, dst_ref=rows, send_sem=ref["send"].at[base + len(result)],
                    recv_sem=ref["recv"].at[base + len(result)],
                    device_id=(gx + there, gy), device_id_type=MESH,
                )
                copy.start()
                started.append(copy)
                result.append(copy)
        return result

    def coarse_layer(buffer, a, z):
        sub, half = z % 8, z // 8
        pieces = [buffer[a, pl.ds(64 * i + sub, 8, stride=8), :] for i in range(4)]
        low = jnp.concatenate(pieces[0:2], axis=0)
        high = jnp.concatenate(pieces[2:4], axis=0)
        lane = iota((16, 128), 1)
        if half == 0:
            return jnp.where(lane < 64, low, rot(high, 64, 1))
        return jnp.where(lane < 64, rot(low, 64, 1), high)

    def coarse_sum(buffer):
        value = jnp.where(at_sum, buffer[0, 0:8, :], 0.0)
        for k in range(1, GX):
            value = value + jnp.where(at_sum, buffer[0, 8 * k : 8 * k + 8, :], 0.0)
        return total_of(value)

    def coarse_at(name, z):
        return ref[name][16 * z : 16 * z + 16, :]

    for copy in loads[0:3]:
        copy.wait()
    use = land_use[...]
    table = jnp.zeros(use.shape, F32)
    fraction = jnp.zeros(use.shape, F32)
    for category in range(CLASSES):
        table = table + jnp.where(use == category, storage_table[category], 0.0)
        fraction = fraction + jnp.where(use == category, return_table[category], 0.0)
    cells, rates, returns = well_cells[...], well_rates[...], return_cells[...]
    wells = rates.shape[1]

    def hits(count, index):
        return iota((count, wells), 0) == index

    def outer(count, index_row, index_column):
        left = jnp.where(hits(count, index_row), rates, 0.0)
        right = jnp.where(hits(256, index_column), 1.0, 0.0).astype(F32)
        return lax.dot_general(
            left, right, (((1,), (1,)), ((), ())),
            precision=lax.Precision.HIGHEST, preferred_element_type=F32,
        )

    storage_sum = jnp.zeros((16, 256), F32)
    for z in range(NZ):
        relief = jnp.exp(ALPHA * jnp.minimum(pressure[z], 0.0))
        ref["P0"][z, 0:16, 0:256] = conductivity[z] * relief
        storage = table * relief
        ref["S0"][z, 0:16, 0:256] = storage
        storage_sum = storage_sum + storage
    pl.semaphore_wait(barrier, len(peers))
    copies_p = send_fine(ref["P0"], 0)
    copies_s = send_fine(ref["S0"], 1)
    loads[3].wait()
    pumped = outer(256, cells >> 8, cells & 255)
    recharge = fraction * outer(16, returns >> 8, returns & 255)
    for z in range(NZ):
        source = residual[z] - pumped[16 * z : 16 * z + 16]
        if z == 0:
            source = source + recharge
        ref["rhs0"][z, 0:16, 0:256] = source
    copies_r = send_fine(ref["rhs0"], 2)
    receive_fine(copies_p, ref["P0"], 0, 0.0)

    flags = [
        jnp.where(inside, 1.0, 0.0).astype(F32)
        for inside in (gx < GX - 1, gx > 0, gy < GY - 1, gy > 0)
    ]
    row = iota((32, 384), 0)
    lane = iota((32, 384), 1)
    inside = jnp.where(row < 16, 1.0, jnp.where(row < 24, flags[0], flags[1]))
    inside = inside * jnp.where(lane < 256, 1.0, jnp.where(lane < 320, flags[2], flags[3]))

    def harmonic(first_value, second_value):
        return 2.0 * first_value * second_value / (first_value + second_value + 1e-30)

    above = None
    for z in range(NZ):
        here = ref["P0"][0] * inside if z == 0 else beneath
        east = harmonic(here, rot(here, -1, 0))
        north = harmonic(here, rot(here, -1, 1))
        diagonal = east + rot(east, 1, 0) + north + rot(north, 1, 1)
        if z > 0:
            diagonal = diagonal + above
        if z < NZ - 1:
            beneath = ref["P0"][z + 1] * inside
            above = VERTICAL * harmonic(here, beneath)
            diagonal = diagonal + above
        else:
            above = jnp.zeros_like(here)
        ref["D0"][z] = above
        ref["E0"][z] = east
        ref["N0"][z] = north
        ref["diag0"][z] = diagonal
    receive_fine(copies_s, ref["S0"], 1, 1.0)
    for z in range(NZ):
        ref["diag0"][z] = ref["diag0"][z] + ref["S0"][z]
    factor(0)

    def place(level, names, pieces):
        for z in range(NZ):
            for k, name in enumerate(names):
                fill = 1.0 if name == "diag" else 0.0
                target = ref[f"{name}{level}"]
                if level == 1:
                    target[z, :, 0:128] = pieces[0][k][z]
                    lane = iota((16, 128), 1)
                    target[z, :, 128:256] = jnp.where((lane < 32) | (lane >= 96), pieces[1][k][z], fill)
                else:
                    lane = iota((16, 128), 1)
                    target[z] = jnp.where((lane < 48) | (lane >= 112), pieces[0][k][z], fill)

    names = ("E", "N", "D", "diag")
    fills = (0.0, 0.0, 0.0, 1.0)
    place(1, names, coarsen(0))
    (coarse2,) = coarsen(1)
    own2 = [[keep_own(coarse2[k][z], fills[k]) for z in range(NZ)] for k in range(4)]
    copies_c2 = send_wide("c2", B_C2, lambda k, z: own2[k][z])
    tiles = [pack_tile(value) for value in coarsest_coefficients(coarse2)]
    stage = gather_columns("gc", tiles, total_of(storage_sum), B_GC1)

    receive_fine(copies_r, ref["rhs0"], 2, 0.0)
    first_sweep(0)
    sweep(0)
    place(1, ("rhs",), [[piece] for piece in restrict(0)])
    factor(1)
    first_sweep(1)
    sweep(1)
    (values,) = restrict(1)
    copies_x2 = send_wide("x2", B_X2, lambda k, z: values[z])
    copies_v1 = send_u1()

    stage = gather_along_z("gc", stage, B_GCZ)

    receive_wide("c2", copies_c2, [ref[f"{name}2"] for name in names], fills)
    place(3, names, coarsen(2))
    factor(2)
    factor(3)
    receive_wide("x2", copies_x2, [ref["rhs2"]], (0.0,))
    stage_c = gather_along_x("gc", stage, B_GCX)
    first_sweep(2)
    sweep(2)
    place(3, ("rhs",), [[piece] for piece in restrict(2)])
    first_sweep(3)
    sweep(3)
    (values,) = restrict(3)
    tile = pack_tile(stack_layers(values))
    stage = gather_columns("gr", [tile], total_of(tile), B_GR1)
    receive_u1(copies_v1)
    for name in ("E", "N", "g", "inv", "rhs", "u"):
        for z in range(NZ):
            ref[f"{name}2c"][z, 0:8, :] = ref[f"{name}2"][z, 0:8, :]
            ref[f"{name}2c"][z, 8:16, :] = ref[f"{name}2"][z, 24:32, :]
    stage_r = gather_rows("gr", stage, B_GR2)

    for copy in stage_c:
        copy.wait_recv()
    lane = iota((16, 128), 1)
    row = iota((16, 128), 0)
    gap = (lane & 63) >= 48
    before = None
    for z in range(NZ):
        pivot = jnp.where(gap, 1.0, coarse_layer(ref["gc_r2"], 0, z))
        if z > 0:
            pivot = pivot - before * below
        inverse = 1.0 / pivot
        below = coarse_layer(ref["gc_r2"], 3, z)
        before = below * inverse
        at = slice(16 * z, 16 * z + 16)
        ref["inv4"][at, :] = inverse
        ref["g4"][at, :] = before
        ref["E4"][at, :] = coarse_layer(ref["gc_r2"], 1, z)
        ref["N4"][at, :] = coarse_layer(ref["gc_r2"], 2, z)
    storage_total = coarse_sum(ref["gc_r2"])
    for copy in stage_r:
        copy.wait_recv()
    shift = coarse_sum(ref["gr_r2"]) / storage_total
    for z in range(NZ):
        at = slice(16 * z, 16 * z + 16)
        ref["rhs4"][at, :] = coarse_layer(ref["gr_r2"], 0, z)
        ref["u4"][at, :] = jnp.broadcast_to(shift, (16, 128))

    def coarse_sweep(step, carry):
        value = None
        for z in range(NZ):
            u, east, north = coarse_at("u4", z), coarse_at("E4", z), coarse_at("N4", z)
            from_e = rot(u, -1, 0)
            from_e = jnp.where(row == 15, rot(from_e, 64, 1), from_e)
            from_w = rot(east * u, 1, 0)
            from_w = jnp.where(row == 0, rot(from_w, 64, 1), from_w)
            right = coarse_at("rhs4", z) + east * from_e + from_w + north * rot(u, -1, 1) + rot(north * u, 1, 1)
            value = right if z == 0 else right + coarse_at("g4", z - 1) * value
            ref["f4"][16 * z : 16 * z + 16, :] = value
        for z in range(NZ - 1, -1, -1):
            solved = coarse_at("f4", z) * coarse_at("inv4", z)
            value = solved if z == NZ - 1 else solved + coarse_at("g4", z) * value
            old = coarse_at("u4", z)
            ref["u4"][16 * z : 16 * z + 16, :] = old + OMEGA * (value - old)
        return carry

    lax.fori_loop(0, COARSE_SWEEPS, coarse_sweep, 0)

    turn = lax.rem(GX - gx, GX)

    def coarsest(_, z):
        value = coarse_at("u4", z)
        value = pltpu.roll(jnp.concatenate([value, rot(value, 64, 1)], axis=0), turn, 0)
        both = rot(jnp.where(row8 < 4, value[0:8], value[24:32]), -16, 1)
        return jnp.where((lane8 < 24) | (lane8 >= 112), both, 0.0)

    def from3(_, z):
        return jnp.where(row8 < 4, ref["u3"][z, 0:8, :], ref["u3"][z, 8:16, :])

    def from2(i, z):
        value = jnp.where(row8 < 6, ref["u2c"][z, 0:8, :], ref["u2c"][z, 8:16, :])
        return value if i == 0 else rot(value, 64, 1)

    prolong(3, coarsest)
    sweep(3)
    sweep(3)
    prolong("2c", from3)
    sweep("2c")
    sweep("2c")
    prolong(1, from2)
    sweep(1)
    sweep(1)
    prolong(0, lambda i, z: ref["u1"][z, :, 128 * i : 128 * (i + 1)])
    sweep(0)
    sweep(0, last=out)
    for copy in started:
        copy.wait_send()


def shards(
    newton_residual, pressure_head, conductivity, land_use, storage_table, return_table,
    well_cells, well_rates, return_cells,
):
    vmem = pl.BlockSpec(memory_space=pltpu.VMEM)
    hbm = pl.BlockSpec(memory_space=pltpu.HBM)
    smem = pl.BlockSpec(memory_space=pltpu.SMEM)
    wells = well_cells.shape[-1]
    return pl.pallas_call(
        kernel,
        out_shape=jax.ShapeDtypeStruct(newton_residual.shape, F32),
        in_specs=[hbm] * 4 + [smem] * 2 + [vmem] * 3,
        out_specs=vmem,
        scratch_shapes=list(PLAN.values()),
        compiler_params=pltpu.CompilerParams(
            collective_id=0, has_side_effects=True, vmem_limit_bytes=36 * 1024 * 1024
        ),
    )(
        newton_residual, pressure_head, conductivity, land_use, storage_table, return_table,
        well_cells.reshape(1, wells), well_rates.reshape(1, wells), return_cells.reshape(1, wells),
    )


def solution(mesh):
    return jax.shard_map(
        shards,
        mesh=mesh,
        in_specs=(
            P(None, "gx", "gy"),
            P(None, "gx", "gy"),
            P(None, "gx", "gy"),
            P("gx", "gy"),
            P(),
            P(),
            P("gx", "gy", None),
            P("gx", "gy", None),
            P("gx", "gy", None),
        ),
        out_specs=P(None, "gx", "gy"),
        check_vma=False,
    )
```

```python
import functools

import jax
import jax.numpy as jnp
from jax import lax
from jax.experimental import pallas as pl
from jax.experimental.pallas import tpu as pltpu
from jax.sharding import PartitionSpec as P

NZ = 16
CLASSES = 8
COARSE_SWEEPS = 12
OMEGA = 0.8
VERTICAL = 4.0
ALPHA = 0.5
F32 = jnp.float32
MESH = pl.DeviceIdType.MESH

NX = (16, 8, 4, 2)
NY = (256, 128, 64, 32)
XR = (32, 16, 32, 16)
YR = (384, 256, 128, 128)
REACH = 3
SIDES = [d for d in range(-REACH, REACH + 1) if d != 0]
GY, GX = 8, 32
N_E0 = 24
N_WIDE = 6 * REACH + 2
N_V1 = 8
B_E0 = 0
B_C2 = B_E0 + N_E0
B_X2 = B_C2 + N_WIDE
B_V1 = B_X2 + N_WIDE
N_HALO = B_V1 + N_V1
GZ, GXX = 8, 4
B_GC1 = N_HALO
B_GCZ = B_GC1 + GY - 1
B_GCX = B_GCZ + GZ - 1
B_GR1 = B_GCX + GZ * (GXX - 1)
B_GR2 = B_GR1 + GY - 1
N_SEM = B_GR2 + GX - 1
LEVEL_ARRAYS = ("E", "N", "D", "diag", "g", "inv", "rhs", "u", "f")


def rot(value, shift, axis):
    shift %= value.shape[axis]
    return value if shift == 0 else pltpu.roll(value, shift, axis)


def iota(shape, axis):
    return lax.broadcasted_iota(jnp.int32, shape, axis)


def between(index, start, count):
    return (index >= start) & (index < start + count)


def exact_dot(left, right):
    return jnp.dot(left, right, precision=lax.Precision.HIGHEST, preferred_element_type=F32)


def scratch_plan():
    plan = {}
    for level in range(4):
        for name in LEVEL_ARRAYS:
            plan[f"{name}{level}"] = pltpu.VMEM((NZ, XR[level], YR[level]), F32)
    for name in ("E", "N", "g", "inv", "rhs", "u", "f"):
        plan[f"{name}2c"] = pltpu.VMEM((NZ, 16, 128), F32)
    plan["P0"] = pltpu.VMEM((NZ, XR[0], YR[0]), F32)
    plan["S0"] = pltpu.VMEM((NZ, XR[0], YR[0]), F32)
    for name in ("E4", "N4", "g4", "inv4", "rhs4", "u4", "f4"):
        plan[name] = pltpu.VMEM((NZ * 16, 128), F32)
    for name in ("ta", "tb", "tc", "td"):
        plan[name] = pltpu.VMEM((NZ, 3, 32, 128), F32)
    plan["e0_sy"] = pltpu.VMEM((2, 3, 16, 128), F32)
    plan["e0_ry"] = pltpu.VMEM((2, 3, 16, 128), F32)
    plan["e0_rc"] = pltpu.VMEM((4, 3, 8, 128), F32)
    for kind in ("s", "r"):
        plan[f"e0_{kind}a"] = pltpu.VMEM((2, NZ, 8, 256), F32)
        plan[f"e0_{kind}b"] = pltpu.VMEM((2, NZ // 2, 8, 256), F32)
    for name, count in (("c2", 4), ("x2", 1)):
        plan[f"{name}_sx"] = pltpu.VMEM((count, 4, 8, 128), F32)
        plan[f"{name}_rx"] = pltpu.VMEM((2 * REACH + 1, count, 4, 8, 128), F32)
        plan[f"{name}_sy"] = pltpu.VMEM((2, count, 8, 128), F32)
        plan[f"{name}_ry"] = pltpu.VMEM((2, 2 * REACH + 1, count, 8, 128), F32)
    for kind in ("s", "r"):
        plan[f"v1_{kind}x"] = pltpu.VMEM((2, 8, 8, 128), F32)
        plan[f"v1_{kind}y"] = pltpu.VMEM((2, 8, 128), F32)
    plan["v1_rc"] = pltpu.VMEM((4, 8, 128), F32)
    for name in ("residual", "pressure", "conductivity"):
        plan[name] = pltpu.VMEM((NZ, NX[0], NY[0]), F32)
    plan["land_use"] = pltpu.VMEM((NX[0], NY[0]), jnp.int32)
    plan["relay"] = pltpu.SemaphoreType.REGULAR((4,))
    plan["load"] = pltpu.SemaphoreType.DMA((4,))
    for name, count in (("gc", 4), ("gr", 1)):
        plan[f"{name}_s1"] = pltpu.VMEM((count, 8, 128), F32)
        plan[f"{name}_r1"] = pltpu.VMEM((GY, count, 8, 128), F32)
        plan[f"{name}_s2"] = pltpu.VMEM((count, 8, 128), F32)
        plan[f"{name}_r2"] = pltpu.VMEM((count, GX * 8, 128), F32)
    plan["send"] = pltpu.SemaphoreType.DMA((N_SEM,))
    plan["recv"] = pltpu.SemaphoreType.DMA((N_SEM,))
    return plan


PLAN = scratch_plan()


def kernel(
    residual_in, pressure_in, conductivity_in, land_use_in, storage_table, return_table,
    well_cells, well_rates, return_cells, out, *scratch,
):
    ref = dict(zip(PLAN, scratch))
    gx = lax.axis_index("gx")
    gy = lax.axis_index("gy")

    def device(dx, dy):
        return (lax.rem(gx + (dx + GX), GX), lax.rem(gy + (dy + GY), GY))

    peers = [(dx, dy) for dx in (-1, 0, 1) for dy in (-1, 0, 1) if (dx, dy) != (0, 0)]
    relays = (peers, [(2 * dx, 2 * dy) for dx, dy in peers], [(-4, 0), (4, 0)], [(-8, 0), (8, 0)])

    def relay(stage):
        for dx, dy in relays[stage]:
            pl.semaphore_signal(
                ref["relay"].at[stage], inc=1, device_id=device(dx, dy), device_id_type=MESH
            )

    def await_relay(stage):
        pl.semaphore_wait(ref["relay"].at[stage], len(relays[stage]))

    barrier = pltpu.get_barrier_semaphore()
    for dx, dy in peers:
        pl.semaphore_signal(barrier, inc=1, device_id=device(dx, dy), device_id_type=MESH)

    loads = []
    for i, (name, source) in enumerate(
        (("land_use", land_use_in), ("pressure", pressure_in), ("conductivity", conductivity_in), ("residual", residual_in))
    ):
        loads.append(pltpu.make_async_copy(source, ref[name], ref["load"].at[i]))
        loads[-1].start()
    residual, pressure, conductivity, land_use = (
        ref[name] for name in ("residual", "pressure", "conductivity", "land_use")
    )
    started = []

    def remote(src, dst, index, dx, dy):
        copy = pltpu.make_async_remote_copy(
            src_ref=src, dst_ref=dst, send_sem=ref["send"].at[index], recv_sem=ref["recv"].at[index],
            device_id=device(dx, dy), device_id_type=MESH,
        )
        copy.start()
        started.append(copy)
        return copy

    row8 = iota((8, 128), 0)
    lane8 = iota((8, 128), 1)

    def send_permeable(array):
        copies = []
        for side, (own, there, dx) in enumerate(((0, 16, -1), (8, 24, 1))):
            copies.append(
                remote(
                    array.at[:, pl.ds(own, 8), pl.ds(0, 256)],
                    array.at[:, pl.ds(there, 8), pl.ds(0, 256)],
                    B_E0 + side, dx, 0,
                )
            )
        return copies

    row_wide = iota((8, 256), 0)

    def pack_rows(storage, source):
        sa, sb = ref["e0_sa"], ref["e0_sb"]
        for z in range(NZ):
            for side in (0, 1):
                at = slice(8 * side, 8 * side + 8)
                kept, moved = storage[z, at, 0:256], source[z, at, 0:256]
                if side == 0:
                    sa[side, z] = jnp.where(row_wide < 6, kept, rot(moved, 6, 0))
                else:
                    sa[side, z] = jnp.where(row_wide >= 2, kept, rot(moved, 2, 0))
                if z % 2 == 1:
                    first = source[z - 1, at, 0:256]
                    sb[side, z // 2] = jnp.where(row_wide < 4, rot(first, -2, 0), rot(moved, 2, 0))

    def send_rows():
        sa, sb, ra, rb = (ref[f"e0_{kind}"] for kind in ("sa", "sb", "ra", "rb"))
        copies = []
        for side, dx in ((0, -1), (1, 1)):
            copies.append(remote(sa.at[side], ra.at[side], B_E0 + 20 + side, dx, 0))
            copies.append(remote(sb.at[side], rb.at[side], B_E0 + 22 + side, dx, 0))
        return copies

    def receive_rows(copies, storage, source):
        for copy in copies:
            copy.wait_recv()
        ra, rb = ref["e0_ra"], ref["e0_rb"]
        middle = (row_wide >= 2) & (row_wide < 6)
        for z in range(NZ):
            shift = 2 if z % 2 == 0 else -2
            for side in (0, 1):
                at = slice(16 + 8 * side, 24 + 8 * side)
                tile, rest = ra[side, z], rot(rb[side, z // 2], shift, 0)
                if side == 0:
                    storage[z, at, 0:256] = jnp.where(row_wide < 6, tile, 1.0)
                    near = jnp.where(row_wide < 2, rot(tile, -6, 0), 0.0)
                else:
                    storage[z, at, 0:256] = jnp.where(row_wide >= 2, tile, 1.0)
                    near = jnp.where(row_wide >= 6, rot(tile, -2, 0), 0.0)
                source[z, at, 0:256] = jnp.where(middle, rest, near)

    def pack_columns(array, k):
        sy = ref["e0_sy"]
        lane = iota((16, 128), 1)
        low = jnp.zeros((16, 128), F32)
        high = jnp.zeros((16, 128), F32)
        for z in range(NZ):
            here = between(lane, 8 * z, 8)
            low = jnp.where(here, rot(array[z, 0:16, 0:128], 8 * z, 1), low)
            high = jnp.where(here, rot(array[z, 0:16, 128:256], 8 * z + 8, 1), high)
        sy[0, k] = low
        sy[1, k] = high

    def send_columns(k):
        sy, ry, rc = ref["e0_sy"], ref["e0_ry"], ref["e0_rc"]
        base = B_E0 + 2 + 6 * k
        copies = []
        first, last = pl.ds(0, 8), pl.ds(8, 8)
        moves = (
            (sy.at[0, k], ry.at[0, k], 0, -1),
            (sy.at[1, k], ry.at[1, k], 0, 1),
            (sy.at[0, k, first], rc.at[0, k], -1, -1),
            (sy.at[0, k, last], rc.at[1, k], 1, -1),
            (sy.at[1, k, first], rc.at[2, k], -1, 1),
            (sy.at[1, k, last], rc.at[3, k], 1, 1),
        )
        for i, (src, dst, dx, dy) in enumerate(moves):
            copies.append(remote(src, dst, base + i, dx, dy))
        return copies

    def receive_columns(copies, array, k, fill):
        for copy in copies:
            copy.wait_recv()
        ry, rc = ref["e0_ry"], ref["e0_rc"]
        lane = iota((32, 128), 1)
        north = jnp.concatenate([ry[0, k], rc[0, k], rc[1, k]], axis=0)
        south = jnp.concatenate([ry[1, k], rc[2, k], rc[3, k]], axis=0)
        for z in range(NZ):
            value = jnp.where(lane >= 120, rot(south, -8 * (z + 1), 1), fill)
            array[z, :, 256:384] = jnp.where(lane < 8, rot(north, -8 * z, 1), value)

    def pack_wide(name, get):
        sx, sy, rx = (ref[f"{name}_{kind}"] for kind in ("sx", "sy", "rx"))
        for a in range(sx.shape[0]):
            values = [get(a, z) for z in range(NZ)]
            for t in range(4):
                left = jnp.where(row8 < 4, values[t], rot(values[t + 4], 4, 0))
                right = jnp.where(row8 < 4, values[t + 8], rot(values[t + 12], 4, 0))
                tile = jnp.where(lane8 < 64, left, rot(right, 64, 1))
                sx[a, t] = tile
                rx[REACH, a, t] = tile
            low = jnp.zeros((8, 128), F32)
            high = jnp.zeros((8, 128), F32)
            for q in range(8):
                both = jnp.where(row8 < 4, values[q], rot(values[q + 8], 4, 0))
                here = between(lane8, 16 * q, 16)
                low = jnp.where(here, rot(both, 16 * q, 1), low)
                high = jnp.where(here, rot(both, 16 * q - 48, 1), high)
            sy[0, a] = low
            sy[1, a] = high

    def send_wide(name, base):
        return send_wide_to(name, base, [d for d in SIDES if abs(d) < REACH])

    def send_wide_to(name, base, sides):
        sx, sy, rx, ry = (ref[f"{name}_{kind}"] for kind in ("sx", "sy", "rx", "ry"))
        far = REACH in sides
        copies = []
        for d in sides:
            copies.append(remote(sx, rx.at[REACH - d], base + SIDES.index(d), d, 0))
        for side, dy in ((0, -1), (1, 1)):
            for d in sides if far else sides + [0]:
                index = 2 * REACH + side * (2 * REACH + 1) + d + REACH
                copies.append(remote(sy.at[side], ry.at[side, REACH - d], base + index, d, dy))
        return copies

    def receive_wide(name, copies, targets, fills, far):
        for copy in copies:
            copy.wait_recv()
        rx, ry = ref[f"{name}_rx"], ref[f"{name}_ry"]
        empty = jnp.zeros((8, 128), F32)

        def join(first, second):
            return (
                jnp.where(row8 < 4, first, rot(second, 4, 0)),
                jnp.where(row8 < 4, rot(first, 4, 0), second),
            )

        for a, (target, fill) in enumerate(zip(targets, fills)):
            tiles = {0: (0, 1), 1: (2, None), 2: (None, None), 3: (-2, -1)}
            if far:
                tiles = {1: (2, 3), 2: (None, -3)}
            for p, (k0, k1) in tiles.items():
                if k0 is None and k1 is None:
                    for z in range(NZ):
                        target[z, 8 * p : 8 * p + 8, :] = jnp.full((8, 128), fill, F32)
                    continue
                layers = [None] * NZ
                for t in range(4):
                    first = empty if k0 is None else rx[REACH + k0, a, t]
                    second = empty if k1 is None else rx[REACH + k1, a, t]
                    for i, both in enumerate(join(first, second)):
                        layers[t + 4 * i] = both
                        layers[t + 4 * i + 8] = rot(both, 64, 1)
                sides = []
                for side in (0, 1):
                    first = empty if k0 is None else ry[side, REACH + k0, a]
                    second = empty if k1 is None else ry[side, REACH + k1, a]
                    sides.append(join(first, second))
                for z in range(NZ):
                    q = z % 8
                    north = rot(sides[0][z // 8], 64 - 16 * q, 1)
                    south = rot(sides[1][z // 8], 112 - 16 * q, 1)
                    value = jnp.where(lane8 < 80, north, jnp.where(lane8 >= 112, south, fill))
                    value = jnp.where(lane8 < 64, layers[z], value)
                    if k0 is None:
                        value = jnp.where(row8 < 4, fill, value)
                    if k1 is None:
                        value = jnp.where(row8 < 4, value, fill)
                    target[z, 8 * p : 8 * p + 8, :] = value

    def send_u1():
        sx, sy, rx, ry, rc = (ref[f"v1_{kind}"] for kind in ("sx", "sy", "rx", "ry", "rc"))
        low = jnp.zeros((8, 128), F32)
        high = jnp.zeros((8, 128), F32)
        for z in range(NZ):
            u = ref["u1"][z, 0:8, 0:128]
            if z % 2 == 0:
                before = u
            else:
                sx[0, z // 2] = jnp.where(row8 < 4, before, rot(u, 4, 0))
                sx[1, z // 2] = jnp.where(row8 < 4, rot(before, 4, 0), u)
            here = between(lane8, 4 * z, 4)
            low = jnp.where(here, rot(u, 4 * z, 1), low)
            high = jnp.where(here, rot(u, 4 * z + 4, 1), high)
        sy[0] = low
        sy[1] = high
        moves = (
            (sx.at[0], rx.at[0], -1, 0),
            (sx.at[1], rx.at[1], 1, 0),
            (sy.at[0], ry.at[0], 0, -1),
            (sy.at[1], ry.at[1], 0, 1),
            (sy.at[0], rc.at[0], -1, -1),
            (sy.at[0], rc.at[1], 1, -1),
            (sy.at[1], rc.at[2], -1, 1),
            (sy.at[1], rc.at[3], 1, 1),
        )
        return [remote(src, dst, B_V1 + i, dx, dy) for i, (src, dst, dx, dy) in enumerate(moves)]

    def receive_u1(copies):
        for copy in copies:
            copy.wait_recv()
        rx, ry, rc = (ref[f"v1_{kind}"] for kind in ("rx", "ry", "rc"))
        lane = iota((16, 128), 1)
        north = jnp.concatenate([ry[0], jnp.where(row8 < 4, rc[0], rc[1])], axis=0)
        south = jnp.concatenate([ry[1], jnp.where(row8 < 4, rc[2], rc[3])], axis=0)
        u = ref["u1"]
        for z in range(NZ):
            east, west = rx[0, z // 2], rx[1, z // 2]
            if z % 2 == 0:
                value = jnp.where(row8 < 4, east, rot(west, 4, 0))
            else:
                value = jnp.where(row8 < 4, rot(east, 4, 0), west)
            u[z, 8:16, 0:128] = value
            value = jnp.where(lane >= 124, rot(south, -4 * (z + 1), 1), 0.0)
            u[z, :, 128:256] = jnp.where(lane < 4, rot(north, -4 * z, 1), value)

    def factor(level):
        diag, down, g, inv = (ref[f"{name}{level}"] for name in ("diag", "D", "g", "inv"))
        before = None
        for z in range(NZ):
            pivot = diag[z]
            if z > 0:
                pivot = pivot - before * down[z - 1]
            inverse = 1.0 / pivot
            inv[z] = inverse
            if z < NZ - 1:
                before = down[z] * inverse
                g[z] = before

    def back_substitute(level, update):
        g, inv, f = (ref[f"{name}{level}"] for name in ("g", "inv", "f"))
        value = f[NZ - 1] * inv[NZ - 1]
        update(NZ - 1, value)
        for z in range(NZ - 2, -1, -1):
            value = f[z] * inv[z] + g[z] * value
            update(z, value)

    def first_sweep(level):
        g, f, rhs, u = (ref[f"{name}{level}"] for name in ("g", "f", "rhs", "u"))
        value = rhs[0]
        f[0] = value
        for z in range(1, NZ):
            value = rhs[z] + g[z - 1] * value
            f[z] = value

        def update(z, solved):
            u[z] = OMEGA * solved

        back_substitute(level, update)

    def lateral(level, z, u):
        east, north = ref[f"E{level}"][z], ref[f"N{level}"][z]
        return (
            east * rot(u, -1, 0) + rot(east * u, 1, 0) + north * rot(u, -1, 1) + rot(north * u, 1, 1)
        )

    def sweep(level, last=None):
        g, f, rhs, u = (ref[f"{name}{level}"] for name in ("g", "f", "rhs", "u"))
        inv = ref[f"inv{level}"]
        rows, lanes = u.shape[1:] if last is None else last.shape[1:]
        at = (slice(0, rows), slice(0, lanes))
        value = None
        for z in range(NZ):
            right = rhs[(z, *at)] + lateral(level, z, u[z])[at]
            value = right if z == 0 else right + g[(z - 1, *at)] * value
            f[(z, *at)] = value
        for z in range(NZ - 1, -1, -1):
            solved = f[(z, *at)] * inv[(z, *at)]
            value = solved if z == NZ - 1 else solved + g[(z, *at)] * value
            old = u[(z, *at)]
            value_new = old + OMEGA * (value - old)
            if last is None:
                u[z] = value_new
            else:
                last[z] = value_new

    def remainder(level, z):
        diag, down, rhs, u = (ref[f"{name}{level}"] for name in ("diag", "D", "rhs", "u"))
        here = u[z]
        value = rhs[z] + lateral(level, z, here) - diag[z] * here
        if z < NZ - 1:
            value = value + down[z] * u[z + 1]
        if z > 0:
            value = value + down[z - 1] * u[z - 1]
        return value

    PIECES = (
        ((0, 256, 256, 256), (256, 128, 64, 128)),
        ((0, 128, 128, 128),),
        ((0, 128, 96, 128),),
        ((0, 128, 128, 32),),
    )
    ROWS = (32, 8, 32, 8)

    def lane_matrix(piece, kind, transpose=False):
        _, count, turn, limit = piece
        shape = (128, count) if transpose else (count, 128)
        fine = iota(shape, 1 if transpose else 0)
        coarse = iota(shape, 0 if transpose else 1)
        hit = (((fine >> 1) + jnp.where(fine >= turn, 64, 0)) == coarse) & (fine < limit)
        if kind != "sum":
            hit = hit & ((fine & 1) == (1 if kind == "odd" else 0))
        return jnp.where(hit, 1.0, 0.0).astype(F32)

    def put_rows(buffer, rows, z, value):
        for t in range(value.shape[1] // 128):
            buffer[z, t, 0:rows, :] = value[0:rows, 128 * t : 128 * (t + 1)]

    def row_half(buffer, count_rows, piece, z, odd):
        start, count = piece[0], piece[1]
        parts = []
        for t in range(start // 128, (start + count) // 128):
            rows = [buffer[z, t, pl.ds(i + odd, 8, stride=2), :] for i in range(0, count_rows, 16)]
            parts.append(rows[0] if len(rows) == 1 else jnp.concatenate(rows, axis=0))
        return parts[0] if len(parts) == 1 else jnp.concatenate(parts, axis=1)

    def coarse_rows(rows):
        return max(8, rows // 2)

    def lanes_of(level):
        return sum(piece[1] for piece in PIECES[level])

    def layers_of(value, rows):
        return [value[rows * z : rows * (z + 1)] for z in range(NZ)]

    def keep_own(value, fill):
        return jnp.where((row8 < 4) & (lane8 < 64), value, fill)

    def restrict(level):
        for z in range(NZ):
            put_rows(ref["ta"], ROWS[level], z, remainder(level, z)[:, 0 : lanes_of(level)])
        pieces = []
        for piece in PIECES[level]:
            summed = jnp.concatenate(
                [
                    row_half(ref["ta"], ROWS[level], piece, z, 0) + row_half(ref["ta"], ROWS[level], piece, z, 1)
                    for z in range(NZ)
                ],
                axis=0,
            )
            pieces.append(layers_of(exact_dot(summed, lane_matrix(piece, "sum")), coarse_rows(ROWS[level])))
        return pieces

    def coarsen(level, own=False):
        rows_fine = 16 if own else ROWS[level]
        lanes = 256 if own else lanes_of(level)
        names = ("E", "N", "D", "diag")
        buffers = [ref[name] for name in ("ta", "tb", "tc", "td")]
        for z in range(NZ):
            for name, buffer in zip(names, buffers):
                value = ref[f"{name}{level}"][z, 0:rows_fine, 0:lanes]
                if own and name == "diag":
                    value = value + ref["S0"][z, 0:rows_fine, 0:lanes]
                put_rows(buffer, rows_fine, z, value)
        pieces = []
        for piece in PIECES[level][0:1] if own else PIECES[level]:
            odd_e, sum_n, sum_d, sum_g = [], [], [], []
            for z in range(NZ):
                (e0, e1), (n0, n1), (d0, d1), (g0, g1) = (
                    [row_half(buffer, rows_fine, piece, z, odd) for odd in (0, 1)] for buffer in buffers
                )
                odd_e.append(e1)
                sum_n.append(n0 + n1)
                sum_d.append(d0 + d1)
                sum_g.append(g0 + g1 - 2.0 * e0)
            total = lane_matrix(piece, "sum")
            rows = coarse_rows(rows_fine)
            east = exact_dot(jnp.concatenate(odd_e, axis=0), total)
            down = exact_dot(jnp.concatenate(sum_d, axis=0), total)
            north = jnp.concatenate(sum_n, axis=0)
            diagonal = exact_dot(jnp.concatenate(sum_g, axis=0), total) - 2.0 * exact_dot(
                north, lane_matrix(piece, "even")
            )
            north = exact_dot(north, lane_matrix(piece, "odd"))
            pieces.append([layers_of(value, rows) for value in (east, north, down, diagonal)])
        return pieces

    def prolong(level, coarse):
        buffer = ref["ta"]
        u = ref[f"u{level}"]
        pieces = {
            0: ((0, 256, 256, 256), (256, 128, 64, 128)),
            1: ((0, 128, 128, 128), (128, 128, 128, 128)),
            "2c": ((0, 128, 96, 128),),
            3: ((0, 128, 96, 128),),
        }[level]
        for i, piece in enumerate(pieces):
            value = jnp.concatenate([coarse(i, z) for z in range(NZ)], axis=0)
            rows = value.shape[0] // NZ
            fine = exact_dot(value, lane_matrix(piece, "sum", transpose=True))
            start, count = piece[0], piece[1]
            for z in range(NZ):
                for t in range(count // 128):
                    for r in range(0, rows, 8):
                        part = fine[rows * z + r : rows * z + r + 8, 128 * t : 128 * (t + 1)]
                        for odd in (0, 1):
                            buffer[z, start // 128 + t, pl.ds(2 * r + odd, 8, stride=2), :] = part
        for z in range(NZ):
            add = [buffer[z, t, 0 : u.shape[1], :] for t in range(u.shape[2] // 128)]
            u[z] = u[z] + (add[0] if len(add) == 1 else jnp.concatenate(add, axis=1))

    at_sum = (lane8 == 48) & (row8 == 0)

    def pack_tile(stacked):
        stacked = jnp.where(iota((16, 128), 1) < 16, stacked, 0.0)
        return rot(stacked[0:8], 16, 1) + rot(stacked[8:16], 80, 1)

    def stack_layers(values):
        row16 = iota((16, 128), 0)
        stacked = jnp.zeros((16, 128), F32)
        for z in range(NZ):
            stacked = jnp.where(row16 == z, jnp.broadcast_to(values[z][0:1], (16, 128)), stacked)
        return stacked

    def coarsest_coefficients(coarse2):
        east, north, down, diagonal = (
            jnp.concatenate([keep_own(value, 0.0) for value in values], axis=0) for values in coarse2
        )
        layer, row_of = iota((16, 128), 0), iota((16, 128), 1)
        rows = jnp.where((row_of >> 3) == layer, 1.0, 0.0).astype(F32)
        last_row = jnp.where(row_of == 8 * layer + 3, 1.0, 0.0).astype(F32)
        inner = jnp.where((iota((128, 128), 0) & 7) < 3, 2.0, 0.0) * east
        fine, coarse = iota((128, 128), 0), iota((128, 128), 1)
        hit = ((fine >> 2) == coarse) & (fine < 64)
        lanes = jnp.where(hit, 1.0, 0.0).astype(F32)
        last_lane = jnp.where(hit & ((fine & 3) == 3), 1.0, 0.0).astype(F32)
        summed = exact_dot(
            jnp.concatenate(
                [exact_dot(last_row, east), exact_dot(rows, down), exact_dot(rows, diagonal - inner)], axis=0
            ),
            lanes,
        )
        north = exact_dot(rows, north)
        north4 = exact_dot(north, last_lane)
        diagonal4 = summed[32:48] - 2.0 * exact_dot(north, lanes - last_lane)
        return diagonal4, summed[0:16], north4, summed[16:32]

    def total_of(value):
        return jnp.sum(jnp.sum(value, axis=1, keepdims=True), axis=0, keepdims=True)

    def gather_columns(name, tiles, part, base):
        s1, r1 = ref[f"{name}_s1"], ref[f"{name}_r1"]
        for a, tile in enumerate(tiles):
            s1[a] = jnp.where(at_sum, part, tile) if a == 0 else tile
        copies = []
        for d in range(1, GY):
            near = d in (1, GY - 1)
            copies.append(
                remote(s1 if near else s1.at[0], r1.at[d] if near else r1.at[d, 0], base + d - 1, 0, d)
            )
        return copies

    def at_row(gx_of):
        return pl.ds(pl.multiple_of(8 * gx_of, 8), 8)

    def window_of(name, copies):
        for copy in copies:
            copy.wait_recv()
        s1, r1, s2, r2 = (ref[f"{name}_{kind}"] for kind in ("s1", "r1", "s2", "r2"))
        for a in range(s1.shape[0]):
            clean = [s1[a], r1[1, a], r1[GY - 1, a]]
            if a == 0:
                clean = [jnp.where(at_sum, 0.0, tile) for tile in clean]
            window = clean[0] + rot(clean[1], -16, 1) + rot(clean[2], 16, 1)
            if a == 0:
                parts = s1[0]
                for d in range(1, GY):
                    parts = parts + r1[d, 0]
                window = jnp.where(at_sum, parts, window)
            s2[a] = window
            r2[a, at_row(gx), :] = window
        return s2, r2

    def gather_rows(name, copies, base):
        s2, r2 = window_of(name, copies)
        return [remote(s2, r2.at[:, at_row(gx), :], base + d - 1, d, 0) for d in range(1, GX)]

    def gather_along_z(name, copies, base):
        s2, r2 = window_of(name, copies)
        return [remote(s2, r2.at[:, at_row(gx), :], base + d - 1, GXX * d, 0) for d in range(1, GZ)]

    def gather_along_x(name, copies, base):
        for copy in copies:
            copy.wait_recv()
        r2 = ref[f"{name}_r2"]
        x = lax.rem(gx, GXX)
        result = []
        for d in range(1, GXX):
            there = lax.rem(x + d, GXX) - x
            for z in range(GZ):
                rows = r2.at[:, at_row(GXX * z + x), :]
                copy = pltpu.make_async_remote_copy(
                    src_ref=rows, dst_ref=rows, send_sem=ref["send"].at[base + len(result)],
                    recv_sem=ref["recv"].at[base + len(result)],
                    device_id=(gx + there, gy), device_id_type=MESH,
                )
                copy.start()
                started.append(copy)
                result.append(copy)
        return result

    def coarse_layer(buffer, a, z):
        sub, half = z % 8, z // 8
        pieces = [buffer[a, pl.ds(64 * i + sub, 8, stride=8), :] for i in range(4)]
        low = jnp.concatenate(pieces[0:2], axis=0)
        high = jnp.concatenate(pieces[2:4], axis=0)
        lane = iota((16, 128), 1)
        if half == 0:
            return jnp.where(lane < 64, low, rot(high, 64, 1))
        return jnp.where(lane < 64, rot(low, 64, 1), high)

    def coarse_sum(buffer):
        value = jnp.where(at_sum, buffer[0, 0:8, :], 0.0)
        for k in range(1, GX):
            value = value + jnp.where(at_sum, buffer[0, 8 * k : 8 * k + 8, :], 0.0)
        return total_of(value)

    def coarse_at(name, z):
        return ref[name][16 * z : 16 * z + 16, :]

    for copy in loads:
        copy.wait()
    use = land_use[...]
    table = jnp.zeros(use.shape, F32)
    fraction = jnp.zeros(use.shape, F32)
    for category in range(CLASSES):
        table = table + jnp.where(use == category, storage_table[category], 0.0)
        fraction = fraction + jnp.where(use == category, return_table[category], 0.0)
    cells, rates, returns = well_cells[...], well_rates[...], return_cells[...]
    wells = rates.shape[1]

    def hits(count, index):
        return iota((count, wells), 0) == index

    def outer(count, index_row, index_column):
        left = jnp.where(hits(count, index_row), rates, 0.0)
        right = jnp.where(hits(256, index_column), 1.0, 0.0).astype(F32)
        return lax.dot_general(
            left, right, (((1,), (1,)), ((), ())),
            precision=lax.Precision.HIGHEST, preferred_element_type=F32,
        )

    storage_sum = jnp.zeros((16, 256), F32)
    for z in range(NZ):
        relief = jnp.exp(ALPHA * jnp.minimum(pressure[z], 0.0))
        ref["P0"][z, 0:16, 0:256] = conductivity[z] * relief
        storage = table * relief
        ref["S0"][z, 0:16, 0:256] = storage
        storage_sum = storage_sum + storage
    pumped = outer(256, cells >> 8, cells & 255)
    recharge = fraction * outer(16, returns >> 8, returns & 255)
    for z in range(NZ):
        source = residual[z] - pumped[16 * z : 16 * z + 16]
        if z == 0:
            source = source + recharge
        ref["rhs0"][z, 0:16, 0:256] = source
    for k, name in enumerate(("P0", "S0", "rhs0")):
        pack_columns(ref[name], k)
    pack_rows(ref["S0"], ref["rhs0"])
    pl.semaphore_wait(barrier, len(peers))
    copies_p = send_permeable(ref["P0"]) + send_columns(0)
    copies_rows = send_rows()
    copies_s = send_columns(1)
    copies_r = send_columns(2)
    relay(0)
    await_relay(0)
    relay(1)
    receive_columns(copies_p, ref["P0"], 0, 0.0)

    flags = [
        jnp.where(inside, 1.0, 0.0).astype(F32)
        for inside in (gx < GX - 1, gx > 0, gy < GY - 1, gy > 0)
    ]
    row = iota((32, 384), 0)
    lane = iota((32, 384), 1)
    inside = jnp.where(row < 16, 1.0, jnp.where(row < 24, flags[0], flags[1]))
    inside = inside * jnp.where(lane < 256, 1.0, jnp.where(lane < 320, flags[2], flags[3]))

    def harmonic(first_value, second_value):
        return 2.0 * first_value * second_value / (first_value + second_value + 1e-30)

    above = None
    for z in range(NZ):
        here = ref["P0"][0] * inside if z == 0 else beneath
        east = harmonic(here, rot(here, -1, 0))
        north = harmonic(here, rot(here, -1, 1))
        diagonal = east + rot(east, 1, 0) + north + rot(north, 1, 1)
        if z > 0:
            diagonal = diagonal + above
        if z < NZ - 1:
            beneath = ref["P0"][z + 1] * inside
            above = VERTICAL * harmonic(here, beneath)
            diagonal = diagonal + above
        else:
            above = jnp.zeros_like(here)
        ref["D0"][z] = above
        ref["E0"][z] = east
        ref["N0"][z] = north
        ref["diag0"][z] = diagonal
    def place(level, names, pieces):
        for z in range(NZ):
            for k, name in enumerate(names):
                fill = 1.0 if name == "diag" else 0.0
                target = ref[f"{name}{level}"]
                if level == 1:
                    target[z, :, 0:128] = pieces[0][k][z]
                    lane = iota((16, 128), 1)
                    target[z, :, 128:256] = jnp.where((lane < 32) | (lane >= 96), pieces[1][k][z], fill)
                else:
                    lane = iota((16, 128), 1)
                    target[z] = jnp.where((lane < 48) | (lane >= 112), pieces[0][k][z], fill)

    names = ("E", "N", "D", "diag")
    fills = (0.0, 0.0, 0.0, 1.0)
    (own1,) = coarsen(0, own=True)
    for k, name in enumerate(names):
        for z in range(NZ):
            ref[f"{name}1"][z, 0:8, 0:128] = own1[k][z]
    (coarse2,) = coarsen(1)
    own2 = [[keep_own(coarse2[k][z], fills[k]) for z in range(NZ)] for k in range(4)]
    pack_wide("c2", lambda k, z: own2[k][z])
    tiles = [pack_tile(value) for value in coarsest_coefficients(coarse2)]
    await_relay(1)
    relay(2)
    copies_c2 = send_wide("c2", B_C2)
    stage = gather_columns("gc", tiles, total_of(storage_sum), B_GC1)

    receive_rows(copies_rows, ref["S0"], ref["rhs0"])
    receive_columns(copies_s, ref["S0"], 1, 1.0)
    for z in range(NZ):
        ref["diag0"][z] = ref["diag0"][z] + ref["S0"][z]
    factor(0)
    place(1, names, coarsen(0))
    factor(1)

    receive_columns(copies_r, ref["rhs0"], 2, 0.0)
    first_sweep(0)
    sweep(0)
    first_sweep(0)
    sweep(0)
    await_relay(2)
    relay(3)
    place(1, ("rhs",), [[piece] for piece in restrict(0)])
    first_sweep(1)
    sweep(1)
    (values,) = restrict(1)
    pack_wide("x2", lambda k, z: values[z])
    copies_x2 = send_wide("x2", B_X2)
    copies_v1 = send_u1()
    far_sides = [-REACH, REACH]
    copies_far = send_wide_to("c2", B_C2, far_sides)
    copies_far_x = send_wide_to("x2", B_X2, far_sides)

    await_relay(3)
    stage = gather_along_z("gc", stage, B_GCZ)

    two = [ref[f"{name}2"] for name in names]
    receive_wide("c2", copies_c2, two, fills, False)

    def prepare23():
        place(3, names, coarsen(2))
        factor(2)
        factor(3)

    def down23():
        first_sweep(2)
        sweep(2)
        place(3, ("rhs",), [[piece] for piece in restrict(2)])
        first_sweep(3)
        sweep(3)

    prepare23()
    receive_wide("x2", copies_x2, [ref["rhs2"]], (0.0,), False)
    stage_c = gather_along_x("gc", stage, B_GCX)
    down23()
    (values,) = restrict(3)
    tile = pack_tile(stack_layers(values))
    stage = gather_columns("gr", [tile], total_of(tile), B_GR1)
    receive_u1(copies_v1)
    stage_r = gather_rows("gr", stage, B_GR2)
    receive_wide("c2", copies_far, two, fills, True)
    receive_wide("x2", copies_far_x, [ref["rhs2"]], (0.0,), True)
    prepare23()
    down23()
    for name in ("E", "N", "g", "inv", "rhs", "u"):
        for z in range(NZ):
            ref[f"{name}2c"][z, 0:8, :] = ref[f"{name}2"][z, 0:8, :]
            ref[f"{name}2c"][z, 8:16, :] = ref[f"{name}2"][z, 24:32, :]

    for copy in stage_c:
        copy.wait_recv()
    lane = iota((16, 128), 1)
    row = iota((16, 128), 0)
    gap = (lane & 63) >= 48
    before = None
    for z in range(NZ):
        pivot = jnp.where(gap, 1.0, coarse_layer(ref["gc_r2"], 0, z))
        if z > 0:
            pivot = pivot - before * below
        inverse = 1.0 / pivot
        below = coarse_layer(ref["gc_r2"], 3, z)
        before = below * inverse
        at = slice(16 * z, 16 * z + 16)
        ref["inv4"][at, :] = inverse
        ref["g4"][at, :] = before
        ref["E4"][at, :] = coarse_layer(ref["gc_r2"], 1, z)
        ref["N4"][at, :] = coarse_layer(ref["gc_r2"], 2, z)
    storage_total = coarse_sum(ref["gc_r2"])
    for copy in stage_r:
        copy.wait_recv()
    shift = coarse_sum(ref["gr_r2"]) / storage_total
    for z in range(NZ):
        at = slice(16 * z, 16 * z + 16)
        ref["rhs4"][at, :] = coarse_layer(ref["gr_r2"], 0, z)
        ref["u4"][at, :] = jnp.broadcast_to(shift, (16, 128))

    def coarse_sweep(step, carry):
        value = None
        for z in range(NZ):
            u, east, north = coarse_at("u4", z), coarse_at("E4", z), coarse_at("N4", z)
            from_e = rot(u, -1, 0)
            from_e = jnp.where(row == 15, rot(from_e, 64, 1), from_e)
            from_w = rot(east * u, 1, 0)
            from_w = jnp.where(row == 0, rot(from_w, 64, 1), from_w)
            right = coarse_at("rhs4", z) + east * from_e + from_w + north * rot(u, -1, 1) + rot(north * u, 1, 1)
            value = right if z == 0 else right + coarse_at("g4", z - 1) * value
            ref["f4"][16 * z : 16 * z + 16, :] = value
        for z in range(NZ - 1, -1, -1):
            solved = coarse_at("f4", z) * coarse_at("inv4", z)
            value = solved if z == NZ - 1 else solved + coarse_at("g4", z) * value
            old = coarse_at("u4", z)
            ref["u4"][16 * z : 16 * z + 16, :] = old + OMEGA * (value - old)
        return carry

    lax.fori_loop(0, COARSE_SWEEPS, coarse_sweep, 0)

    turn = lax.rem(GX - gx, GX)

    def coarsest(_, z):
        value = coarse_at("u4", z)
        value = pltpu.roll(jnp.concatenate([value, rot(value, 64, 1)], axis=0), turn, 0)
        both = rot(jnp.where(row8 < 4, value[0:8], value[24:32]), -16, 1)
        return jnp.where((lane8 < 24) | (lane8 >= 112), both, 0.0)

    def from3(_, z):
        return jnp.where(row8 < 4, ref["u3"][z, 0:8, :], ref["u3"][z, 8:16, :])

    def from2(i, z):
        value = jnp.where(row8 < 6, ref["u2c"][z, 0:8, :], ref["u2c"][z, 8:16, :])
        return value if i == 0 else rot(value, 64, 1)

    prolong(3, coarsest)
    sweep(3)
    sweep(3)
    prolong("2c", from3)
    sweep("2c")
    sweep("2c")
    prolong(1, from2)
    sweep(1)
    sweep(1)
    prolong(0, lambda i, z: ref["u1"][z, :, 128 * i : 128 * (i + 1)])
    sweep(0)
    sweep(0, last=out)
    for copy in started:
        copy.wait_send()


def shards(
    newton_residual, pressure_head, conductivity, land_use, storage_table, return_table,
    well_cells, well_rates, return_cells,
):
    vmem = pl.BlockSpec(memory_space=pltpu.VMEM)
    hbm = pl.BlockSpec(memory_space=pltpu.HBM)
    smem = pl.BlockSpec(memory_space=pltpu.SMEM)
    wells = well_cells.shape[-1]
    return pl.pallas_call(
        kernel,
        out_shape=jax.ShapeDtypeStruct(newton_residual.shape, F32),
        in_specs=[hbm] * 4 + [smem] * 2 + [vmem] * 3,
        out_specs=vmem,
        scratch_shapes=list(PLAN.values()),
        compiler_params=pltpu.CompilerParams(
            collective_id=0, has_side_effects=True, vmem_limit_bytes=36 * 1024 * 1024
        ),
    )(
        newton_residual, pressure_head, conductivity, land_use, storage_table, return_table,
        well_cells.reshape(1, wells), well_rates.reshape(1, wells), return_cells.reshape(1, wells),
    )


def solution(mesh):
    return jax.shard_map(
        shards,
        mesh=mesh,
        in_specs=(
            P(None, "gx", "gy"),
            P(None, "gx", "gy"),
            P(None, "gx", "gy"),
            P("gx", "gy"),
            P(),
            P(),
            P("gx", "gy", None),
            P("gx", "gy", None),
            P("gx", "gy", None),
        ),
        out_specs=P(None, "gx", "gy"),
        check_vma=False,
    )
```

```python
import functools

import jax
import jax.numpy as jnp
from jax import lax
from jax.experimental import pallas as pl
from jax.experimental.pallas import tpu as pltpu
from jax.sharding import PartitionSpec as P

NZ = 16
CLASSES = 8
COARSE_SWEEPS = 12
OMEGA = 0.8
VERTICAL = 4.0
ALPHA = 0.5
F32 = jnp.float32
MESH = pl.DeviceIdType.MESH

NX = (16, 8, 4, 2)
NY = (256, 128, 64, 32)
XR = (32, 16, 32, 16)
YR = (384, 256, 128, 128)
REACH = 3
SIDES = [d for d in range(-REACH, REACH + 1) if d != 0]
GY, GX = 8, 32
N_E0 = 24
N_WIDE = 6 * REACH + 2
N_V1 = 8
B_E0 = 0
B_C2 = B_E0 + N_E0
B_X2 = B_C2 + N_WIDE
B_V1 = B_X2 + N_WIDE
N_HALO = B_V1 + N_V1
GZ, GXX = 8, 4
B_GC1 = N_HALO
B_GCZ = B_GC1 + GY - 1
B_GCX = B_GCZ + GZ - 1
B_GR1 = B_GCX + GZ * (GXX - 1)
B_GR2 = B_GR1 + GY - 1
N_SEM = B_GR2 + GX - 1
LEVEL_ARRAYS = ("E", "N", "D", "diag", "g", "inv", "rhs", "u", "f")


def rot(value, shift, axis):
    shift %= value.shape[axis]
    return value if shift == 0 else pltpu.roll(value, shift, axis)


def iota(shape, axis):
    return lax.broadcasted_iota(jnp.int32, shape, axis)


def between(index, start, count):
    return (index >= start) & (index < start + count)


def exact_dot(left, right):
    return jnp.dot(left, right, precision=lax.Precision.HIGHEST, preferred_element_type=F32)


def scratch_plan():
    plan = {}
    for level in range(4):
        for name in LEVEL_ARRAYS:
            plan[f"{name}{level}"] = pltpu.VMEM((NZ, XR[level], YR[level]), F32)
    for name in ("E", "N", "g", "inv", "rhs", "u", "f"):
        plan[f"{name}2c"] = pltpu.VMEM((NZ, 16, 128), F32)
    plan["P0"] = pltpu.VMEM((NZ, XR[0], YR[0]), F32)
    plan["S0"] = pltpu.VMEM((NZ, XR[0], YR[0]), F32)
    for name in ("E4", "N4", "g4", "inv4", "rhs4", "u4", "f4"):
        plan[name] = pltpu.VMEM((NZ * 16, 128), F32)
    for name in ("ta", "tb", "tc", "td"):
        plan[name] = pltpu.VMEM((NZ, 3, 32, 128), F32)
    plan["e0_sy"] = pltpu.VMEM((2, 3, 16, 128), F32)
    plan["e0_ry"] = pltpu.VMEM((2, 3, 16, 128), F32)
    plan["e0_rc"] = pltpu.VMEM((4, 3, 8, 128), F32)
    for kind in ("s", "r"):
        plan[f"e0_{kind}a"] = pltpu.VMEM((2, NZ, 8, 256), F32)
        plan[f"e0_{kind}b"] = pltpu.VMEM((2, NZ // 2, 8, 256), F32)
    for name, count in (("c2", 4), ("x2", 1)):
        plan[f"{name}_sx"] = pltpu.VMEM((count, 4, 8, 128), F32)
        plan[f"{name}_rx"] = pltpu.VMEM((2 * REACH + 1, count, 4, 8, 128), F32)
        plan[f"{name}_sy"] = pltpu.VMEM((2, count, 8, 128), F32)
        plan[f"{name}_ry"] = pltpu.VMEM((2, 2 * REACH + 1, count, 8, 128), F32)
    for kind in ("s", "r"):
        plan[f"v1_{kind}x"] = pltpu.VMEM((2, 8, 8, 128), F32)
        plan[f"v1_{kind}y"] = pltpu.VMEM((2, 8, 128), F32)
    plan["v1_rc"] = pltpu.VMEM((4, 8, 128), F32)
    for name in ("residual", "pressure", "conductivity"):
        plan[name] = pltpu.VMEM((NZ, NX[0], NY[0]), F32)
    plan["land_use"] = pltpu.VMEM((NX[0], NY[0]), jnp.int32)
    plan["relay"] = pltpu.SemaphoreType.REGULAR((4,))
    plan["load"] = pltpu.SemaphoreType.DMA((4,))
    for name, count in (("gc", 4), ("gr", 1)):
        plan[f"{name}_s1"] = pltpu.VMEM((count, 8, 128), F32)
        plan[f"{name}_r1"] = pltpu.VMEM((GY, count, 8, 128), F32)
        plan[f"{name}_s2"] = pltpu.VMEM((count, 8, 128), F32)
        plan[f"{name}_r2"] = pltpu.VMEM((count, GX * 8, 128), F32)
    plan["send"] = pltpu.SemaphoreType.DMA((N_SEM,))
    plan["recv"] = pltpu.SemaphoreType.DMA((N_SEM,))
    return plan


PLAN = scratch_plan()


def kernel(
    residual_in, pressure_in, conductivity_in, land_use_in, storage_table, return_table,
    well_cells, well_rates, return_cells, out, *scratch,
):
    ref = dict(zip(PLAN, scratch))
    gx = lax.axis_index("gx")
    gy = lax.axis_index("gy")

    def device(dx, dy):
        return (lax.rem(gx + (dx + GX), GX), lax.rem(gy + (dy + GY), GY))

    peers = [(dx, dy) for dx in (-1, 0, 1) for dy in (-1, 0, 1) if (dx, dy) != (0, 0)]
    relays = (peers, [(2 * dx, 2 * dy) for dx, dy in peers], [(-4, 0), (4, 0)], [(-8, 0), (8, 0)])

    def relay(stage):
        for dx, dy in relays[stage]:
            pl.semaphore_signal(
                ref["relay"].at[stage], inc=1, device_id=device(dx, dy), device_id_type=MESH
            )

    def await_relay(stage):
        pl.semaphore_wait(ref["relay"].at[stage], len(relays[stage]))

    barrier = pltpu.get_barrier_semaphore()
    for dx, dy in peers:
        pl.semaphore_signal(barrier, inc=1, device_id=device(dx, dy), device_id_type=MESH)

    loads = []
    for i, (name, source) in enumerate(
        (("land_use", land_use_in), ("pressure", pressure_in), ("conductivity", conductivity_in), ("residual", residual_in))
    ):
        loads.append(pltpu.make_async_copy(source, ref[name], ref["load"].at[i]))
        loads[-1].start()
    residual, pressure, conductivity, land_use = (
        ref[name] for name in ("residual", "pressure", "conductivity", "land_use")
    )
    started = []

    def remote(src, dst, index, dx, dy):
        copy = pltpu.make_async_remote_copy(
            src_ref=src, dst_ref=dst, send_sem=ref["send"].at[index], recv_sem=ref["recv"].at[index],
            device_id=device(dx, dy), device_id_type=MESH,
        )
        copy.start()
        started.append(copy)
        return copy

    row8 = iota((8, 128), 0)
    lane8 = iota((8, 128), 1)

    def send_permeable(array):
        copies = []
        for side, (own, there, dx) in enumerate(((0, 16, -1), (8, 24, 1))):
            copies.append(
                remote(
                    array.at[:, pl.ds(own, 8), pl.ds(0, 256)],
                    array.at[:, pl.ds(there, 8), pl.ds(0, 256)],
                    B_E0 + side, dx, 0,
                )
            )
        return copies

    row_wide = iota((8, 256), 0)

    def pack_rows(storage, source):
        sa, sb = ref["e0_sa"], ref["e0_sb"]
        for z in range(NZ):
            for side in (0, 1):
                at = slice(8 * side, 8 * side + 8)
                kept, moved = storage[z, at, 0:256], source[z, at, 0:256]
                if side == 0:
                    sa[side, z] = jnp.where(row_wide < 6, kept, rot(moved, 6, 0))
                else:
                    sa[side, z] = jnp.where(row_wide >= 2, kept, rot(moved, 2, 0))
                if z % 2 == 1:
                    first = source[z - 1, at, 0:256]
                    sb[side, z // 2] = jnp.where(row_wide < 4, rot(first, -2, 0), rot(moved, 2, 0))

    def send_rows():
        sa, sb, ra, rb = (ref[f"e0_{kind}"] for kind in ("sa", "sb", "ra", "rb"))
        copies = []
        for side, dx in ((0, -1), (1, 1)):
            copies.append(remote(sa.at[side], ra.at[side], B_E0 + 20 + side, dx, 0))
            copies.append(remote(sb.at[side], rb.at[side], B_E0 + 22 + side, dx, 0))
        return copies

    def receive_rows(copies, storage, source):
        for copy in copies:
            copy.wait_recv()
        ra, rb = ref["e0_ra"], ref["e0_rb"]
        middle = (row_wide >= 2) & (row_wide < 6)
        for z in range(NZ):
            shift = 2 if z % 2 == 0 else -2
            for side in (0, 1):
                at = slice(16 + 8 * side, 24 + 8 * side)
                tile, rest = ra[side, z], rot(rb[side, z // 2], shift, 0)
                if side == 0:
                    storage[z, at, 0:256] = jnp.where(row_wide < 6, tile, 1.0)
                    near = jnp.where(row_wide < 2, rot(tile, -6, 0), 0.0)
                else:
                    storage[z, at, 0:256] = jnp.where(row_wide >= 2, tile, 1.0)
                    near = jnp.where(row_wide >= 6, rot(tile, -2, 0), 0.0)
                source[z, at, 0:256] = jnp.where(middle, rest, near)

    def pack_columns(array, k):
        sy = ref["e0_sy"]
        lane = iota((16, 128), 1)
        low = jnp.zeros((16, 128), F32)
        high = jnp.zeros((16, 128), F32)
        for z in range(NZ):
            here = between(lane, 8 * z, 8)
            low = jnp.where(here, rot(array[z, 0:16, 0:128], 8 * z, 1), low)
            high = jnp.where(here, rot(array[z, 0:16, 128:256], 8 * z + 8, 1), high)
        sy[0, k] = low
        sy[1, k] = high

    def send_columns(k):
        sy, ry, rc = ref["e0_sy"], ref["e0_ry"], ref["e0_rc"]
        base = B_E0 + 2 + 6 * k
        copies = []
        first, last = pl.ds(0, 8), pl.ds(8, 8)
        moves = (
            (sy.at[0, k], ry.at[0, k], 0, -1),
            (sy.at[1, k], ry.at[1, k], 0, 1),
            (sy.at[0, k, first], rc.at[0, k], -1, -1),
            (sy.at[0, k, last], rc.at[1, k], 1, -1),
            (sy.at[1, k, first], rc.at[2, k], -1, 1),
            (sy.at[1, k, last], rc.at[3, k], 1, 1),
        )
        for i, (src, dst, dx, dy) in enumerate(moves):
            copies.append(remote(src, dst, base + i, dx, dy))
        return copies

    def receive_columns(copies, array, k, fill):
        for copy in copies:
            copy.wait_recv()
        ry, rc = ref["e0_ry"], ref["e0_rc"]
        lane = iota((32, 128), 1)
        north = jnp.concatenate([ry[0, k], rc[0, k], rc[1, k]], axis=0)
        south = jnp.concatenate([ry[1, k], rc[2, k], rc[3, k]], axis=0)
        for z in range(NZ):
            value = jnp.where(lane >= 120, rot(south, -8 * (z + 1), 1), fill)
            array[z, :, 256:384] = jnp.where(lane < 8, rot(north, -8 * z, 1), value)

    def pack_wide(name, get):
        sx, sy, rx = (ref[f"{name}_{kind}"] for kind in ("sx", "sy", "rx"))
        for a in range(sx.shape[0]):
            values = [get(a, z) for z in range(NZ)]
            for t in range(4):
                left = jnp.where(row8 < 4, values[t], rot(values[t + 4], 4, 0))
                right = jnp.where(row8 < 4, values[t + 8], rot(values[t + 12], 4, 0))
                tile = jnp.where(lane8 < 64, left, rot(right, 64, 1))
                sx[a, t] = tile
                rx[REACH, a, t] = tile
            low = jnp.zeros((8, 128), F32)
            high = jnp.zeros((8, 128), F32)
            for q in range(8):
                both = jnp.where(row8 < 4, values[q], rot(values[q + 8], 4, 0))
                here = between(lane8, 16 * q, 16)
                low = jnp.where(here, rot(both, 16 * q, 1), low)
                high = jnp.where(here, rot(both, 16 * q - 48, 1), high)
            sy[0, a] = low
            sy[1, a] = high

    def send_wide(name, base):
        return send_wide_to(name, base, [d for d in SIDES if abs(d) < REACH])

    def send_wide_to(name, base, sides):
        sx, sy, rx, ry = (ref[f"{name}_{kind}"] for kind in ("sx", "sy", "rx", "ry"))
        far = REACH in sides
        copies = []
        for d in sides:
            copies.append(remote(sx, rx.at[REACH - d], base + SIDES.index(d), d, 0))
        for side, dy in ((0, -1), (1, 1)):
            for d in sides if far else sides + [0]:
                index = 2 * REACH + side * (2 * REACH + 1) + d + REACH
                copies.append(remote(sy.at[side], ry.at[side, REACH - d], base + index, d, dy))
        return copies

    def receive_wide(name, copies, targets, fills, far):
        for copy in copies:
            copy.wait_recv()
        rx, ry = ref[f"{name}_rx"], ref[f"{name}_ry"]
        empty = jnp.zeros((8, 128), F32)

        def join(first, second):
            return (
                jnp.where(row8 < 4, first, rot(second, 4, 0)),
                jnp.where(row8 < 4, rot(first, 4, 0), second),
            )

        for a, (target, fill) in enumerate(zip(targets, fills)):
            tiles = {0: (0, 1), 1: (2, None), 2: (None, None), 3: (-2, -1)}
            if far:
                tiles = {1: (2, 3), 2: (None, -3)}
            for p, (k0, k1) in tiles.items():
                if k0 is None and k1 is None:
                    for z in range(NZ):
                        target[z, 8 * p : 8 * p + 8, :] = jnp.full((8, 128), fill, F32)
                    continue
                layers = [None] * NZ
                for t in range(4):
                    first = empty if k0 is None else rx[REACH + k0, a, t]
                    second = empty if k1 is None else rx[REACH + k1, a, t]
                    for i, both in enumerate(join(first, second)):
                        layers[t + 4 * i] = both
                        layers[t + 4 * i + 8] = rot(both, 64, 1)
                sides = []
                for side in (0, 1):
                    first = empty if k0 is None else ry[side, REACH + k0, a]
                    second = empty if k1 is None else ry[side, REACH + k1, a]
                    sides.append(join(first, second))
                for z in range(NZ):
                    q = z % 8
                    north = rot(sides[0][z // 8], 64 - 16 * q, 1)
                    south = rot(sides[1][z // 8], 112 - 16 * q, 1)
                    value = jnp.where(lane8 < 80, north, jnp.where(lane8 >= 112, south, fill))
                    value = jnp.where(lane8 < 64, layers[z], value)
                    if k0 is None:
                        value = jnp.where(row8 < 4, fill, value)
                    if k1 is None:
                        value = jnp.where(row8 < 4, value, fill)
                    target[z, 8 * p : 8 * p + 8, :] = value

    def send_u1():
        sx, sy, rx, ry, rc = (ref[f"v1_{kind}"] for kind in ("sx", "sy", "rx", "ry", "rc"))
        low = jnp.zeros((8, 128), F32)
        high = jnp.zeros((8, 128), F32)
        for z in range(NZ):
            u = ref["u1"][z, 0:8, 0:128]
            if z % 2 == 0:
                before = u
            else:
                sx[0, z // 2] = jnp.where(row8 < 4, before, rot(u, 4, 0))
                sx[1, z // 2] = jnp.where(row8 < 4, rot(before, 4, 0), u)
            here = between(lane8, 4 * z, 4)
            low = jnp.where(here, rot(u, 4 * z, 1), low)
            high = jnp.where(here, rot(u, 4 * z + 4, 1), high)
        sy[0] = low
        sy[1] = high
        moves = (
            (sx.at[0], rx.at[0], -1, 0),
            (sx.at[1], rx.at[1], 1, 0),
            (sy.at[0], ry.at[0], 0, -1),
            (sy.at[1], ry.at[1], 0, 1),
            (sy.at[0], rc.at[0], -1, -1),
            (sy.at[0], rc.at[1], 1, -1),
            (sy.at[1], rc.at[2], -1, 1),
            (sy.at[1], rc.at[3], 1, 1),
        )
        return [remote(src, dst, B_V1 + i, dx, dy) for i, (src, dst, dx, dy) in enumerate(moves)]

    def receive_u1(copies):
        for copy in copies:
            copy.wait_recv()
        rx, ry, rc = (ref[f"v1_{kind}"] for kind in ("rx", "ry", "rc"))
        lane = iota((16, 128), 1)
        north = jnp.concatenate([ry[0], jnp.where(row8 < 4, rc[0], rc[1])], axis=0)
        south = jnp.concatenate([ry[1], jnp.where(row8 < 4, rc[2], rc[3])], axis=0)
        u = ref["u1"]
        for z in range(NZ):
            east, west = rx[0, z // 2], rx[1, z // 2]
            if z % 2 == 0:
                value = jnp.where(row8 < 4, east, rot(west, 4, 0))
            else:
                value = jnp.where(row8 < 4, rot(east, 4, 0), west)
            u[z, 8:16, 0:128] = value
            value = jnp.where(lane >= 124, rot(south, -4 * (z + 1), 1), 0.0)
            u[z, :, 128:256] = jnp.where(lane < 4, rot(north, -4 * z, 1), value)

    HALF = NZ // 2

    def factor_columns(diag, down, put):
        top = bottom = None
        for i in range(HALF):
            z = i
            pivot = diag(z) if i == 0 else diag(z) - top * down(z - 1)
            inverse = 1.0 / pivot
            top = down(z) * inverse
            put(z, inverse, top)
            z = NZ - 1 - i
            pivot = diag(z) if i == 0 else diag(z) - bottom * down(z)
            if z == HALF:
                pivot = pivot - top * down(z - 1)
            inverse = 1.0 / pivot
            bottom = down(z - 1) * inverse
            put(z, inverse, bottom)

    def factor(level):
        diag, down, g, inv = (ref[f"{name}{level}"] for name in ("diag", "D", "g", "inv"))

        def put(z, inverse, inwards):
            inv[z] = inverse
            g[z] = inwards

        factor_columns(lambda z: diag[z], lambda z: down[z], put)

    def solve_columns(right, g, inv, put_f, get_f, update):
        top = bottom = None
        for i in range(HALF):
            z = i
            top = right(z) if i == 0 else right(z) + g(z - 1) * top
            put_f(z, top)
            z = NZ - 1 - i
            bottom = right(z) if i == 0 else right(z) + g(z + 1) * bottom
            if z > HALF:
                put_f(z, bottom)
        below = (bottom + g(HALF - 1) * top) * inv(HALF)
        update(HALF, below)
        above = below
        for i in range(HALF):
            z = HALF - 1 - i
            above = get_f(z) * inv(z) + g(z) * above
            update(z, above)
            z = HALF + 1 + i
            if z < NZ:
                below = get_f(z) * inv(z) + g(z) * below
                update(z, below)

    def first_sweep(level):
        g, inv, f, rhs, u = (ref[f"{name}{level}"] for name in ("g", "inv", "f", "rhs", "u"))

        def put_f(z, value):
            f[z] = value

        def update(z, solved):
            u[z] = OMEGA * solved

        solve_columns(
            lambda z: rhs[z], lambda z: g[z], lambda z: inv[z], put_f, lambda z: f[z], update
        )

    def lateral(level, z, u):
        east, north = ref[f"E{level}"][z], ref[f"N{level}"][z]
        return (
            east * rot(u, -1, 0) + rot(east * u, 1, 0) + north * rot(u, -1, 1) + rot(north * u, 1, 1)
        )

    def sweep(level, last=None):
        g, f, rhs, u = (ref[f"{name}{level}"] for name in ("g", "f", "rhs", "u"))
        inv = ref[f"inv{level}"]
        rows, lanes = u.shape[1:] if last is None else last.shape[1:]
        at = (slice(0, rows), slice(0, lanes))

        def put_f(z, value):
            f[(z, *at)] = value

        def update(z, solved):
            old = u[(z, *at)]
            value = old + OMEGA * (solved - old)
            if last is None:
                u[z] = value
            else:
                last[z] = value

        solve_columns(
            lambda z: rhs[(z, *at)] + lateral(level, z, u[z])[at], lambda z: g[(z, *at)],
            lambda z: inv[(z, *at)], put_f, lambda z: f[(z, *at)], update,
        )

    def remainder(level, z):
        diag, down, rhs, u = (ref[f"{name}{level}"] for name in ("diag", "D", "rhs", "u"))
        here = u[z]
        value = rhs[z] + lateral(level, z, here) - diag[z] * here
        if z < NZ - 1:
            value = value + down[z] * u[z + 1]
        if z > 0:
            value = value + down[z - 1] * u[z - 1]
        return value

    PIECES = (
        ((0, 256, 256, 256), (256, 128, 64, 128)),
        ((0, 128, 128, 128),),
        ((0, 128, 96, 128),),
        ((0, 128, 128, 32),),
    )
    ROWS = (32, 8, 32, 8)

    def lane_matrix(piece, kind, transpose=False):
        _, count, turn, limit = piece
        shape = (128, count) if transpose else (count, 128)
        fine = iota(shape, 1 if transpose else 0)
        coarse = iota(shape, 0 if transpose else 1)
        hit = (((fine >> 1) + jnp.where(fine >= turn, 64, 0)) == coarse) & (fine < limit)
        if kind != "sum":
            hit = hit & ((fine & 1) == (1 if kind == "odd" else 0))
        return jnp.where(hit, 1.0, 0.0).astype(F32)

    def put_rows(buffer, rows, z, value):
        for t in range(value.shape[1] // 128):
            buffer[z, t, 0:rows, :] = value[0:rows, 128 * t : 128 * (t + 1)]

    def row_half(buffer, count_rows, piece, z, odd):
        start, count = piece[0], piece[1]
        parts = []
        for t in range(start // 128, (start + count) // 128):
            rows = [buffer[z, t, pl.ds(i + odd, 8, stride=2), :] for i in range(0, count_rows, 16)]
            parts.append(rows[0] if len(rows) == 1 else jnp.concatenate(rows, axis=0))
        return parts[0] if len(parts) == 1 else jnp.concatenate(parts, axis=1)

    def coarse_rows(rows):
        return max(8, rows // 2)

    def lanes_of(level):
        return sum(piece[1] for piece in PIECES[level])

    def layers_of(value, rows):
        return [value[rows * z : rows * (z + 1)] for z in range(NZ)]

    def keep_own(value, fill):
        return jnp.where((row8 < 4) & (lane8 < 64), value, fill)

    def aggregate(level, rows, pieces_of, get):
        for z in range(NZ):
            put_rows(ref["ta"], rows, z, get(z))
        pieces = []
        for piece in pieces_of:
            summed = jnp.concatenate(
                [row_half(ref["ta"], rows, piece, z, 0) + row_half(ref["ta"], rows, piece, z, 1) for z in range(NZ)],
                axis=0,
            )
            pieces.append(layers_of(exact_dot(summed, lane_matrix(piece, "sum")), coarse_rows(rows)))
        return pieces

    def restrict(level):
        lanes = lanes_of(level)
        return aggregate(level, ROWS[level], PIECES[level], lambda z: remainder(level, z)[:, 0:lanes])

    def coarsen(level, extra=None):
        rows_fine = ROWS[level]
        lanes = lanes_of(level)
        names = ("E", "N", "D", "diag")
        buffers = [ref[name] for name in ("ta", "tb", "tc", "td")]
        for z in range(NZ):
            for name, buffer in zip(names, buffers):
                value = ref[f"{name}{level}"][z, 0:rows_fine, 0:lanes]
                if extra is not None and name == "diag":
                    value = value + extra[z]
                put_rows(buffer, rows_fine, z, value)
        pieces = []
        for piece in PIECES[level]:
            odd_e, sum_n, sum_d, sum_g = [], [], [], []
            for z in range(NZ):
                (e0, e1), (n0, n1), (d0, d1), (g0, g1) = (
                    [row_half(buffer, rows_fine, piece, z, odd) for odd in (0, 1)] for buffer in buffers
                )
                odd_e.append(e1)
                sum_n.append(n0 + n1)
                sum_d.append(d0 + d1)
                sum_g.append(g0 + g1 - 2.0 * e0)
            total = lane_matrix(piece, "sum")
            rows = coarse_rows(rows_fine)
            east = exact_dot(jnp.concatenate(odd_e, axis=0), total)
            down = exact_dot(jnp.concatenate(sum_d, axis=0), total)
            north = jnp.concatenate(sum_n, axis=0)
            diagonal = exact_dot(jnp.concatenate(sum_g, axis=0), total) - 2.0 * exact_dot(
                north, lane_matrix(piece, "even")
            )
            north = exact_dot(north, lane_matrix(piece, "odd"))
            pieces.append([layers_of(value, rows) for value in (east, north, down, diagonal)])
        return pieces

    def prolong(level, coarse):
        buffer = ref["ta"]
        u = ref[f"u{level}"]
        pieces = {
            0: ((0, 256, 256, 256), (256, 128, 64, 128)),
            1: ((0, 128, 128, 128), (128, 128, 128, 128)),
            "2c": ((0, 128, 96, 128),),
            3: ((0, 128, 96, 128),),
        }[level]
        for i, piece in enumerate(pieces):
            value = jnp.concatenate([coarse(i, z) for z in range(NZ)], axis=0)
            rows = value.shape[0] // NZ
            fine = exact_dot(value, lane_matrix(piece, "sum", transpose=True))
            start, count = piece[0], piece[1]
            for z in range(NZ):
                for t in range(count // 128):
                    for r in range(0, rows, 8):
                        part = fine[rows * z + r : rows * z + r + 8, 128 * t : 128 * (t + 1)]
                        for odd in (0, 1):
                            buffer[z, start // 128 + t, pl.ds(2 * r + odd, 8, stride=2), :] = part
        for z in range(NZ):
            add = [buffer[z, t, 0 : u.shape[1], :] for t in range(u.shape[2] // 128)]
            u[z] = u[z] + (add[0] if len(add) == 1 else jnp.concatenate(add, axis=1))

    at_sum = (lane8 == 48) & (row8 == 0)

    def pack_tile(stacked):
        stacked = jnp.where(iota((16, 128), 1) < 16, stacked, 0.0)
        return rot(stacked[0:8], 16, 1) + rot(stacked[8:16], 80, 1)

    def stack_layers(values):
        row16 = iota((16, 128), 0)
        stacked = jnp.zeros((16, 128), F32)
        for z in range(NZ):
            stacked = jnp.where(row16 == z, jnp.broadcast_to(values[z][0:1], (16, 128)), stacked)
        return stacked

    def coarsest_coefficients(coarse2):
        east, north, down, diagonal = (
            jnp.concatenate([keep_own(value, 0.0) for value in values], axis=0) for values in coarse2
        )
        layer, row_of = iota((16, 128), 0), iota((16, 128), 1)
        rows = jnp.where((row_of >> 3) == layer, 1.0, 0.0).astype(F32)
        last_row = jnp.where(row_of == 8 * layer + 3, 1.0, 0.0).astype(F32)
        inner = jnp.where((iota((128, 128), 0) & 7) < 3, 2.0, 0.0) * east
        fine, coarse = iota((128, 128), 0), iota((128, 128), 1)
        hit = ((fine >> 2) == coarse) & (fine < 64)
        lanes = jnp.where(hit, 1.0, 0.0).astype(F32)
        last_lane = jnp.where(hit & ((fine & 3) == 3), 1.0, 0.0).astype(F32)
        summed = exact_dot(
            jnp.concatenate(
                [exact_dot(last_row, east), exact_dot(rows, down), exact_dot(rows, diagonal - inner)], axis=0
            ),
            lanes,
        )
        north = exact_dot(rows, north)
        north4 = exact_dot(north, last_lane)
        diagonal4 = summed[32:48] - 2.0 * exact_dot(north, lanes - last_lane)
        return diagonal4, summed[0:16], north4, summed[16:32]

    def total_of(value):
        return jnp.sum(jnp.sum(value, axis=1, keepdims=True), axis=0, keepdims=True)

    def gather_columns(name, tiles, part, base):
        s1, r1 = ref[f"{name}_s1"], ref[f"{name}_r1"]
        for a, tile in enumerate(tiles):
            s1[a] = jnp.where(at_sum, part, tile) if a == 0 else tile
        copies = []
        for d in range(1, GY):
            near = d in (1, GY - 1)
            copies.append(
                remote(s1 if near else s1.at[0], r1.at[d] if near else r1.at[d, 0], base + d - 1, 0, d)
            )
        return copies

    def at_row(gx_of):
        return pl.ds(pl.multiple_of(8 * gx_of, 8), 8)

    def window_of(name, copies):
        for copy in copies:
            copy.wait_recv()
        s1, r1, s2, r2 = (ref[f"{name}_{kind}"] for kind in ("s1", "r1", "s2", "r2"))
        for a in range(s1.shape[0]):
            clean = [s1[a], r1[1, a], r1[GY - 1, a]]
            if a == 0:
                clean = [jnp.where(at_sum, 0.0, tile) for tile in clean]
            window = clean[0] + rot(clean[1], -16, 1) + rot(clean[2], 16, 1)
            if a == 0:
                parts = s1[0]
                for d in range(1, GY):
                    parts = parts + r1[d, 0]
                window = jnp.where(at_sum, parts, window)
            s2[a] = window
            r2[a, at_row(gx), :] = window
        return s2, r2

    def gather_rows(name, copies, base):
        s2, r2 = window_of(name, copies)
        return [remote(s2, r2.at[:, at_row(gx), :], base + d - 1, d, 0) for d in range(1, GX)]

    def gather_along_z(name, copies, base):
        s2, r2 = window_of(name, copies)
        return [remote(s2, r2.at[:, at_row(gx), :], base + d - 1, GXX * d, 0) for d in range(1, GZ)]

    def gather_along_x(name, copies, base):
        for copy in copies:
            copy.wait_recv()
        r2 = ref[f"{name}_r2"]
        x = lax.rem(gx, GXX)
        result = []
        for d in range(1, GXX):
            there = lax.rem(x + d, GXX) - x
            for z in range(GZ):
                rows = r2.at[:, at_row(GXX * z + x), :]
                copy = pltpu.make_async_remote_copy(
                    src_ref=rows, dst_ref=rows, send_sem=ref["send"].at[base + len(result)],
                    recv_sem=ref["recv"].at[base + len(result)],
                    device_id=(gx + there, gy), device_id_type=MESH,
                )
                copy.start()
                started.append(copy)
                result.append(copy)
        return result

    def coarse_layer(buffer, a, z):
        sub, half = z % 8, z // 8
        pieces = [buffer[a, pl.ds(64 * i + sub, 8, stride=8), :] for i in range(4)]
        low = jnp.concatenate(pieces[0:2], axis=0)
        high = jnp.concatenate(pieces[2:4], axis=0)
        lane = iota((16, 128), 1)
        if half == 0:
            return jnp.where(lane < 64, low, rot(high, 64, 1))
        return jnp.where(lane < 64, rot(low, 64, 1), high)

    def coarse_sum(buffer):
        value = jnp.where(at_sum, buffer[0, 0:8, :], 0.0)
        for k in range(1, GX):
            value = value + jnp.where(at_sum, buffer[0, 8 * k : 8 * k + 8, :], 0.0)
        return total_of(value)

    def put_layer(name, z, value):
        ref[name][16 * z : 16 * z + 16, :] = value

    def coarse_at(name, z):
        return ref[name][16 * z : 16 * z + 16, :]

    for copy in loads:
        copy.wait()
    use = land_use[...]
    table = jnp.zeros(use.shape, F32)
    fraction = jnp.zeros(use.shape, F32)
    for category in range(CLASSES):
        table = table + jnp.where(use == category, storage_table[category], 0.0)
        fraction = fraction + jnp.where(use == category, return_table[category], 0.0)
    cells, rates, returns = well_cells[...], well_rates[...], return_cells[...]
    wells = rates.shape[1]

    def hits(count, index):
        return iota((count, wells), 0) == index

    def outer(count, index_row, index_column):
        left = jnp.where(hits(count, index_row), rates, 0.0)
        right = jnp.where(hits(256, index_column), 1.0, 0.0).astype(F32)
        return lax.dot_general(
            left, right, (((1,), (1,)), ((), ())),
            precision=lax.Precision.HIGHEST, preferred_element_type=F32,
        )

    storage_sum = jnp.zeros((16, 256), F32)
    for z in range(NZ):
        relief = jnp.exp(ALPHA * jnp.minimum(pressure[z], 0.0))
        ref["P0"][z, 0:16, 0:256] = conductivity[z] * relief
        storage = table * relief
        ref["S0"][z, 0:16, 0:256] = storage
        storage_sum = storage_sum + storage
    pumped = outer(256, cells >> 8, cells & 255)
    recharge = fraction * outer(16, returns >> 8, returns & 255)
    for z in range(NZ):
        source = residual[z] - pumped[16 * z : 16 * z + 16]
        if z == 0:
            source = source + recharge
        ref["rhs0"][z, 0:16, 0:256] = source
    for k, name in enumerate(("P0", "S0", "rhs0")):
        pack_columns(ref[name], k)
    pack_rows(ref["S0"], ref["rhs0"])
    pl.semaphore_wait(barrier, len(peers))
    copies_p = send_permeable(ref["P0"]) + send_columns(0)
    copies_rows = send_rows()
    copies_s = send_columns(1)
    copies_r = send_columns(2)
    relay(0)
    await_relay(0)
    relay(1)
    receive_columns(copies_p, ref["P0"], 0, 0.0)

    flags = [
        jnp.where(inside, 1.0, 0.0).astype(F32)
        for inside in (gx < GX - 1, gx > 0, gy < GY - 1, gy > 0)
    ]
    row = iota((32, 384), 0)
    lane = iota((32, 384), 1)
    inside = jnp.where(row < 16, 1.0, jnp.where(row < 24, flags[0], flags[1]))
    inside = inside * jnp.where(lane < 256, 1.0, jnp.where(lane < 320, flags[2], flags[3]))

    def harmonic(first_value, second_value):
        return 2.0 * first_value * second_value / (first_value + second_value + 1e-30)

    above = None
    for z in range(NZ):
        here = ref["P0"][0] * inside if z == 0 else beneath
        east = harmonic(here, rot(here, -1, 0))
        north = harmonic(here, rot(here, -1, 1))
        diagonal = east + rot(east, 1, 0) + north + rot(north, 1, 1)
        if z > 0:
            diagonal = diagonal + above
        if z < NZ - 1:
            beneath = ref["P0"][z + 1] * inside
            above = VERTICAL * harmonic(here, beneath)
            diagonal = diagonal + above
        else:
            above = jnp.zeros_like(here)
        ref["D0"][z] = above
        ref["E0"][z] = east
        ref["N0"][z] = north
        ref["diag0"][z] = diagonal
    def place(level, names, pieces):
        for z in range(NZ):
            for k, name in enumerate(names):
                fill = 1.0 if name == "diag" else 0.0
                target = ref[f"{name}{level}"]
                if level == 1:
                    target[z, :, 0:128] = pieces[0][k][z]
                    lane = iota((16, 128), 1)
                    target[z, :, 128:256] = jnp.where((lane < 32) | (lane >= 96), pieces[1][k][z], fill)
                else:
                    lane = iota((16, 128), 1)
                    target[z] = jnp.where((lane < 48) | (lane >= 112), pieces[0][k][z], fill)

    names = ("E", "N", "D", "diag")
    fills = (0.0, 0.0, 0.0, 1.0)
    place(1, names, coarsen(0))
    (own_storage,) = aggregate(0, 16, PIECES[0][0:1], lambda z: ref["S0"][z, 0:16, 0:256])
    (coarse2,) = coarsen(1, extra=own_storage)
    own2 = [[keep_own(coarse2[k][z], fills[k]) for z in range(NZ)] for k in range(4)]
    pack_wide("c2", lambda k, z: own2[k][z])
    tiles = [pack_tile(value) for value in coarsest_coefficients(coarse2)]
    await_relay(1)
    relay(2)
    copies_c2 = send_wide("c2", B_C2)
    stage = gather_columns("gc", tiles, total_of(storage_sum), B_GC1)

    receive_rows(copies_rows, ref["S0"], ref["rhs0"])
    receive_columns(copies_s, ref["S0"], 1, 1.0)
    for z in range(NZ):
        ref["diag0"][z] = ref["diag0"][z] + ref["S0"][z]
    factor(0)
    storage1 = aggregate(0, 32, PIECES[0], lambda z: ref["S0"][z])
    lane = iota((16, 128), 1)
    for z in range(NZ):
        diagonal = ref["diag1"]
        diagonal[z, :, 0:128] = diagonal[z, :, 0:128] + storage1[0][z]
        tail = jnp.where((lane < 32) | (lane >= 96), storage1[1][z], 0.0)
        diagonal[z, :, 128:256] = diagonal[z, :, 128:256] + tail
    factor(1)

    receive_columns(copies_r, ref["rhs0"], 2, 0.0)
    first_sweep(0)
    sweep(0)
    first_sweep(0)
    sweep(0)
    await_relay(2)
    relay(3)
    place(1, ("rhs",), [[piece] for piece in restrict(0)])
    first_sweep(1)
    sweep(1)
    (values,) = restrict(1)
    pack_wide("x2", lambda k, z: values[z])
    copies_x2 = send_wide("x2", B_X2)
    copies_v1 = send_u1()
    far_sides = [-REACH, REACH]
    copies_far = send_wide_to("c2", B_C2, far_sides)
    copies_far_x = send_wide_to("x2", B_X2, far_sides)

    await_relay(3)
    stage = gather_along_z("gc", stage, B_GCZ)

    two = [ref[f"{name}2"] for name in names]
    receive_wide("c2", copies_c2, two, fills, False)

    def prepare23():
        place(3, names, coarsen(2))
        factor(2)
        factor(3)

    def down23():
        first_sweep(2)
        sweep(2)
        place(3, ("rhs",), [[piece] for piece in restrict(2)])
        first_sweep(3)
        sweep(3)

    prepare23()
    receive_wide("x2", copies_x2, [ref["rhs2"]], (0.0,), False)
    down23()
    (values,) = restrict(3)
    tile = pack_tile(stack_layers(values))
    stage_r = gather_columns("gr", [tile], total_of(tile), B_GR1)
    stage_c = gather_along_x("gc", stage, B_GCX)
    receive_u1(copies_v1)
    stage_r = gather_rows("gr", stage_r, B_GR2)
    receive_wide("c2", copies_far, two, fills, True)
    receive_wide("x2", copies_far_x, [ref["rhs2"]], (0.0,), True)
    prepare23()
    down23()
    for name in ("E", "N", "g", "inv", "rhs", "u"):
        for z in range(NZ):
            ref[f"{name}2c"][z, 0:8, :] = ref[f"{name}2"][z, 0:8, :]
            ref[f"{name}2c"][z, 8:16, :] = ref[f"{name}2"][z, 24:32, :]

    for copy in stage_c:
        copy.wait_recv()
    lane = iota((16, 128), 1)
    row = iota((16, 128), 0)
    gap = (lane & 63) >= 48

    def put_coarse(z, inverse, inwards):
        put_layer("inv4", z, inverse)
        put_layer("g4", z, inwards)

    factor_columns(
        lambda z: jnp.where(gap, 1.0, coarse_layer(ref["gc_r2"], 0, z)),
        lambda z: coarse_layer(ref["gc_r2"], 3, z),
        put_coarse,
    )
    for z in range(NZ):
        put_layer("E4", z, coarse_layer(ref["gc_r2"], 1, z))
        put_layer("N4", z, coarse_layer(ref["gc_r2"], 2, z))
    storage_total = coarse_sum(ref["gc_r2"])
    for copy in stage_r:
        copy.wait_recv()
    shift = coarse_sum(ref["gr_r2"]) / storage_total
    for z in range(NZ):
        at = slice(16 * z, 16 * z + 16)
        ref["rhs4"][at, :] = coarse_layer(ref["gr_r2"], 0, z)
        ref["u4"][at, :] = jnp.broadcast_to(shift, (16, 128))

    def coarse_sweep(step, carry):
        def right(z):
            u, east, north = coarse_at("u4", z), coarse_at("E4", z), coarse_at("N4", z)
            from_e = rot(u, -1, 0)
            from_e = jnp.where(row == 15, rot(from_e, 64, 1), from_e)
            from_w = rot(east * u, 1, 0)
            from_w = jnp.where(row == 0, rot(from_w, 64, 1), from_w)
            return (
                coarse_at("rhs4", z) + east * from_e + from_w + north * rot(u, -1, 1) + rot(north * u, 1, 1)
            )

        def update(z, solved):
            old = coarse_at("u4", z)
            put_layer("u4", z, old + OMEGA * (solved - old))

        solve_columns(
            right, lambda z: coarse_at("g4", z), lambda z: coarse_at("inv4", z),
            lambda z, value: put_layer("f4", z, value), lambda z: coarse_at("f4", z), update,
        )
        return carry

    lax.fori_loop(0, COARSE_SWEEPS, coarse_sweep, 0)

    turn = lax.rem(GX - gx, GX)

    def coarsest(_, z):
        value = coarse_at("u4", z)
        value = pltpu.roll(jnp.concatenate([value, rot(value, 64, 1)], axis=0), turn, 0)
        both = rot(jnp.where(row8 < 4, value[0:8], value[24:32]), -16, 1)
        return jnp.where((lane8 < 24) | (lane8 >= 112), both, 0.0)

    def from3(_, z):
        return jnp.where(row8 < 4, ref["u3"][z, 0:8, :], ref["u3"][z, 8:16, :])

    def from2(i, z):
        value = jnp.where(row8 < 6, ref["u2c"][z, 0:8, :], ref["u2c"][z, 8:16, :])
        return value if i == 0 else rot(value, 64, 1)

    prolong(3, coarsest)
    sweep(3)
    sweep(3)
    prolong("2c", from3)
    sweep("2c")
    sweep("2c")
    prolong(1, from2)
    sweep(1)
    sweep(1)
    prolong(0, lambda i, z: ref["u1"][z, :, 128 * i : 128 * (i + 1)])
    sweep(0)
    sweep(0, last=out)
    for copy in started:
        copy.wait_send()


def shards(
    newton_residual, pressure_head, conductivity, land_use, storage_table, return_table,
    well_cells, well_rates, return_cells,
):
    vmem = pl.BlockSpec(memory_space=pltpu.VMEM)
    hbm = pl.BlockSpec(memory_space=pl.ANY)
    smem = pl.BlockSpec(memory_space=pltpu.SMEM)
    wells = well_cells.shape[-1]
    return pl.pallas_call(
        kernel,
        out_shape=jax.ShapeDtypeStruct(newton_residual.shape, F32),
        in_specs=[hbm] * 4 + [smem] * 2 + [vmem] * 3,
        out_specs=vmem,
        scratch_shapes=list(PLAN.values()),
        compiler_params=pltpu.CompilerParams(
            collective_id=0, has_side_effects=True, vmem_limit_bytes=54784 * 1024
        ),
    )(
        newton_residual, pressure_head, conductivity, land_use, storage_table, return_table,
        well_cells.reshape(1, wells), well_rates.reshape(1, wells), return_cells.reshape(1, wells),
    )


def solution(mesh):
    return jax.shard_map(
        shards,
        mesh=mesh,
        in_specs=(
            P(None, "gx", "gy"),
            P(None, "gx", "gy"),
            P(None, "gx", "gy"),
            P("gx", "gy"),
            P(),
            P(),
            P("gx", "gy", None),
            P("gx", "gy", None),
            P("gx", "gy", None),
        ),
        out_specs=P(None, "gx", "gy"),
        check_vma=False,
    )
```

```python
import functools

import jax
import jax.numpy as jnp
from jax import lax
from jax.experimental import pallas as pl
from jax.experimental.pallas import tpu as pltpu
from jax.sharding import PartitionSpec as P

NZ = 16
CLASSES = 8
COARSE_SWEEPS = 12
OMEGA = 0.8
VERTICAL = 4.0
ALPHA = 0.5
F32 = jnp.float32
MESH = pl.DeviceIdType.MESH

NX = (16, 8, 4, 2)
NY = (256, 128, 64, 32)
XR = (32, 16, 32, 16)
YR = (384, 256, 128, 128)
REACH = 3
SIDES = [d for d in range(-REACH, REACH + 1) if d != 0]
GY, GX = 8, 32
N_E0 = 24
N_WIDE = 6 * REACH + 2
N_V1 = 8
B_E0 = 0
B_C2 = B_E0 + N_E0
B_X2 = B_C2 + N_WIDE
B_V1 = B_X2 + N_WIDE
N_HALO = B_V1 + N_V1
GZ, GXX = 8, 4
B_GC1 = N_HALO
B_GCZ = B_GC1 + GY - 1
B_GCX = B_GCZ + GZ - 1
B_GR1 = B_GCX + GZ * (GXX - 1)
B_GR2 = B_GR1 + GY - 1
N_SEM = B_GR2 + GX - 1
LEVEL_ARRAYS = ("E", "N", "D", "diag", "g", "inv", "rhs", "u", "f")


def rot(value, shift, axis):
    shift %= value.shape[axis]
    return value if shift == 0 else pltpu.roll(value, shift, axis)


def iota(shape, axis):
    return lax.broadcasted_iota(jnp.int32, shape, axis)


def between(index, start, count):
    return (index >= start) & (index < start + count)


def full_dot(left, right):
    return jnp.dot(left, right, precision=lax.Precision.HIGHEST, preferred_element_type=F32)


def exact_dot(left, choice):
    choice = choice.astype(jnp.bfloat16)
    high = left.astype(jnp.bfloat16)
    rest = left - high.astype(F32)
    middle = rest.astype(jnp.bfloat16)
    low = (rest - middle.astype(F32)).astype(jnp.bfloat16)
    parts = [jnp.dot(part, choice, preferred_element_type=F32) for part in (high, middle, low)]
    return parts[0] + (parts[1] + parts[2])


def scratch_plan():
    plan = {}
    for level in range(4):
        for name in LEVEL_ARRAYS:
            plan[f"{name}{level}"] = pltpu.VMEM((NZ, XR[level], YR[level]), F32)
    for name in ("E", "N", "g", "inv", "rhs", "u", "f"):
        plan[f"{name}2c"] = pltpu.VMEM((NZ, 16, 128), F32)
    plan["P0"] = pltpu.VMEM((NZ, XR[0], YR[0]), F32)
    plan["S0"] = pltpu.VMEM((NZ, XR[0], YR[0]), F32)
    for name in ("E4", "N4", "g4", "inv4", "rhs4", "u4", "f4"):
        plan[name] = pltpu.VMEM((NZ * 16, 128), F32)
    for name in ("ta", "tb", "tc", "td"):
        plan[name] = pltpu.VMEM((NZ, 3, 32, 128), F32)
    plan["e0_sy"] = pltpu.VMEM((2, 3, 16, 128), F32)
    plan["e0_ry"] = pltpu.VMEM((2, 3, 16, 128), F32)
    plan["e0_rc"] = pltpu.VMEM((4, 3, 8, 128), F32)
    for kind in ("s", "r"):
        plan[f"e0_{kind}a"] = pltpu.VMEM((2, NZ, 8, 256), F32)
        plan[f"e0_{kind}b"] = pltpu.VMEM((2, NZ // 2, 8, 256), F32)
    for name, count in (("c2", 4), ("x2", 1)):
        plan[f"{name}_sx"] = pltpu.VMEM((count, 4, 8, 128), F32)
        plan[f"{name}_rx"] = pltpu.VMEM((2 * REACH + 1, count, 4, 8, 128), F32)
        plan[f"{name}_sy"] = pltpu.VMEM((2, count, 8, 128), F32)
        plan[f"{name}_ry"] = pltpu.VMEM((2, 2 * REACH + 1, count, 8, 128), F32)
    for kind in ("s", "r"):
        plan[f"v1_{kind}x"] = pltpu.VMEM((2, 8, 8, 128), F32)
        plan[f"v1_{kind}y"] = pltpu.VMEM((2, 8, 128), F32)
    plan["v1_rc"] = pltpu.VMEM((4, 8, 128), F32)
    for name in ("residual", "pressure", "conductivity"):
        plan[name] = pltpu.VMEM((NZ, NX[0], NY[0]), F32)
    plan["land_use"] = pltpu.VMEM((NX[0], NY[0]), jnp.int32)
    plan["relay"] = pltpu.SemaphoreType.REGULAR((4,))
    plan["load"] = pltpu.SemaphoreType.DMA((4,))
    for name, count in (("gc", 4), ("gr", 1)):
        plan[f"{name}_s1"] = pltpu.VMEM((count, 8, 128), F32)
        plan[f"{name}_r1"] = pltpu.VMEM((GY, count, 8, 128), F32)
        plan[f"{name}_s2"] = pltpu.VMEM((count, 8, 128), F32)
        plan[f"{name}_r2"] = pltpu.VMEM((count, GX * 8, 128), F32)
    plan["send"] = pltpu.SemaphoreType.DMA((N_SEM,))
    plan["recv"] = pltpu.SemaphoreType.DMA((N_SEM,))
    return plan


PLAN = scratch_plan()


def kernel(
    residual_in, pressure_in, conductivity_in, land_use_in, storage_table, return_table,
    well_cells, well_rates, return_cells, out, *scratch,
):
    ref = dict(zip(PLAN, scratch))
    gx = lax.axis_index("gx")
    gy = lax.axis_index("gy")

    def device(dx, dy):
        return (lax.rem(gx + (dx + GX), GX), lax.rem(gy + (dy + GY), GY))

    peers = [(dx, dy) for dx in (-1, 0, 1) for dy in (-1, 0, 1) if (dx, dy) != (0, 0)]
    relays = (peers, [(2 * dx, 2 * dy) for dx, dy in peers], [(-4, 0), (4, 0)], [(-8, 0), (8, 0)])

    def relay(stage):
        for dx, dy in relays[stage]:
            pl.semaphore_signal(
                ref["relay"].at[stage], inc=1, device_id=device(dx, dy), device_id_type=MESH
            )

    def await_relay(stage):
        pl.semaphore_wait(ref["relay"].at[stage], len(relays[stage]))

    barrier = pltpu.get_barrier_semaphore()
    for dx, dy in peers:
        pl.semaphore_signal(barrier, inc=1, device_id=device(dx, dy), device_id_type=MESH)

    loads = []
    for i, (name, source) in enumerate(
        (("land_use", land_use_in), ("pressure", pressure_in), ("conductivity", conductivity_in), ("residual", residual_in))
    ):
        loads.append(pltpu.make_async_copy(source, ref[name], ref["load"].at[i]))
        loads[-1].start()
    residual, pressure, conductivity, land_use = (
        ref[name] for name in ("residual", "pressure", "conductivity", "land_use")
    )
    started = []

    def remote(src, dst, index, dx, dy):
        copy = pltpu.make_async_remote_copy(
            src_ref=src, dst_ref=dst, send_sem=ref["send"].at[index], recv_sem=ref["recv"].at[index],
            device_id=device(dx, dy), device_id_type=MESH,
        )
        copy.start()
        started.append(copy)
        return copy

    row8 = iota((8, 128), 0)
    lane8 = iota((8, 128), 1)

    def send_permeable(array):
        copies = []
        for side, (own, there, dx) in enumerate(((0, 16, -1), (8, 24, 1))):
            copies.append(
                remote(
                    array.at[:, pl.ds(own, 8), pl.ds(0, 256)],
                    array.at[:, pl.ds(there, 8), pl.ds(0, 256)],
                    B_E0 + side, dx, 0,
                )
            )
        return copies

    row_wide = iota((8, 256), 0)

    def pack_rows(storage, source):
        sa, sb = ref["e0_sa"], ref["e0_sb"]
        for z in range(NZ):
            for side in (0, 1):
                at = slice(8 * side, 8 * side + 8)
                kept, moved = storage[z, at, 0:256], source[z, at, 0:256]
                if side == 0:
                    sa[side, z] = jnp.where(row_wide < 6, kept, rot(moved, 6, 0))
                else:
                    sa[side, z] = jnp.where(row_wide >= 2, kept, rot(moved, 2, 0))
                if z % 2 == 1:
                    first = source[z - 1, at, 0:256]
                    sb[side, z // 2] = jnp.where(row_wide < 4, rot(first, -2, 0), rot(moved, 2, 0))

    def send_rows():
        sa, sb, ra, rb = (ref[f"e0_{kind}"] for kind in ("sa", "sb", "ra", "rb"))
        copies = []
        for side, dx in ((0, -1), (1, 1)):
            copies.append(remote(sa.at[side], ra.at[side], B_E0 + 20 + side, dx, 0))
            copies.append(remote(sb.at[side], rb.at[side], B_E0 + 22 + side, dx, 0))
        return copies

    def receive_rows(copies, storage, source):
        for copy in copies:
            copy.wait_recv()
        ra, rb = ref["e0_ra"], ref["e0_rb"]
        middle = (row_wide >= 2) & (row_wide < 6)
        for z in range(NZ):
            shift = 2 if z % 2 == 0 else -2
            for side in (0, 1):
                at = slice(16 + 8 * side, 24 + 8 * side)
                tile, rest = ra[side, z], rot(rb[side, z // 2], shift, 0)
                if side == 0:
                    storage[z, at, 0:256] = jnp.where(row_wide < 6, tile, 1.0)
                    near = jnp.where(row_wide < 2, rot(tile, -6, 0), 0.0)
                else:
                    storage[z, at, 0:256] = jnp.where(row_wide >= 2, tile, 1.0)
                    near = jnp.where(row_wide >= 6, rot(tile, -2, 0), 0.0)
                source[z, at, 0:256] = jnp.where(middle, rest, near)

    def pack_columns(array, k):
        sy = ref["e0_sy"]
        lane = iota((16, 128), 1)
        low = jnp.zeros((16, 128), F32)
        high = jnp.zeros((16, 128), F32)
        for z in range(NZ):
            here = between(lane, 8 * z, 8)
            low = jnp.where(here, rot(array[z, 0:16, 0:128], 8 * z, 1), low)
            high = jnp.where(here, rot(array[z, 0:16, 128:256], 8 * z + 8, 1), high)
        sy[0, k] = low
        sy[1, k] = high

    def send_columns(k):
        sy, ry, rc = ref["e0_sy"], ref["e0_ry"], ref["e0_rc"]
        base = B_E0 + 2 + 6 * k
        copies = []
        first, last = pl.ds(0, 8), pl.ds(8, 8)
        moves = (
            (sy.at[0, k], ry.at[0, k], 0, -1),
            (sy.at[1, k], ry.at[1, k], 0, 1),
            (sy.at[0, k, first], rc.at[0, k], -1, -1),
            (sy.at[0, k, last], rc.at[1, k], 1, -1),
            (sy.at[1, k, first], rc.at[2, k], -1, 1),
            (sy.at[1, k, last], rc.at[3, k], 1, 1),
        )
        for i, (src, dst, dx, dy) in enumerate(moves):
            copies.append(remote(src, dst, base + i, dx, dy))
        return copies

    def receive_columns(copies, array, k, fill):
        for copy in copies:
            copy.wait_recv()
        ry, rc = ref["e0_ry"], ref["e0_rc"]
        lane = iota((32, 128), 1)
        north = jnp.concatenate([ry[0, k], rc[0, k], rc[1, k]], axis=0)
        south = jnp.concatenate([ry[1, k], rc[2, k], rc[3, k]], axis=0)
        for z in range(NZ):
            value = jnp.where(lane >= 120, rot(south, -8 * (z + 1), 1), fill)
            array[z, :, 256:384] = jnp.where(lane < 8, rot(north, -8 * z, 1), value)

    def pack_wide(name, get):
        sx, sy, rx = (ref[f"{name}_{kind}"] for kind in ("sx", "sy", "rx"))
        for a in range(sx.shape[0]):
            values = [get(a, z) for z in range(NZ)]
            for t in range(4):
                left = jnp.where(row8 < 4, values[t], rot(values[t + 4], 4, 0))
                right = jnp.where(row8 < 4, values[t + 8], rot(values[t + 12], 4, 0))
                tile = jnp.where(lane8 < 64, left, rot(right, 64, 1))
                sx[a, t] = tile
                rx[REACH, a, t] = tile
            low = jnp.zeros((8, 128), F32)
            high = jnp.zeros((8, 128), F32)
            for q in range(8):
                both = jnp.where(row8 < 4, values[q], rot(values[q + 8], 4, 0))
                here = between(lane8, 16 * q, 16)
                low = jnp.where(here, rot(both, 16 * q, 1), low)
                high = jnp.where(here, rot(both, 16 * q - 48, 1), high)
            sy[0, a] = low
            sy[1, a] = high

    def send_wide(name, base):
        return send_wide_to(name, base, [d for d in SIDES if abs(d) < REACH])

    def send_wide_to(name, base, sides):
        sx, sy, rx, ry = (ref[f"{name}_{kind}"] for kind in ("sx", "sy", "rx", "ry"))
        far = REACH in sides
        copies = []
        for d in sides:
            copies.append(remote(sx, rx.at[REACH - d], base + SIDES.index(d), d, 0))
        for side, dy in ((0, -1), (1, 1)):
            for d in sides if far else sides + [0]:
                index = 2 * REACH + side * (2 * REACH + 1) + d + REACH
                copies.append(remote(sy.at[side], ry.at[side, REACH - d], base + index, d, dy))
        return copies

    def receive_wide(name, copies, targets, fills, far):
        for copy in copies:
            copy.wait_recv()
        rx, ry = ref[f"{name}_rx"], ref[f"{name}_ry"]
        empty = jnp.zeros((8, 128), F32)

        def join(first, second):
            return (
                jnp.where(row8 < 4, first, rot(second, 4, 0)),
                jnp.where(row8 < 4, rot(first, 4, 0), second),
            )

        for a, (target, fill) in enumerate(zip(targets, fills)):
            tiles = {0: (0, 1), 1: (2, None), 2: (None, None), 3: (-2, -1)}
            if far:
                tiles = {1: (2, 3), 2: (None, -3)}
            for p, (k0, k1) in tiles.items():
                if k0 is None and k1 is None:
                    for z in range(NZ):
                        target[z, 8 * p : 8 * p + 8, :] = jnp.full((8, 128), fill, F32)
                    continue
                layers = [None] * NZ
                for t in range(4):
                    first = empty if k0 is None else rx[REACH + k0, a, t]
                    second = empty if k1 is None else rx[REACH + k1, a, t]
                    for i, both in enumerate(join(first, second)):
                        layers[t + 4 * i] = both
                        layers[t + 4 * i + 8] = rot(both, 64, 1)
                sides = []
                for side in (0, 1):
                    first = empty if k0 is None else ry[side, REACH + k0, a]
                    second = empty if k1 is None else ry[side, REACH + k1, a]
                    sides.append(join(first, second))
                for z in range(NZ):
                    q = z % 8
                    north = rot(sides[0][z // 8], 64 - 16 * q, 1)
                    south = rot(sides[1][z // 8], 112 - 16 * q, 1)
                    value = jnp.where(lane8 < 80, north, jnp.where(lane8 >= 112, south, fill))
                    value = jnp.where(lane8 < 64, layers[z], value)
                    if k0 is None:
                        value = jnp.where(row8 < 4, fill, value)
                    if k1 is None:
                        value = jnp.where(row8 < 4, value, fill)
                    target[z, 8 * p : 8 * p + 8, :] = value

    def send_u1():
        sx, sy, rx, ry, rc = (ref[f"v1_{kind}"] for kind in ("sx", "sy", "rx", "ry", "rc"))
        low = jnp.zeros((8, 128), F32)
        high = jnp.zeros((8, 128), F32)
        for z in range(NZ):
            u = ref["u1"][z, 0:8, 0:128]
            if z % 2 == 0:
                before = u
            else:
                sx[0, z // 2] = jnp.where(row8 < 4, before, rot(u, 4, 0))
                sx[1, z // 2] = jnp.where(row8 < 4, rot(before, 4, 0), u)
            here = between(lane8, 4 * z, 4)
            low = jnp.where(here, rot(u, 4 * z, 1), low)
            high = jnp.where(here, rot(u, 4 * z + 4, 1), high)
        sy[0] = low
        sy[1] = high
        moves = (
            (sx.at[0], rx.at[0], -1, 0),
            (sx.at[1], rx.at[1], 1, 0),
            (sy.at[0], ry.at[0], 0, -1),
            (sy.at[1], ry.at[1], 0, 1),
            (sy.at[0], rc.at[0], -1, -1),
            (sy.at[0], rc.at[1], 1, -1),
            (sy.at[1], rc.at[2], -1, 1),
            (sy.at[1], rc.at[3], 1, 1),
        )
        return [remote(src, dst, B_V1 + i, dx, dy) for i, (src, dst, dx, dy) in enumerate(moves)]

    def receive_u1(copies):
        for copy in copies:
            copy.wait_recv()
        rx, ry, rc = (ref[f"v1_{kind}"] for kind in ("rx", "ry", "rc"))
        lane = iota((16, 128), 1)
        north = jnp.concatenate([ry[0], jnp.where(row8 < 4, rc[0], rc[1])], axis=0)
        south = jnp.concatenate([ry[1], jnp.where(row8 < 4, rc[2], rc[3])], axis=0)
        u = ref["u1"]
        for z in range(NZ):
            east, west = rx[0, z // 2], rx[1, z // 2]
            if z % 2 == 0:
                value = jnp.where(row8 < 4, east, rot(west, 4, 0))
            else:
                value = jnp.where(row8 < 4, rot(east, 4, 0), west)
            u[z, 8:16, 0:128] = value
            value = jnp.where(lane >= 124, rot(south, -4 * (z + 1), 1), 0.0)
            u[z, :, 128:256] = jnp.where(lane < 4, rot(north, -4 * z, 1), value)

    HALF = NZ // 2

    def factor_columns(diag, down, put):
        top = bottom = None
        for i in range(HALF):
            z = i
            pivot = diag(z) if i == 0 else diag(z) - top * down(z - 1)
            inverse = 1.0 / pivot
            top = down(z) * inverse
            put(z, inverse, top)
            z = NZ - 1 - i
            pivot = diag(z) if i == 0 else diag(z) - bottom * down(z)
            if z == HALF:
                pivot = pivot - top * down(z - 1)
            inverse = 1.0 / pivot
            bottom = down(z - 1) * inverse
            put(z, inverse, bottom)

    def factor(level):
        diag, down, g, inv = (ref[f"{name}{level}"] for name in ("diag", "D", "g", "inv"))

        def put(z, inverse, inwards):
            inv[z] = inverse
            g[z] = inwards

        factor_columns(lambda z: diag[z], lambda z: down[z], put)

    def solve_columns(right, g, inv, put_f, get_f, update):
        top = bottom = None
        for i in range(HALF):
            z = i
            top = right(z) if i == 0 else right(z) + g(z - 1) * top
            put_f(z, top)
            z = NZ - 1 - i
            bottom = right(z) if i == 0 else right(z) + g(z + 1) * bottom
            if z > HALF:
                put_f(z, bottom)
        below = (bottom + g(HALF - 1) * top) * inv(HALF)
        update(HALF, below)
        above = below
        for i in range(HALF):
            z = HALF - 1 - i
            above = get_f(z) * inv(z) + g(z) * above
            update(z, above)
            z = HALF + 1 + i
            if z < NZ:
                below = get_f(z) * inv(z) + g(z) * below
                update(z, below)

    def first_sweep(level):
        g, inv, f, rhs, u = (ref[f"{name}{level}"] for name in ("g", "inv", "f", "rhs", "u"))

        def put_f(z, value):
            f[z] = value

        def update(z, solved):
            u[z] = OMEGA * solved

        solve_columns(
            lambda z: rhs[z], lambda z: g[z], lambda z: inv[z], put_f, lambda z: f[z], update
        )

    def lateral(level, z, u):
        east, north = ref[f"E{level}"][z], ref[f"N{level}"][z]
        return (
            east * rot(u, -1, 0) + rot(east * u, 1, 0) + north * rot(u, -1, 1) + rot(north * u, 1, 1)
        )

    def sweep(level, last=None):
        g, f, rhs, u = (ref[f"{name}{level}"] for name in ("g", "f", "rhs", "u"))
        inv = ref[f"inv{level}"]
        rows, lanes = u.shape[1:] if last is None else last.shape[1:]
        at = (slice(0, rows), slice(0, lanes))

        def put_f(z, value):
            f[(z, *at)] = value

        def update(z, solved):
            old = u[(z, *at)]
            value = old + OMEGA * (solved - old)
            if last is None:
                u[z] = value
            else:
                last[z] = value

        solve_columns(
            lambda z: rhs[(z, *at)] + lateral(level, z, u[z])[at], lambda z: g[(z, *at)],
            lambda z: inv[(z, *at)], put_f, lambda z: f[(z, *at)], update,
        )

    def remainder(level, z):
        diag, down, rhs, u = (ref[f"{name}{level}"] for name in ("diag", "D", "rhs", "u"))
        here = u[z]
        value = rhs[z] + lateral(level, z, here) - diag[z] * here
        if z < NZ - 1:
            value = value + down[z] * u[z + 1]
        if z > 0:
            value = value + down[z - 1] * u[z - 1]
        return value

    PIECES = (
        ((0, 256, 256, 256), (256, 128, 64, 128)),
        ((0, 128, 128, 128),),
        ((0, 128, 96, 128),),
        ((0, 128, 128, 32),),
    )
    ROWS = (32, 8, 32, 8)

    def lane_matrix(piece, kind, transpose=False):
        _, count, turn, limit = piece
        shape = (128, count) if transpose else (count, 128)
        fine = iota(shape, 1 if transpose else 0)
        coarse = iota(shape, 0 if transpose else 1)
        hit = (((fine >> 1) + jnp.where(fine >= turn, 64, 0)) == coarse) & (fine < limit)
        if kind != "sum":
            hit = hit & ((fine & 1) == (1 if kind == "odd" else 0))
        return jnp.where(hit, 1.0, 0.0).astype(F32)

    def put_rows(buffer, rows, z, value):
        for t in range(value.shape[1] // 128):
            buffer[z, t, 0:rows, :] = value[0:rows, 128 * t : 128 * (t + 1)]

    def row_half(buffer, count_rows, piece, z, odd):
        start, count = piece[0], piece[1]
        parts = []
        for t in range(start // 128, (start + count) // 128):
            rows = [buffer[z, t, pl.ds(i + odd, 8, stride=2), :] for i in range(0, count_rows, 16)]
            parts.append(rows[0] if len(rows) == 1 else jnp.concatenate(rows, axis=0))
        return parts[0] if len(parts) == 1 else jnp.concatenate(parts, axis=1)

    def coarse_rows(rows):
        return max(8, rows // 2)

    def lanes_of(level):
        return sum(piece[1] for piece in PIECES[level])

    def layers_of(value, rows):
        return [value[rows * z : rows * (z + 1)] for z in range(NZ)]

    def keep_own(value, fill):
        return jnp.where((row8 < 4) & (lane8 < 64), value, fill)

    def aggregate(level, rows, pieces_of, get):
        for z in range(NZ):
            put_rows(ref["ta"], rows, z, get(z))
        pieces = []
        for piece in pieces_of:
            summed = jnp.concatenate(
                [row_half(ref["ta"], rows, piece, z, 0) + row_half(ref["ta"], rows, piece, z, 1) for z in range(NZ)],
                axis=0,
            )
            pieces.append(layers_of(exact_dot(summed, lane_matrix(piece, "sum")), coarse_rows(rows)))
        return pieces

    def restrict(level):
        lanes = lanes_of(level)
        return aggregate(level, ROWS[level], PIECES[level], lambda z: remainder(level, z)[:, 0:lanes])

    def coarsen(level, extra=None):
        rows_fine = ROWS[level]
        lanes = lanes_of(level)
        names = ("E", "N", "D", "diag")
        buffers = [ref[name] for name in ("ta", "tb", "tc", "td")]
        for z in range(NZ):
            for name, buffer in zip(names, buffers):
                value = ref[f"{name}{level}"][z, 0:rows_fine, 0:lanes]
                if extra is not None and name == "diag":
                    value = value + extra[z]
                put_rows(buffer, rows_fine, z, value)
        pieces = []
        for piece in PIECES[level]:
            odd_e, sum_n, sum_d, sum_g = [], [], [], []
            for z in range(NZ):
                (e0, e1), (n0, n1), (d0, d1), (g0, g1) = (
                    [row_half(buffer, rows_fine, piece, z, odd) for odd in (0, 1)] for buffer in buffers
                )
                odd_e.append(e1)
                sum_n.append(n0 + n1)
                sum_d.append(d0 + d1)
                sum_g.append(g0 + g1 - 2.0 * e0)
            total = lane_matrix(piece, "sum")
            rows = coarse_rows(rows_fine)
            east = exact_dot(jnp.concatenate(odd_e, axis=0), total)
            down = exact_dot(jnp.concatenate(sum_d, axis=0), total)
            north = jnp.concatenate(sum_n, axis=0)
            diagonal = exact_dot(jnp.concatenate(sum_g, axis=0), total) - 2.0 * exact_dot(
                north, lane_matrix(piece, "even")
            )
            north = exact_dot(north, lane_matrix(piece, "odd"))
            pieces.append([layers_of(value, rows) for value in (east, north, down, diagonal)])
        return pieces

    def prolong(level, coarse):
        buffer = ref["ta"]
        u = ref[f"u{level}"]
        pieces = {
            0: ((0, 256, 256, 256), (256, 128, 64, 128)),
            1: ((0, 128, 128, 128), (128, 128, 128, 128)),
            "2c": ((0, 128, 96, 128),),
            3: ((0, 128, 96, 128),),
        }[level]
        for i, piece in enumerate(pieces):
            value = jnp.concatenate([coarse(i, z) for z in range(NZ)], axis=0)
            rows = value.shape[0] // NZ
            fine = exact_dot(value, lane_matrix(piece, "sum", transpose=True))
            start, count = piece[0], piece[1]
            for z in range(NZ):
                for t in range(count // 128):
                    for r in range(0, rows, 8):
                        part = fine[rows * z + r : rows * z + r + 8, 128 * t : 128 * (t + 1)]
                        for odd in (0, 1):
                            buffer[z, start // 128 + t, pl.ds(2 * r + odd, 8, stride=2), :] = part
        for z in range(NZ):
            add = [buffer[z, t, 0 : u.shape[1], :] for t in range(u.shape[2] // 128)]
            u[z] = u[z] + (add[0] if len(add) == 1 else jnp.concatenate(add, axis=1))

    at_sum = (lane8 == 48) & (row8 == 0)

    def pack_tile(stacked):
        stacked = jnp.where(iota((16, 128), 1) < 16, stacked, 0.0)
        return rot(stacked[0:8], 16, 1) + rot(stacked[8:16], 80, 1)

    def stack_layers(values):
        row16 = iota((16, 128), 0)
        stacked = jnp.zeros((16, 128), F32)
        for z in range(NZ):
            stacked = jnp.where(row16 == z, jnp.broadcast_to(values[z][0:1], (16, 128)), stacked)
        return stacked

    def coarsest_coefficients(coarse2):
        east, north, down, diagonal = (
            jnp.concatenate([keep_own(value, 0.0) for value in values], axis=0) for values in coarse2
        )
        layer, row_of = iota((16, 128), 0), iota((16, 128), 1)
        rows = jnp.where((row_of >> 3) == layer, 1.0, 0.0).astype(F32)
        last_row = jnp.where(row_of == 8 * layer + 3, 1.0, 0.0).astype(F32)
        inner = jnp.where((iota((128, 128), 0) & 7) < 3, 2.0, 0.0) * east
        fine, coarse = iota((128, 128), 0), iota((128, 128), 1)
        hit = ((fine >> 2) == coarse) & (fine < 64)
        lanes = jnp.where(hit, 1.0, 0.0).astype(F32)
        last_lane = jnp.where(hit & ((fine & 3) == 3), 1.0, 0.0).astype(F32)
        summed = exact_dot(
            jnp.concatenate(
                [full_dot(last_row, east), full_dot(rows, down), full_dot(rows, diagonal - inner)], axis=0
            ),
            lanes,
        )
        north = full_dot(rows, north)
        north4 = exact_dot(north, last_lane)
        diagonal4 = summed[32:48] - 2.0 * exact_dot(north, lanes - last_lane)
        return diagonal4, summed[0:16], north4, summed[16:32]

    def total_of(value):
        return jnp.sum(jnp.sum(value, axis=1, keepdims=True), axis=0, keepdims=True)

    def gather_columns(name, tiles, part, base):
        s1, r1 = ref[f"{name}_s1"], ref[f"{name}_r1"]
        for a, tile in enumerate(tiles):
            s1[a] = jnp.where(at_sum, part, tile) if a == 0 else tile
        copies = []
        for d in range(1, GY):
            near = d in (1, GY - 1)
            copies.append(
                remote(s1 if near else s1.at[0], r1.at[d] if near else r1.at[d, 0], base + d - 1, 0, d)
            )
        return copies

    def at_row(gx_of):
        return pl.ds(pl.multiple_of(8 * gx_of, 8), 8)

    def window_of(name, copies):
        for copy in copies:
            copy.wait_recv()
        s1, r1, s2, r2 = (ref[f"{name}_{kind}"] for kind in ("s1", "r1", "s2", "r2"))
        for a in range(s1.shape[0]):
            clean = [s1[a], r1[1, a], r1[GY - 1, a]]
            if a == 0:
                clean = [jnp.where(at_sum, 0.0, tile) for tile in clean]
            window = clean[0] + rot(clean[1], -16, 1) + rot(clean[2], 16, 1)
            if a == 0:
                parts = s1[0]
                for d in range(1, GY):
                    parts = parts + r1[d, 0]
                window = jnp.where(at_sum, parts, window)
            s2[a] = window
            r2[a, at_row(gx), :] = window
        return s2, r2

    def gather_rows(name, copies, base):
        s2, r2 = window_of(name, copies)
        return [remote(s2, r2.at[:, at_row(gx), :], base + d - 1, d, 0) for d in range(1, GX)]

    def gather_along_z(name, copies, base):
        s2, r2 = window_of(name, copies)
        return [remote(s2, r2.at[:, at_row(gx), :], base + d - 1, GXX * d, 0) for d in range(1, GZ)]

    def gather_along_x(name, copies, base):
        for copy in copies:
            copy.wait_recv()
        r2 = ref[f"{name}_r2"]
        x = lax.rem(gx, GXX)
        result = []
        for d in range(1, GXX):
            there = lax.rem(x + d, GXX) - x
            for z in range(GZ):
                rows = r2.at[:, at_row(GXX * z + x), :]
                copy = pltpu.make_async_remote_copy(
                    src_ref=rows, dst_ref=rows, send_sem=ref["send"].at[base + len(result)],
                    recv_sem=ref["recv"].at[base + len(result)],
                    device_id=(gx + there, gy), device_id_type=MESH,
                )
                copy.start()
                started.append(copy)
                result.append(copy)
        return result

    def coarse_layer(buffer, a, z):
        sub, half = z % 8, z // 8
        pieces = [buffer[a, pl.ds(64 * i + sub, 8, stride=8), :] for i in range(4)]
        low = jnp.concatenate(pieces[0:2], axis=0)
        high = jnp.concatenate(pieces[2:4], axis=0)
        lane = iota((16, 128), 1)
        if half == 0:
            return jnp.where(lane < 64, low, rot(high, 64, 1))
        return jnp.where(lane < 64, rot(low, 64, 1), high)

    def coarse_sum(buffer):
        value = jnp.where(at_sum, buffer[0, 0:8, :], 0.0)
        for k in range(1, GX):
            value = value + jnp.where(at_sum, buffer[0, 8 * k : 8 * k + 8, :], 0.0)
        return total_of(value)

    def put_layer(name, z, value):
        ref[name][16 * z : 16 * z + 16, :] = value

    def coarse_at(name, z):
        return ref[name][16 * z : 16 * z + 16, :]

    for copy in loads:
        copy.wait()
    use = land_use[...]
    table = jnp.zeros(use.shape, F32)
    fraction = jnp.zeros(use.shape, F32)
    for category in range(CLASSES):
        table = table + jnp.where(use == category, storage_table[category], 0.0)
        fraction = fraction + jnp.where(use == category, return_table[category], 0.0)
    cells, rates, returns = well_cells[...], well_rates[...], return_cells[...]
    wells = rates.shape[1]

    def hits(count, index):
        return iota((count, wells), 0) == index

    def outer(count, index_row, index_column):
        left = jnp.where(hits(count, index_row), rates, 0.0)
        right = jnp.where(hits(256, index_column), 1.0, 0.0).astype(F32)
        return lax.dot_general(
            left, right, (((1,), (1,)), ((), ())),
            precision=lax.Precision.HIGHEST, preferred_element_type=F32,
        )

    storage_sum = jnp.zeros((16, 256), F32)
    for z in range(NZ):
        relief = jnp.exp(ALPHA * jnp.minimum(pressure[z], 0.0))
        ref["P0"][z, 0:16, 0:256] = conductivity[z] * relief
        storage = table * relief
        ref["S0"][z, 0:16, 0:256] = storage
        storage_sum = storage_sum + storage
    pumped = outer(256, cells >> 8, cells & 255)
    recharge = fraction * outer(16, returns >> 8, returns & 255)
    for z in range(NZ):
        source = residual[z] - pumped[16 * z : 16 * z + 16]
        if z == 0:
            source = source + recharge
        ref["rhs0"][z, 0:16, 0:256] = source
    for k, name in enumerate(("P0", "S0", "rhs0")):
        pack_columns(ref[name], k)
    pack_rows(ref["S0"], ref["rhs0"])
    pl.semaphore_wait(barrier, len(peers))
    copies_p = send_permeable(ref["P0"]) + send_columns(0)
    copies_rows = send_rows()
    copies_s = send_columns(1)
    copies_r = send_columns(2)
    relay(0)
    await_relay(0)
    relay(1)
    receive_columns(copies_p, ref["P0"], 0, 0.0)

    flags = [
        jnp.where(inside, 1.0, 0.0).astype(F32)
        for inside in (gx < GX - 1, gx > 0, gy < GY - 1, gy > 0)
    ]
    row = iota((32, 384), 0)
    lane = iota((32, 384), 1)
    inside = jnp.where(row < 16, 1.0, jnp.where(row < 24, flags[0], flags[1]))
    inside = inside * jnp.where(lane < 256, 1.0, jnp.where(lane < 320, flags[2], flags[3]))

    def harmonic(first_value, second_value):
        return 2.0 * first_value * second_value / (first_value + second_value + 1e-30)

    above = None
    for z in range(NZ):
        here = ref["P0"][0] * inside if z == 0 else beneath
        east = harmonic(here, rot(here, -1, 0))
        north = harmonic(here, rot(here, -1, 1))
        diagonal = east + rot(east, 1, 0) + north + rot(north, 1, 1)
        if z > 0:
            diagonal = diagonal + above
        if z < NZ - 1:
            beneath = ref["P0"][z + 1] * inside
            above = VERTICAL * harmonic(here, beneath)
            diagonal = diagonal + above
        else:
            above = jnp.zeros_like(here)
        ref["D0"][z] = above
        ref["E0"][z] = east
        ref["N0"][z] = north
        ref["diag0"][z] = diagonal
    def place(level, names, pieces):
        for z in range(NZ):
            for k, name in enumerate(names):
                fill = 1.0 if name == "diag" else 0.0
                target = ref[f"{name}{level}"]
                if level == 1:
                    target[z, :, 0:128] = pieces[0][k][z]
                    lane = iota((16, 128), 1)
                    target[z, :, 128:256] = jnp.where((lane < 32) | (lane >= 96), pieces[1][k][z], fill)
                else:
                    lane = iota((16, 128), 1)
                    target[z] = jnp.where((lane < 48) | (lane >= 112), pieces[0][k][z], fill)

    names = ("E", "N", "D", "diag")
    fills = (0.0, 0.0, 0.0, 1.0)
    place(1, names, coarsen(0))
    (own_storage,) = aggregate(0, 16, PIECES[0][0:1], lambda z: ref["S0"][z, 0:16, 0:256])
    (coarse2,) = coarsen(1, extra=own_storage)
    own2 = [[keep_own(coarse2[k][z], fills[k]) for z in range(NZ)] for k in range(4)]
    pack_wide("c2", lambda k, z: own2[k][z])
    tiles = [pack_tile(value) for value in coarsest_coefficients(coarse2)]
    await_relay(1)
    relay(2)
    copies_c2 = send_wide("c2", B_C2)
    stage = gather_columns("gc", tiles, total_of(storage_sum), B_GC1)

    receive_rows(copies_rows, ref["S0"], ref["rhs0"])
    receive_columns(copies_s, ref["S0"], 1, 1.0)
    for z in range(NZ):
        ref["diag0"][z] = ref["diag0"][z] + ref["S0"][z]
    factor(0)
    storage1 = aggregate(0, 32, PIECES[0], lambda z: ref["S0"][z])
    lane = iota((16, 128), 1)
    for z in range(NZ):
        diagonal = ref["diag1"]
        diagonal[z, :, 0:128] = diagonal[z, :, 0:128] + storage1[0][z]
        tail = jnp.where((lane < 32) | (lane >= 96), storage1[1][z], 0.0)
        diagonal[z, :, 128:256] = diagonal[z, :, 128:256] + tail
    factor(1)

    receive_columns(copies_r, ref["rhs0"], 2, 0.0)
    first_sweep(0)
    sweep(0)
    first_sweep(0)
    sweep(0)
    await_relay(2)
    relay(3)
    place(1, ("rhs",), [[piece] for piece in restrict(0)])
    first_sweep(1)
    sweep(1)
    (values,) = restrict(1)
    pack_wide("x2", lambda k, z: values[z])
    copies_x2 = send_wide("x2", B_X2)
    copies_v1 = send_u1()
    far_sides = [-REACH, REACH]
    copies_far = send_wide_to("c2", B_C2, far_sides)
    copies_far_x = send_wide_to("x2", B_X2, far_sides)

    await_relay(3)
    stage = gather_along_z("gc", stage, B_GCZ)

    two = [ref[f"{name}2"] for name in names]
    receive_wide("c2", copies_c2, two, fills, False)

    def prepare23():
        place(3, names, coarsen(2))
        factor(2)
        factor(3)

    def down23():
        first_sweep(2)
        sweep(2)
        place(3, ("rhs",), [[piece] for piece in restrict(2)])
        first_sweep(3)
        sweep(3)

    prepare23()
    receive_wide("x2", copies_x2, [ref["rhs2"]], (0.0,), False)
    down23()
    (values,) = restrict(3)
    tile = pack_tile(stack_layers(values))
    stage_r = gather_columns("gr", [tile], total_of(tile), B_GR1)
    stage_c = gather_along_x("gc", stage, B_GCX)
    receive_u1(copies_v1)
    stage_r = gather_rows("gr", stage_r, B_GR2)
    receive_wide("c2", copies_far, two, fills, True)
    receive_wide("x2", copies_far_x, [ref["rhs2"]], (0.0,), True)
    prepare23()
    down23()
    for name in ("E", "N", "g", "inv", "rhs", "u"):
        for z in range(NZ):
            ref[f"{name}2c"][z, 0:8, :] = ref[f"{name}2"][z, 0:8, :]
            ref[f"{name}2c"][z, 8:16, :] = ref[f"{name}2"][z, 24:32, :]

    for copy in stage_c:
        copy.wait_recv()
    lane = iota((16, 128), 1)
    row = iota((16, 128), 0)
    gap = (lane & 63) >= 48

    def put_coarse(z, inverse, inwards):
        put_layer("inv4", z, inverse)
        put_layer("g4", z, inwards)

    factor_columns(
        lambda z: jnp.where(gap, 1.0, coarse_layer(ref["gc_r2"], 0, z)),
        lambda z: coarse_layer(ref["gc_r2"], 3, z),
        put_coarse,
    )
    for z in range(NZ):
        put_layer("E4", z, coarse_layer(ref["gc_r2"], 1, z))
        put_layer("N4", z, coarse_layer(ref["gc_r2"], 2, z))
    storage_total = coarse_sum(ref["gc_r2"])
    for copy in started:
        copy.wait_send()
    for copy in stage_r:
        copy.wait_recv()
    shift = coarse_sum(ref["gr_r2"]) / storage_total
    for z in range(NZ):
        at = slice(16 * z, 16 * z + 16)
        ref["rhs4"][at, :] = coarse_layer(ref["gr_r2"], 0, z)
        ref["u4"][at, :] = jnp.broadcast_to(shift, (16, 128))

    def coarse_sweep(step, carry):
        def right(z):
            u, east, north = coarse_at("u4", z), coarse_at("E4", z), coarse_at("N4", z)
            from_e = rot(u, -1, 0)
            from_e = jnp.where(row == 15, rot(from_e, 64, 1), from_e)
            from_w = rot(east * u, 1, 0)
            from_w = jnp.where(row == 0, rot(from_w, 64, 1), from_w)
            return (
                coarse_at("rhs4", z) + east * from_e + from_w + north * rot(u, -1, 1) + rot(north * u, 1, 1)
            )

        def update(z, solved):
            old = coarse_at("u4", z)
            put_layer("u4", z, old + OMEGA * (solved - old))

        solve_columns(
            right, lambda z: coarse_at("g4", z), lambda z: coarse_at("inv4", z),
            lambda z, value: put_layer("f4", z, value), lambda z: coarse_at("f4", z), update,
        )
        return carry

    lax.fori_loop(0, COARSE_SWEEPS, coarse_sweep, 0)

    turn = lax.rem(GX - gx, GX)

    def coarsest(_, z):
        value = coarse_at("u4", z)
        value = pltpu.roll(jnp.concatenate([value, rot(value, 64, 1)], axis=0), turn, 0)
        both = rot(jnp.where(row8 < 4, value[0:8], value[24:32]), -16, 1)
        return jnp.where((lane8 < 24) | (lane8 >= 112), both, 0.0)

    def from3(_, z):
        return jnp.where(row8 < 4, ref["u3"][z, 0:8, :], ref["u3"][z, 8:16, :])

    def from2(i, z):
        value = jnp.where(row8 < 6, ref["u2c"][z, 0:8, :], ref["u2c"][z, 8:16, :])
        return value if i == 0 else rot(value, 64, 1)

    prolong(3, coarsest)
    sweep(3)
    sweep(3)
    prolong("2c", from3)
    sweep("2c")
    sweep("2c")
    prolong(1, from2)
    sweep(1)
    sweep(1)
    prolong(0, lambda i, z: ref["u1"][z, :, 128 * i : 128 * (i + 1)])
    sweep(0)
    sweep(0, last=out)


def shards(
    newton_residual, pressure_head, conductivity, land_use, storage_table, return_table,
    well_cells, well_rates, return_cells,
):
    vmem = pl.BlockSpec(memory_space=pltpu.VMEM)
    hbm = pl.BlockSpec(memory_space=pl.ANY)
    smem = pl.BlockSpec(memory_space=pltpu.SMEM)
    wells = well_cells.shape[-1]
    return pl.pallas_call(
        kernel,
        out_shape=jax.ShapeDtypeStruct(newton_residual.shape, F32),
        in_specs=[hbm] * 4 + [smem] * 2 + [vmem] * 3,
        out_specs=vmem,
        scratch_shapes=list(PLAN.values()),
        compiler_params=pltpu.CompilerParams(
            collective_id=0, has_side_effects=True, vmem_limit_bytes=54784 * 1024
        ),
    )(
        newton_residual, pressure_head, conductivity, land_use, storage_table, return_table,
        well_cells.reshape(1, wells), well_rates.reshape(1, wells), return_cells.reshape(1, wells),
    )


def solution(mesh):
    return jax.shard_map(
        shards,
        mesh=mesh,
        in_specs=(
            P(None, "gx", "gy"),
            P(None, "gx", "gy"),
            P(None, "gx", "gy"),
            P("gx", "gy"),
            P(),
            P(),
            P("gx", "gy", None),
            P("gx", "gy", None),
            P("gx", "gy", None),
        ),
        out_specs=P(None, "gx", "gy"),
        check_vma=False,
    )
```
